128 devices in a mesh: pipe: 2 (over core), dp: 16 (over z, y), tensor: 4 (over x).
Axes of the slice: x: 4, y: 4, z: 4, core: 2. Of those that a mesh axis runs over, the one named last changes fastest.
Arguments:
- boundary: bfloat16 [2, 2, 16, 128, 768], P('pipe', None, 'dp'), may hold values from -6 to 6
- norm_gains: bfloat16 [2, 4, 768], P('pipe', None, 'dp'), may hold values from 0.25 to 1.75
- attn_qkv: bfloat16 [2, 2, 3, 768, 768], P('pipe', None, None, 'dp', 'tensor'), may hold values from -0.21875 to 0.21875
- attn_out: bfloat16 [2, 2, 768, 768], P('pipe', None, 'tensor', 'dp'), may hold values from -0.875 to 0.875
- mlp_in: bfloat16 [2, 768, 3072], P('pipe', 'dp', 'tensor'), may hold values from -0.21875 to 0.21875
- mlp_out: bfloat16 [2, 3072, 768], P('pipe', 'tensor', 'dp'), may hold values from -0.109375 to 0.109375
- expert_in: bfloat16 [2, 16, 768, 3072], P('pipe', 'dp', None, 'tensor'), may hold values from -0.21875 to 0.21875
- expert_out: bfloat16 [2, 16, 3072, 768], P('pipe', 'dp', 'tensor'), may hold values from -0.109375 to 0.109375
- expert_ids: int32 [2, 2, 16, 128, 2], P('pipe', None, 'dp'), may hold values from 0 to 15, as said below
- expert_slots: int32 [2, 2, 16, 128, 2], P('pipe', None, 'dp'), may hold values from 0 to 19, as said below
- gate_weights: float32 [2, 2, 16, 128, 2], P('pipe', None, 'dp'), may hold values from 0.25 to 0.75
Outputs:
- section_results: float32 [2, 2, 16, 128, 768], P('pipe', None, 'dp')
- norm_gains_grad: float32 [2, 4, 768], P('pipe', None, 'dp')
- attn_qkv_grad: float32 [2, 2, 3, 768, 768], P('pipe', None, None, 'dp', 'tensor')
- attn_out_grad: float32 [2, 2, 768, 768], P('pipe', None, 'tensor', 'dp')
- mlp_in_grad: float32 [2, 768, 3072], P('pipe', 'dp', 'tensor')
- mlp_out_grad: float32 [2, 3072, 768], P('pipe', 'tensor', 'dp')
- expert_in_grad: float32 [2, 16, 768, 3072], P('pipe', 'dp', None, 'tensor')
- expert_out_grad: float32 [2, 16, 3072, 768], P('pipe', 'dp', 'tensor')
The draws below stay inside these ranges and needn't reach their ends.
Inputs may be any that keep to these rules, and one draw needn't show every extreme that they name: `expert_ids`: in each section and micro-batch, each of the 128 tokens of one index of dp names two different experts, and no expert is named more than 20 times by them; in each section and micro-batch some expert is named exactly 20 times by the tokens of every index of dp. `expert_slots`: within the tokens of one index of dp in one section and micro-batch, the slots given for one expert are all different.
All inputs are finite; a program needn't handle non-finite values.
Results may differ from the reference program's by a relative error of at most 0.039.
Values may be sent and summed in bfloat16 or wider, within the bound.
A program may use at most 192 MiB of HBM per device.

```python
import jax
import jax.numpy as jnp
from jax import lax

D = 768
HEADS = 12
MLP = 3072
EH = 3072
L = 128
IMG_DEV = 1
MICRO = 2
SECTIONS = 2
EXPERTS = 16
IMAGES = 16
CAP = 20
N_DP = 16


def shuffle_experts(key):
    return jax.random.permutation(key, EXPERTS).astype(jnp.int32)


def shuffle_slots(key):
    return jax.random.permutation(key, CAP).astype(jnp.int32)


def route_block(key, hot_expert):
    tokens = IMG_DEV * L
    half_count = EXPERTS // 2
    key_list = jax.random.split(key, 5)
    orders = jax.vmap(shuffle_experts)(jax.random.split(key_list[0], CAP))
    column = jnp.arange(EXPERTS, dtype=jnp.int32)[None, :]
    leading = orders[:, 0:1]
    orders = jnp.where(orders == hot_expert, leading, jnp.where(column == 0, hot_expert, orders))
    seat_order = jax.vmap(shuffle_slots)(jax.random.split(key_list[1], EXPERTS))
    left_expert = orders[:, 0::2]
    right_expert = orders[:, 1::2]
    levels_grid = jnp.broadcast_to(jnp.arange(CAP, dtype=jnp.int32)[:, None], (CAP, half_count))
    rest_pick = jax.random.permutation(key_list[2], CAP * (half_count - 1))[:tokens - CAP]
    pick_left = jnp.concatenate([left_expert[:, 0], left_expert[:, 1:].reshape(-1)[rest_pick]])
    pick_right = jnp.concatenate([right_expert[:, 0], right_expert[:, 1:].reshape(-1)[rest_pick]])
    pick_level = jnp.concatenate([levels_grid[:, 0], levels_grid[:, 1:].reshape(-1)[rest_pick]])
    token_order = jax.random.permutation(key_list[3], tokens)
    pick_left = pick_left[token_order]
    pick_right = pick_right[token_order]
    pick_level = pick_level[token_order]
    flip_bits = jax.random.randint(key_list[4], (tokens,), 0, 2)
    expert_one = jnp.where(flip_bits == 1, pick_right, pick_left)
    expert_two = jnp.where(flip_bits == 1, pick_left, pick_right)
    route_ids = jnp.stack([expert_one, expert_two], axis=-1)
    route_slots = jnp.stack([seat_order[expert_one, pick_level], seat_order[expert_two, pick_level]], axis=-1)
    return (route_ids.astype(jnp.int32), route_slots.astype(jnp.int32))


def routing(key):
    blocks = IMAGES // IMG_DEV
    hot_list = jax.random.randint(jax.random.fold_in(key, 11), (SECTIONS * MICRO,), 0, EXPERTS)
    hot_all = jnp.repeat(hot_list, blocks).astype(jnp.int32)
    block_keys = jax.random.split(jax.random.fold_in(key, 12), SECTIONS * MICRO * blocks)
    route_ids, route_slots = jax.vmap(route_block)(block_keys, hot_all)
    shape_full = (SECTIONS, MICRO, IMAGES, L, 2)
    return (route_ids.reshape(shape_full), route_slots.reshape(shape_full))


def draw_expert_ids(key, part):
    shared = routing(key)
    return shared[0]


def draw_expert_slots(key, part):
    shared = routing(key)
    return shared[1]


def block_levels(stream_key, dims, cuts, least, top_value):
    gain, own = 1.0, jax.random.fold_in(stream_key, 6)
    for axis_at, parts in cuts:
        steps = jnp.exp(jax.random.uniform(jax.random.fold_in(own, axis_at), (parts,), jnp.float32, least / len(cuts), top_value / len(cuts)))
        gain = gain * jnp.repeat(steps, dims[axis_at] // parts).reshape([-1 if axis == axis_at else 1 for axis in range(len(dims))])
    return gain


def normal_values(stream_key, extent, scale, bound, shards=(), kind=jnp.bfloat16):
    values = scale * jax.random.normal(stream_key, extent, jnp.float32)
    if shards:
        values = values * block_levels(stream_key, extent, shards, -0.22, 0.18)
    return jnp.clip(values, -bound, bound).astype(kind)


def setup_inputs(seed: int = 0) -> dict:
    streams_of = jax.random.split(jax.random.key(seed), 12)
    return {
        "boundary": normal_values(streams_of[0], (2, MICRO, IMAGES, L, D), 1.0, 6.0, ((0, 2), (2, 16))),
        "norm_gains": jnp.clip(1.0 + 0.15 * jax.random.normal(streams_of[1], (SECTIONS, 4, D), jnp.float32), 0.25, 1.75).astype(jnp.bfloat16),
        "attn_qkv": normal_values(streams_of[2], (SECTIONS, 2, 3, D, D), D ** -0.5, 0.21875, ((0, 2), (3, 16), (4, 4))),
        "attn_out": normal_values(streams_of[3], (SECTIONS, 2, D, D), (D // 16) ** -0.5, 0.875, ((0, 2), (2, 4), (3, 16))),
        "mlp_in": normal_values(streams_of[4], (SECTIONS, D, MLP), D ** -0.5, 0.21875, ((0, 2), (1, 16), (2, 4))),
        "mlp_out": normal_values(streams_of[5], (SECTIONS, MLP, D), MLP ** -0.5, 0.109375, ((0, 2), (1, 4), (2, 16))),
        "expert_in": normal_values(streams_of[6], (SECTIONS, EXPERTS, D, EH), D ** -0.5, 0.21875, ((0, 2), (1, 16), (3, 4))),
        "expert_out": normal_values(streams_of[7], (SECTIONS, EXPERTS, EH, D), EH ** -0.5, 0.109375, ((0, 2), (1, 16), (2, 4))),
        "expert_ids": draw_expert_ids(jax.random.fold_in(streams_of[11], 71), 0),
        "expert_slots": draw_expert_slots(jax.random.fold_in(streams_of[11], 71), 0),
        "gate_weights": jnp.clip(0.25 + 0.5 * jax.random.uniform(streams_of[10], (SECTIONS, MICRO, IMAGES, L, 2), jnp.float32) ** block_levels(streams_of[10], (SECTIONS, MICRO, IMAGES, L, 2), ((0, 2), (2, 16)), -0.2, 0.2), 0.25, 0.75),
    }


epsilon = 1e-06
highest = lax.Precision.HIGHEST

@jax.custom_vjp
def low(v):
    return lax.optimization_barrier(v.astype(jnp.bfloat16)).astype(jnp.float32)

@jax.custom_vjp
def low_back(v):
    return v

def low_keep(v):
    return (low(v), None)

def low_pass(kept, grad):
    return (grad,)

def back_keep(v):
    return (v, None)

def back_low(kept, grad):
    return (low(grad),)
low.defvjp(low_keep, low_pass)
low_back.defvjp(back_keep, back_low)

def norm_rows(stream, norm_gain):
    center = stream - lax.optimization_barrier(jnp.mean(stream, axis=-1, keepdims=True))
    spread = lax.optimization_barrier(jnp.mean(center * center, axis=-1, keepdims=True))
    return center * lax.rsqrt(spread + epsilon) * norm_gain

def attention(stream, norm_gain, w_qkv, w_out):
    images = stream.shape[0]
    head_dim = D // HEADS
    normed = low(norm_rows(stream, norm_gain))
    projected = low_back(low(jnp.einsum('ild,cde->cile', normed, w_qkv, precision=highest)))
    pieces = projected.reshape(3, images, L, HEADS, head_dim)
    logits = jnp.einsum('iqhd,ikhd->ihqk', pieces[0], pieces[1], precision=highest) * head_dim ** (-0.5)
    attention_p = jax.nn.softmax(low_back(logits), axis=-1)
    mixture = jnp.einsum('ihqk,ikhd->iqhd', low(attention_p), pieces[2], precision=highest)
    mixture = low_back(low(mixture)).reshape(images, L, D)
    return stream + low_back(jnp.einsum('ile,ed->ild', mixture, w_out, precision=highest))

def dense_mlp(stream, norm_gain, dense_in, dense_out):
    normed = low(norm_rows(stream, norm_gain))
    pre_act = low_back(jnp.einsum('ild,df->ilf', normed, dense_in, precision=highest))
    activated = low(jax.nn.gelu(pre_act, approximate=False))
    return stream + low_back(jnp.einsum('ilf,fd->ild', activated, dense_out, precision=highest))

def inverse(slot_index):
    tokens = slot_index.shape[0]
    token_ids = jnp.repeat(jnp.arange(tokens, dtype=jnp.int32), 2)
    flat_slots = slot_index.reshape(tokens * 2)
    slot_token = jnp.zeros((EXPERTS * CAP,), jnp.int32).at[flat_slots].set(token_ids)
    filled = jnp.zeros((EXPERTS * CAP,), jnp.float32).at[flat_slots].set(1.0)
    return (slot_token, filled)

def take_rows(table, index):
    return jnp.take(table, index, axis=0)

def expert_layer(stream, norm_gain, in_experts, out_experts, route_ids, route_slots, gate_weights):
    tokens = IMG_DEV * L
    normed = low(norm_rows(stream, norm_gain)).reshape(N_DP, tokens, D)
    slot_index = (route_ids * CAP + route_slots).astype(jnp.int32).reshape(N_DP, tokens, 2)
    slot_token, filled = jax.vmap(inverse)(slot_index)
    dispatched = jax.vmap(take_rows)(normed, slot_token) * filled[:, :, None]
    dispatched = low_back(dispatched.reshape(N_DP, EXPERTS, CAP, D))
    pre_act = low_back(jnp.einsum('secd,edf->secf', dispatched, in_experts, precision=highest))
    activated = low(jax.nn.gelu(pre_act, approximate=False))
    returned = low_back(low(jnp.einsum('secf,efd->secd', activated, out_experts, precision=highest)))
    returned = returned.reshape(N_DP, EXPERTS * CAP, D)
    picked = jax.vmap(take_rows)(returned, slot_index.reshape(N_DP, tokens * 2))
    picked = picked.reshape(N_DP, tokens, 2, D)
    mixture = lax.optimization_barrier(jnp.sum(picked * gate_weights.reshape(N_DP, tokens, 2, 1), axis=2))
    return stream + mixture.reshape(stream.shape)

def section_pair(stream, norm_gains, attn_qkv, attn_out, mlp_in, mlp_out, expert_in, expert_out, route_ids, route_slots, gate_weights):
    stream = attention(stream, norm_gains[0], attn_qkv[0], attn_out[0])
    stream = dense_mlp(stream, norm_gains[1], mlp_in, mlp_out)
    stream = attention(stream, norm_gains[2], attn_qkv[1], attn_out[1])
    return expert_layer(stream, norm_gains[3], expert_in, expert_out, route_ids, route_slots, gate_weights)

def reference(boundary, norm_gains, attn_qkv, attn_out, mlp_in, mlp_out, expert_in, expert_out, expert_ids, expert_slots, gate_weights):
    wide = boundary.astype(jnp.float32)
    inputs = wide[0]
    cotangent = wide[1]
    params = (norm_gains.astype(jnp.float32), attn_qkv.astype(jnp.float32), attn_out.astype(jnp.float32), mlp_in.astype(jnp.float32), mlp_out.astype(jnp.float32), expert_in.astype(jnp.float32), expert_out.astype(jnp.float32))

    def forward(inputs, params):
        outputs = []
        for micro_index in range(MICRO):
            stream = inputs[micro_index]
            for section_index in range(SECTIONS):
                if section_index > 0:
                    stream = low_back(low(stream))
                weights = [member[section_index] for member in params]
                stream = section_pair(stream, *weights, expert_ids[section_index, micro_index], expert_slots[section_index, micro_index], gate_weights[section_index, micro_index])
            outputs.append(stream)
        return jnp.stack(outputs)
    result, pullback = jax.vjp(forward, inputs, params)
    grad_inputs, grads = pullback(cotangent)
    return (jnp.stack([grad_inputs, result]), grads[0], grads[1], grads[2], grads[3], grads[4], grads[5], grads[6])
```

```python
import functools

import jax
import jax.numpy as jnp
from jax import lax
from jax.experimental import pallas as pl
from jax.experimental.pallas import tpu as pltpu
from jax.sharding import PartitionSpec as P

MESH = pl.DeviceIdType.MESH
BF16 = jnp.bfloat16
F32 = jnp.float32
HEAD_DIM = 64
EPSILON = 1e-06
CAP = 20
MAIN = 16
MICRO = 2


def dims(lhs, rhs, left_dim, right_dim):
    return lax.dot_general(
        lhs, rhs, (((left_dim,), (right_dim,)), ((), ())), preferred_element_type=F32
    )


def nn(lhs, rhs):
    return dims(lhs, rhs, 1, 0)


def nt(lhs, rhs):
    return dims(lhs, rhs, 1, 1)


def tn(lhs, rhs):
    return dims(lhs, rhs, 0, 0)


def gelu_both(pre):
    phi = 0.5 * (1.0 + lax.erf(pre * 0.7071067811865476))
    density = 0.3989422804014327 * jnp.exp(-0.5 * pre * pre)
    return pre * phi, phi + pre * density


def kernel(
    nx,
    nd,
    bnd,
    rt_in,
    sa,
    sm,
    sg,
    ein,
    eout,
    res,
    ra,
    rm,
    rg,
    eo,
    ep,
    wa,
    wm,
    we,
    wg,
    gn,
    rt,
    gt,
    bx,
    sel,
    pk,
    hs,
    ags,
    rs_out,
    rs_in,
    a2_out,
    a2_in,
    proj,
    mix,
    prb,
    dgm,
    act,
    arr,
    dge,
    ace,
    ga,
    gm,
    pa,
    pm,
    eg,
    dgn,
    gx,
    gs,
    cur,
    hout,
    gout,
    ag_send,
    ag_recv,
    rs_send,
    rs_recv,
    a2_send,
    a2_recv,
    w_send,
    w_recv,
    w_own,
    wf_send,
    wf_recv,
    m_send,
    m_recv,
    m_own,
    pg_send,
    pg_recv,
    ch_send,
    ch_recv,
    ch_own,
    e_send,
    e_recv,
    e_own,
    res_send,
    res_recv,
    res_own,
    gx_send,
    gx_recv,
    rg_send,
    rg_recv,
    rg_own,
):
    core = lax.axis_index("pipe")
    md = lax.axis_index("dp")
    mx = lax.axis_index("tensor")
    other = 1 - core
    rows, features = cur.shape
    tokens = nx * rows
    shard_rows = sg.shape[0]
    wide_features = wa.shape[4]
    heads = wide_features // HEAD_DIM
    quarters = features // 256
    slots = nd * CAP
    extras = CAP - MAIN

    def x_peer(step):
        return lax.rem(mx + step, nx)

    def d_peer(step):
        return lax.rem(md + step, nd)

    def remote(src, dst, send, recv, **where):
        return pltpu.make_async_remote_copy(
            src_ref=src,
            dst_ref=dst,
            send_sem=send,
            recv_sem=recv,
            device_id=where,
            device_id_type=MESH,
        )

    def local(src, dst, sem):
        return pltpu.make_async_copy(src, dst, sem)

    def wait_for(ref, sem):
        pltpu.make_async_copy(ref, ref, sem).wait()

    barrier = pltpu.get_barrier_semaphore()

    def greet(step, carry):
        pl.semaphore_signal(
            barrier, inc=1, device_id={"dp": d_peer(step)}, device_id_type=MESH
        )
        return carry

    lax.fori_loop(1, nd, greet, 0)
    for step in range(1, nx):
        pl.semaphore_signal(
            barrier, inc=1, device_id={"tensor": x_peer(step)}, device_id_type=MESH
        )
    for step in range(nx):
        pl.semaphore_signal(
            barrier,
            inc=1,
            device_id={"pipe": other, "tensor": x_peer(step)},
            device_id_type=MESH,
        )
    pl.semaphore_wait(barrier, (nd - 1) + (nx - 1) + nx)

    mine = pl.ds(md * shard_rows, shard_rows)
    shard_src = (sg, sa.at[0], sm, sa.at[1])
    shard_dst = (
        wg.at[core, mine],
        wa.at[core, 0, :, mine],
        wm.at[core, :, mine],
        wa.at[core, 1, :, mine],
    )

    def share_weight(which):
        def push(step, carry):
            remote(
                shard_src[which],
                shard_dst[which],
                w_send.at[which],
                w_recv.at[which],
                dp=d_peer(step),
            ).start()
            return carry

        local(shard_src[which], shard_dst[which], w_own.at[which]).start()
        lax.fori_loop(1, nd, push, 0)

    all_but_one = pl.ds(0, (nd - 1) * shard_rows)
    whole = (wg, wa.at[:, 0], wm, wa.at[:, 1])

    def arrived_part(which):
        if which == 0:
            return wg.at[0, all_but_one]
        if which == 2:
            return wm.at[0, :, all_but_one]
        return wa.at[0, which // 2, :, all_but_one]

    def whole_part(which, section):
        if which == 0:
            return wg.at[section]
        if which == 2:
            return wm.at[section]
        return wa.at[section, which // 2]

    def weight_forward(which):
        wait_for(arrived_part(which), w_recv.at[which])
        local(shard_src[which], shard_dst[which], w_own.at[which]).wait()
        remote(
            whole_part(which, core),
            whole_part(which, core),
            wf_send.at[which],
            wf_recv.at[which],
            pipe=other,
        ).start()

    def weight_ready(which):
        wait_for(whole_part(which, 0), wf_recv.at[which])

    def misc_copies():
        part = pl.ds(mx * rows, rows)
        return (
            remote(bnd.at[other, part], bx, m_send.at[0], m_recv.at[0], pipe=other),
            remote(rt_in.at[other], rt.at[core], m_send.at[1], m_recv.at[1], pipe=other),
        )

    def expert_copies():
        return (
            remote(ein, we.at[core, 0], m_send.at[2], m_recv.at[2], pipe=other),
            remote(eout, we.at[core, 1], m_send.at[3], m_recv.at[3], pipe=other),
        )

    def expert_own():
        return (
            local(ein, we.at[core, 0], m_own.at[0]),
            local(eout, we.at[core, 1], m_own.at[1]),
        )

    for copy in misc_copies():
        copy.start()
    share_weight(0)
    share_weight(1)
    for copy in expert_copies() + expert_own():
        copy.start()
    share_weight(2)
    share_weight(3)

    rt[core] = rt_in[core]
    row_id = lax.broadcasted_iota(jnp.int32, (nd * 16, nd * extras), 0)
    col_id = lax.broadcasted_iota(jnp.int32, (nd * 16, nd * extras), 1)
    for q in range(quarters):
        hit = (
            ((row_id >> 4) == (col_id >> 2))
            & (((row_id >> 2) & 3) == q)
            & ((row_id & 3) == (col_id & 3))
        )
        sel[q] = jnp.where(hit, 1.0, 0.0).astype(BF16)
    dgn[...] = jnp.zeros_like(dgn)

    for copy in misc_copies():
        copy.wait()
    place = lax.broadcasted_iota(jnp.int32, (slots, tokens), 0)
    for s in range(2):
        table = rt[s]
        for k in range(2):
            hit = place == table[k : k + 1].astype(jnp.int32)
            pk[s, k] = jnp.where(hit, 1.0, 0.0).astype(BF16)
        gt[s] = jnp.transpose(jnp.concatenate([table] * (tokens // 8), axis=0))

    @pl.when(core == 0)
    def first_input():
        cur[...] = bnd[0, pl.ds(mx * rows, rows)].astype(F32)

    @pl.when(core == 1)
    def second_input():
        cur[...] = bx[...].astype(F32)

    weight_forward(0)
    weight_ready(0)
    for s in range(2):
        turned = jnp.transpose(wg[s].astype(F32))
        gn[s] = turned[:8]

    lane = lax.broadcasted_iota(jnp.int32, (1, wide_features), 1)
    head_masks = [
        jnp.where((lane >= h * HEAD_DIM) & (lane < (h + 1) * HEAD_DIM), 1.0, 0.0).astype(BF16)
        for h in range(heads)
    ]

    def per_head(values):
        return [values * mask for mask in head_masks]

    def norm_parts(stream):
        center = stream - jnp.mean(stream, axis=-1, keepdims=True)
        scale = lax.rsqrt(jnp.mean(center * center, axis=-1, keepdims=True) + EPSILON)
        return center * scale, scale

    def norm_back(s, k, grad_normed):
        normal, scale = norm_parts(hs[s, k])
        dgn[s, k : k + 1, :] = jnp.sum(grad_normed * normal, axis=0, keepdims=True)
        pulled = grad_normed * gn[s][k : k + 1]
        return scale * (
            pulled
            - jnp.mean(pulled, axis=-1, keepdims=True)
            - normal * jnp.mean(pulled * normal, axis=-1, keepdims=True)
        )

    some = pl.ds(0, nx - 1)

    def all_rows(s, way, k, own_rows):
        ags[s, way, k, mx] = own_rows.astype(BF16)
        for step in range(1, nx):
            remote(
                ags.at[s, way, k, mx],
                ags.at[s, way, k, mx],
                ag_send.at[0],
                ag_recv.at[s, way, k],
                tensor=x_peer(step),
            ).start()
        wait_for(ags.at[s, way, k, some], ag_recv.at[s, way, k])
        wait_for(ags.at[s, way, k, some], ag_send.at[0])
        return ags[s, way, k].reshape(tokens, features)

    def sum_start(s, way, k, partial_rows):
        rs_out[...] = partial_rows.astype(BF16).reshape(nx, rows, features)
        for step in range(1, nx):
            peer = x_peer(step)
            remote(
                rs_out.at[peer],
                rs_in.at[s, way, k, mx],
                rs_send.at[0],
                rs_recv.at[s, way, k],
                tensor=peer,
            ).start()

    def sum_end(s, way, k):
        wait_for(rs_in.at[s, way, k, some], rs_recv.at[s, way, k])
        wait_for(rs_out.at[some], rs_send.at[0])
        total = rs_out[mx].astype(F32)
        for step in range(1, nx):
            total = total + rs_in[s, way, k, x_peer(step)].astype(F32)
        return total

    def slots_start(s, which, values):
        main = values[: nd * MAIN]
        extra = values[nd * MAIN :]
        folded = None
        for q in range(quarters):
            columns = slice(256 * q, 256 * (q + 1))
            a2_out[:, 16 * q : 16 * (q + 1), :] = main[:, columns].reshape(nd, 16, 256)
            term = nn(sel[q], extra[:, columns])
            folded = term if folded is None else folded + term
        a2_out[:, 16 * quarters :, :] = folded.astype(BF16).reshape(nd, 16, 256)

        def push(step, carry):
            peer = d_peer(step)
            remote(
                a2_out.at[peer],
                a2_in.at[s, which, md],
                a2_send.at[0],
                a2_recv.at[s, which],
                dp=peer,
            ).start()
            return carry

        lax.fori_loop(1, nd, push, 0)
        a2_in[s, which, md] = a2_out[md]

    def slots_end(s, which):
        wait_for(a2_in.at[s, which, pl.ds(0, nd - 1)], a2_recv.at[s, which])
        wait_for(a2_out.at[pl.ds(0, nd - 1)], a2_send.at[0])
        mains = []
        extra = []
        folded = a2_in[s, which, :, 16 * quarters :, :].reshape(nd * 16, 256)
        for q in range(quarters):
            block = a2_in[s, which, :, 16 * q : 16 * (q + 1), :]
            mains.append(block.reshape(nd * 16, 256))
            extra.append(tn(sel[q], folded).astype(BF16))
        return jnp.concatenate(
            [jnp.concatenate(mains, axis=1), jnp.concatenate(extra, axis=1)], axis=0
        )

    def attend(s, j, k):
        stream = cur[...]
        hs[s, k] = stream
        normal, unused = norm_parts(stream)
        normed = all_rows(s, 0, k, normal * gn[s][k : k + 1])

        @pl.when(s == 0)
        def weights():
            weight_ready(1 + 2 * j)

        query, key, value = [nn(normed, wa[s, j, c]).astype(BF16) for c in range(3)]
        proj[s, j, 0] = query
        proj[s, j, 1] = key
        proj[s, j, 2] = value
        logits = nt(jnp.concatenate(per_head(query), axis=0), key) * (HEAD_DIM**-0.5)
        exponent = jnp.exp(logits - jnp.max(logits, axis=-1, keepdims=True))
        probs = exponent / jnp.sum(exponent, axis=-1, keepdims=True)
        prb[s, j] = probs
        low = probs.astype(BF16)
        mixed = None
        for h, part in enumerate(per_head(value)):
            term = nn(low[h * tokens : (h + 1) * tokens], part)
            mixed = term if mixed is None else mixed + term
        mixed = mixed.astype(BF16)
        mix[s, j] = mixed
        sum_start(s, 0, k, nt(mixed, wa[s, j, 3]))

        if j == 0:

            @pl.when(s == 0)
            def onward():
                weight_forward(2)

        cur[...] = stream + sum_end(s, 0, k)

    def feed(s):
        stream = cur[...]
        hs[s, 1] = stream
        normal, unused = norm_parts(stream)
        normed = all_rows(s, 0, 1, normal * gn[s][1:2])

        @pl.when(s == 0)
        def weights():
            weight_ready(2)

        active, slope = gelu_both(nn(normed, wm[s, 0]))
        active = active.astype(BF16)
        dgm[s] = slope
        act[s] = active
        sum_start(s, 0, 1, nt(active, wm[s, 1]))

        @pl.when(s == 0)
        def onward():
            weight_forward(3)

        cur[...] = stream + sum_end(s, 0, 1)

    def experts(s):
        stream = cur[...]
        hs[s, 3] = stream
        normal, unused = norm_parts(stream)
        normed = all_rows(s, 0, 3, normal * gn[s][3:4])
        slots_start(s, 0, nn(pk[s, 0] + pk[s, 1], normed).astype(BF16))

        @pl.when(s == 0)
        def weights():
            for copy in expert_copies() + expert_own():
                copy.wait()

        sent = slots_end(s, 0)
        arr[s] = sent
        active, slope = gelu_both(nn(sent, we[s, 0]))
        active = active.astype(BF16)
        ace[s] = active
        dge[s] = slope
        slots_start(s, 1, nn(active, we[s, 1]).astype(BF16))
        back = slots_end(s, 1)
        gates = gt[s]
        partial_rows = tn(pk[s, 0], back) * gates[:, 2:3] + tn(pk[s, 1], back) * gates[:, 3:4]
        sum_start(s, 0, 3, partial_rows)
        cur[...] = stream + sum_end(s, 0, 3)

    def forward(s, carry):
        cur[...] = cur[...].astype(BF16).astype(F32)
        attend(s, 0, 0)
        feed(s)
        attend(s, 1, 2)
        experts(s)
        return carry

    def result_copies(buffer, target, start):
        slot = core * nx + mx

        @pl.when(core == target)
        def near():
            copy = local(buffer, res.at[slot], res_own.at[0])
            copy.start() if start else copy.wait()

        @pl.when(core != target)
        def far():
            copy = remote(
                buffer,
                res.at[slot],
                res_send.at[1],
                res_recv.at[0],
                pipe=target,
            )
            copy.start() if start else copy.wait_send()

        for step in range(1, nx):
            copy = remote(
                buffer,
                res.at[slot],
                res_send.at[1 + step],
                res_recv.at[0],
                pipe=target,
                tensor=x_peer(step),
            )
            copy.start() if start else copy.wait_send()

    weight_forward(1)
    lax.fori_loop(0, 2, forward, 0)
    hout[...] = cur[...]
    result_copies(hout, 1, True)

    staged = (ga.at[0], gm, ga.at[1])
    partner = (pa.at[0], pm, pa.at[1])
    landing = (ra.at[0], rm, ra.at[1])

    def chunk(which, owner):
        return staged[which].at[:, pl.ds(owner * shard_rows, shard_rows)]

    def staged_wait(which, section):
        @pl.when(core == section)
        def owned():
            wait_for(staged[which].at[:, all_but_one], ch_send.at[which])
            local(chunk(which, md), landing[which].at[md], ch_own.at[which]).wait()

        @pl.when(core != section)
        def lent():
            wait_for(staged[which], pg_send.at[which])

    def lend(which, section):
        @pl.when(core != section)
        def lent():
            remote(
                staged[which],
                partner[which],
                pg_send.at[which],
                pg_recv.at[which],
                pipe=other,
            ).start()

    def combine(which, section):
        @pl.when(core == section)
        def owned():
            wait_for(partner[which], pg_recv.at[which])
            for c in range(staged[which].shape[0]):
                staged[which][c] = (
                    staged[which][c].astype(F32) + partner[which][c].astype(F32)
                ).astype(BF16)

            def push(step, carry):
                peer = d_peer(step)
                remote(
                    chunk(which, peer),
                    landing[which].at[md],
                    ch_send.at[which],
                    ch_recv.at[which],
                    dp=peer,
                ).start()
                return carry

            lax.fori_loop(1, nd, push, 0)
            local(chunk(which, md), landing[which].at[md], ch_own.at[which]).start()

    def experts_back(s):
        grad = cur[...]
        wide = all_rows(s, 1, 3, grad).astype(F32)
        gates = gt[s]
        dback = nn(pk[s, 0], (wide * gates[:, 2:3]).astype(BF16)) + nn(
            pk[s, 1], (wide * gates[:, 3:4]).astype(BF16)
        )
        slots_start(s, 2, dback.astype(BF16))

        @pl.when(s == 0)
        def late():
            combine(0, 1)

        dback = slots_end(s, 2)
        dpre = (nt(dback, we[s, 1]) * dge[s]).astype(BF16)
        slots_start(s, 3, nt(dpre, we[s, 0]).astype(BF16))
        eg[0] = tn(arr[s], dpre)
        eg[1] = tn(ace[s], dback)

        @pl.when(core == s)
        def keep():
            local(eg, eo, e_own.at[0]).start()

        @pl.when(core != s)
        def give():
            remote(eg, ep, e_send.at[0], e_recv.at[0], pipe=other).start()

        dsent = slots_end(s, 3)
        sum_start(s, 1, 3, tn(pk[s, 0] + pk[s, 1], dsent))
        cur[...] = grad + norm_back(s, 3, sum_end(s, 1, 3))

    def attend_back(s, j, k):
        grad = cur[...]
        dz = all_rows(s, 1, k, grad)
        dmixed = nn(dz, wa[s, j, 3]).astype(BF16)
        query, key, value = [proj[s, j, c] for c in range(3)]
        probs = prb[s, j]
        dmixed_heads = jnp.concatenate(per_head(dmixed), axis=0)
        dprobs = nt(dmixed_heads, value)
        dscores = probs * (dprobs - jnp.sum(probs * dprobs, axis=-1, keepdims=True))
        dscores = dscores.astype(BF16)
        dvalue = tn(probs.astype(BF16), dmixed_heads)
        dkey = tn(dscores, jnp.concatenate(per_head(query), axis=0)) * (HEAD_DIM**-0.5)
        dquery = None
        for h, part in enumerate(per_head(key)):
            term = nn(dscores[h * tokens : (h + 1) * tokens], part)
            dquery = term if dquery is None else dquery + term
        dquery = dquery * (HEAD_DIM**-0.5)
        dproj = [d.astype(BF16) for d in (dquery, dkey, dvalue)]
        partial_rows = None
        for c in range(3):
            term = nt(dproj[c], wa[s, j, c])
            partial_rows = term if partial_rows is None else partial_rows + term
        sum_start(s, 1, k, partial_rows)

        @pl.when(s == 0)
        def free():
            staged_wait(2 * j, 1)

        normed = ags[s, 0, k].reshape(tokens, features)
        for c in range(3):
            ga[j, c] = tn(normed, dproj[c]).astype(BF16)
        ga[j, 3] = tn(dz, mix[s, j]).astype(BF16)
        lend(2 * j, s)
        if j == 0:
            combine(1, s)
        cur[...] = grad + norm_back(s, k, sum_end(s, 1, k))

    def feed_back(s):
        grad = cur[...]
        dout = all_rows(s, 1, 1, grad)
        dpre = (nn(dout, wm[s, 1]) * dgm[s]).astype(BF16)
        sum_start(s, 1, 1, nt(dpre, wm[s, 0]))

        @pl.when(s == 0)
        def free():
            staged_wait(1, 1)

        normed = ags[s, 0, 1].reshape(tokens, features)
        gm[0] = tn(normed, dpre).astype(BF16)
        gm[1] = tn(dout, act[s]).astype(BF16)
        lend(1, s)
        combine(2, s)
        cur[...] = grad + norm_back(s, 1, sum_end(s, 1, 1))

    def expert_grads_wait(s):
        @pl.when(core == s)
        def keep():
            local(eg, eo, e_own.at[0]).wait()

        @pl.when(core != s)
        def give():
            wait_for(eg, e_send.at[0])

    def backward(turn, carry):
        s = 1 - turn
        cur[...] = cur[...].astype(BF16).astype(F32)
        experts_back(s)
        attend_back(s, 1, 2)
        feed_back(s)
        attend_back(s, 0, 0)
        expert_grads_wait(s)
        return carry

    @pl.when(core == 1)
    def own_cotangent():
        cur[...] = bnd[1, pl.ds(mx * rows, rows)].astype(F32)

    @pl.when(core == 0)
    def sent_cotangent():
        cur[...] = bx[...].astype(F32)

    lax.fori_loop(0, 2, backward, 0)
    gout[...] = cur[...]
    result_copies(hout, 1, False)
    result_copies(gout, 0, True)

    place_here = core * nx + mx
    for section in range(2):

        @pl.when(core == section)
        def near():
            gx[place_here] = dgn[section]

        @pl.when(core != section)
        def far():
            remote(
                dgn.at[section],
                gx.at[place_here],
                gx_send.at[section, 0],
                gx_recv.at[0],
                pipe=section,
            ).start()

        for step in range(1, nx):
            remote(
                dgn.at[section],
                gx.at[place_here],
                gx_send.at[section, step],
                gx_recv.at[0],
                pipe=section,
                tensor=x_peer(step),
            ).start()
    combine(0, 0)
    wait_for(gx.at[pl.ds(0, 2 * nx - 1)], gx_recv.at[0])
    gains_total = gx[0]
    for source in range(1, 2 * nx):
        gains_total = gains_total + gx[source]
    gs[...] = gains_total

    def push_gains(step, carry):
        remote(gs, rg.at[md], rg_send.at[0], rg_recv.at[0], dp=d_peer(step)).start()
        return carry

    lax.fori_loop(1, nd, push_gains, 0)
    local(gs, rg.at[md], rg_own.at[0]).start()

    for section in range(2):

        @pl.when(core != section)
        def far_end():
            wait_for(dgn.at[section], gx_send.at[section, 0])

        for step in range(1, nx):
            wait_for(dgn.at[section], gx_send.at[section, step])
    for which in range(4):
        wait_for(whole_part(which, 0), wf_send.at[which])
        wait_for(arrived_part(which), w_send.at[which])
    result_copies(gout, 0, False)
    wait_for(res.at[pl.ds(0, 2 * nx - 1)], res_recv.at[0])
    for which in range(3):
        staged_wait(which, 0)
        wait_for(landing[which].at[pl.ds(0, nd - 1)], ch_recv.at[which])
    wait_for(ep, e_recv.at[0])
    wait_for(rg.at[pl.ds(0, nd - 1)], rg_recv.at[0])
    wait_for(rg.at[pl.ds(0, nd - 1)], rg_send.at[0])
    local(gs, rg.at[md], rg_own.at[0]).wait()


def shards(
    nx,
    nd,
    boundary,
    norm_gains,
    attn_qkv,
    attn_out,
    mlp_in,
    mlp_out,
    expert_in,
    expert_out,
    expert_ids,
    expert_slots,
    gate_weights,
):
    tokens, features = boundary.shape[3:]
    rows = tokens // nx
    shard_rows = features // nd
    wide = attn_qkv.shape[4]
    units = mlp_in.shape[2]
    hidden = expert_in.shape[3]
    slots = nd * CAP
    quarters = features // 256
    slab = 16 * quarters + 16
    heads = wide // HEAD_DIM

    slot = expert_slots[0, :, 0]
    owner = expert_ids[0, :, 0]
    place = jnp.where(
        slot < MAIN,
        owner * MAIN + slot,
        nd * MAIN + owner * (CAP - MAIN) + slot - MAIN,
    )
    table = jnp.concatenate(
        [
            jnp.swapaxes(place, 1, 2).astype(F32),
            jnp.swapaxes(gate_weights[0, :, 0], 1, 2),
            jnp.zeros((MICRO, 4, tokens), F32),
        ],
        axis=1,
    )
    sa = jnp.concatenate([attn_qkv[0], jnp.swapaxes(attn_out[0], 1, 2)[:, None]], axis=1)
    sm = jnp.stack([mlp_in[0], mlp_out[0].T])
    sg = jnp.pad(norm_gains[0].T, ((0, 0), (0, 128 - norm_gains.shape[1])))

    vmem = pl.BlockSpec(memory_space=pltpu.VMEM)
    hbm = pl.BlockSpec(memory_space=pl.ANY)
    dma = pltpu.SemaphoreType.DMA
    scratch = [
        pltpu.VMEM((2, 2, 4, features, wide), BF16),
        pltpu.VMEM((2, 2, features, units), BF16),
        pltpu.VMEM((2, 2, features, hidden), BF16),
        pltpu.VMEM((2, features, 128), BF16),
        pltpu.VMEM((2, 8, features), F32),
        pltpu.VMEM((2, 8, tokens), F32),
        pltpu.VMEM((2, tokens, tokens), F32),
        pltpu.VMEM((rows, features), BF16),
        pltpu.VMEM((quarters, nd * 16, nd * (CAP - MAIN)), BF16),
        pltpu.VMEM((2, 2, slots, tokens), BF16),
        pltpu.VMEM((2, 4, rows, features), F32),
        pltpu.VMEM((2, 2, 4, nx, rows, features), BF16),
        pltpu.VMEM((nx, rows, features), BF16),
        pltpu.VMEM((2, 2, 4, nx, rows, features), BF16),
        pltpu.VMEM((nd, slab, 256), BF16),
        pltpu.VMEM((2, 4, nd, slab, 256), BF16),
        pltpu.VMEM((2, 2, 3, tokens, wide), BF16),
        pltpu.VMEM((2, 2, tokens, wide), BF16),
        pltpu.VMEM((2, 2, heads * tokens, tokens), F32),
        pltpu.VMEM((2, tokens, units), F32),
        pltpu.VMEM((2, tokens, units), BF16),
        pltpu.VMEM((2, slots, features), BF16),
        pltpu.VMEM((2, slots, hidden), F32),
        pltpu.VMEM((2, slots, hidden), BF16),
        pltpu.VMEM((2, 4, features, wide), BF16),
        pltpu.VMEM((2, features, units), BF16),
        pltpu.VMEM((2, 4, features, wide), BF16),
        pltpu.VMEM((2, features, units), BF16),
        pltpu.VMEM((2, features, hidden), F32),
        pltpu.VMEM((2, 8, features), F32),
        pltpu.VMEM((2 * nx, 8, features), F32),
        pltpu.VMEM((8, features), F32),
        pltpu.VMEM((rows, features), F32),
        pltpu.VMEM((rows, features), F32),
        pltpu.VMEM((rows, features), F32),
        dma((1,)),
        dma((2, 2, 4)),
        dma((1,)),
        dma((2, 2, 4)),
        dma((1,)),
        dma((2, 4)),
        dma((4,)),
        dma((4,)),
        dma((4,)),
        dma((4,)),
        dma((4,)),
        dma((4,)),
        dma((4,)),
        dma((2,)),
        dma((3,)),
        dma((3,)),
        dma((3,)),
        dma((3,)),
        dma((3,)),
        dma((1,)),
        dma((1,)),
        dma((1,)),
        dma((1 + nx,)),
        dma((1,)),
        dma((1,)),
        dma((2, nx)),
        dma((1,)),
        dma((1,)),
        dma((1,)),
        dma((1,)),
    ]
    res, ra, rm, rg, eo, ep = pl.pallas_call(
        functools.partial(kernel, nx, nd),
        out_shape=(
            jax.ShapeDtypeStruct((2 * nx, rows, features), F32),
            jax.ShapeDtypeStruct((2, nd, 4, shard_rows, wide), BF16),
            jax.ShapeDtypeStruct((nd, 2, shard_rows, units), BF16),
            jax.ShapeDtypeStruct((nd, 8, features), F32),
            jax.ShapeDtypeStruct((2, features, hidden), F32),
            jax.ShapeDtypeStruct((2, features, hidden), F32),
        ),
        in_specs=[vmem, vmem, hbm, hbm, hbm, hbm, hbm],
        out_specs=(hbm,) * 6,
        scratch_shapes=scratch,
        compiler_params=pltpu.CompilerParams(
            collective_id=0, has_side_effects=True, vmem_limit_bytes=VMEM_LIMIT
        ),
    )(boundary[0, :, 0], table, sa, sm, sg, expert_in[0, 0], expert_out[0, 0])

    dense = jnp.sum(ra.astype(F32), axis=1)
    feed = jnp.sum(rm.astype(F32), axis=0)
    gains = jnp.sum(rg, axis=0)[: norm_gains.shape[1]]
    gains = lax.dynamic_slice_in_dim(gains, lax.axis_index("dp") * shard_rows, shard_rows, 1)
    expert = eo + ep
    return (
        res.reshape(1, MICRO, 1, tokens, features),
        gains[None],
        dense[None, :, :3],
        jnp.swapaxes(dense[:, 3], 1, 2)[None],
        feed[0][None],
        feed[1].T[None],
        expert[0][None, None],
        expert[1][None, None],
    )


VMEM_LIMIT = 62 * 1024 * 1024


def solution(mesh):
    in_specs = (
        P("pipe", None, "dp", None, None),
        P("pipe", None, "dp"),
        P("pipe", None, None, "dp", "tensor"),
        P("pipe", None, "tensor", "dp"),
        P("pipe", "dp", "tensor"),
        P("pipe", "tensor", "dp"),
        P("pipe", "dp", None, "tensor"),
        P("pipe", "dp", "tensor", None),
        P("pipe", None, "dp", None, None),
        P("pipe", None, "dp", None, None),
        P("pipe", None, "dp", None, None),
    )
    out_specs = (
        P("pipe", None, "dp", None, None),
        P("pipe", None, "dp"),
        P("pipe", None, None, "dp", "tensor"),
        P("pipe", None, "tensor", "dp"),
        P("pipe", "dp", "tensor"),
        P("pipe", "tensor", "dp"),
        P("pipe", "dp", None, "tensor"),
        P("pipe", "dp", "tensor", None),
    )
    return jax.shard_map(
        functools.partial(shards, mesh.shape["tensor"], mesh.shape["dp"]),
        mesh=mesh,
        in_specs=in_specs,
        out_specs=out_specs,
        check_vma=False,
    )
```

```python
import functools

import jax
import jax.numpy as jnp
from jax import lax
from jax.experimental import pallas as pl
from jax.experimental.pallas import tpu as pltpu
from jax.sharding import PartitionSpec as P

MESH = pl.DeviceIdType.MESH
BF16 = jnp.bfloat16
F32 = jnp.float32
HEAD_DIM = 64
EPSILON = 1e-06
CAP = 20
MAIN = 16
MICRO = 2


def dims(lhs, rhs, left_dim, right_dim):
    return lax.dot_general(
        lhs, rhs, (((left_dim,), (right_dim,)), ((), ())), preferred_element_type=F32
    )


def nn(lhs, rhs):
    return dims(lhs, rhs, 1, 0)


def nt(lhs, rhs):
    return dims(lhs, rhs, 1, 1)


def tn(lhs, rhs):
    return dims(lhs, rhs, 0, 0)


def gelu_both(pre):
    phi = 0.5 * (1.0 + lax.erf(pre * 0.7071067811865476))
    density = 0.3989422804014327 * jnp.exp(-0.5 * pre * pre)
    return pre * phi, phi + pre * density


def kernel(
    nx,
    nd,
    bnd,
    rt_in,
    sa,
    sm,
    sg,
    ein,
    eout,
    res,
    ra,
    rm,
    rg,
    eo,
    ep,
    wa,
    wm,
    we,
    wg,
    gn,
    rt,
    gt,
    bx,
    sel,
    pk,
    hs,
    ags,
    rs_out,
    rs_in,
    a2_out,
    a2_in,
    proj,
    mix,
    prb,
    dgm,
    act,
    arr,
    dge,
    ace,
    ga,
    gm,
    pa,
    pm,
    eg,
    dgn,
    gx,
    gs,
    cur,
    hout,
    gout,
    ag_send,
    ag_recv,
    rs_send,
    rs_recv,
    a2_send,
    a2_recv,
    w_send,
    w_recv,
    w_own,
    wf_send,
    wf_recv,
    m_send,
    m_recv,
    m_own,
    pg_send,
    pg_recv,
    ch_send,
    ch_recv,
    ch_own,
    e_send,
    e_recv,
    e_own,
    res_send,
    res_recv,
    res_own,
    gx_send,
    gx_recv,
    rg_send,
    rg_recv,
    rg_own,
):
    core = lax.axis_index("pipe")
    md = lax.axis_index("dp")
    mx = lax.axis_index("tensor")
    other = 1 - core
    rows, features = cur.shape
    tokens = nx * rows
    shard_rows = sg.shape[0]
    wide_features = wa.shape[4]
    heads = wide_features // HEAD_DIM
    quarters = features // 256
    slots = nd * CAP
    extras = CAP - MAIN

    def x_peer(step):
        return lax.rem(mx + step, nx)

    def d_peer(step):
        return lax.rem(md + step, nd)

    def remote(src, dst, send, recv, **where):
        return pltpu.make_async_remote_copy(
            src_ref=src,
            dst_ref=dst,
            send_sem=send,
            recv_sem=recv,
            device_id=where,
            device_id_type=MESH,
        )

    def local(src, dst, sem):
        return pltpu.make_async_copy(src, dst, sem)

    def wait_for(ref, sem):
        pltpu.make_async_copy(ref, ref, sem).wait()

    barrier = pltpu.get_barrier_semaphore()

    def greet(step, carry):
        pl.semaphore_signal(
            barrier, inc=1, device_id={"dp": d_peer(step)}, device_id_type=MESH
        )
        return carry

    lax.fori_loop(1, nd, greet, 0)
    for step in range(1, nx):
        pl.semaphore_signal(
            barrier, inc=1, device_id={"tensor": x_peer(step)}, device_id_type=MESH
        )
    for step in range(nx):
        pl.semaphore_signal(
            barrier,
            inc=1,
            device_id={"pipe": other, "tensor": x_peer(step)},
            device_id_type=MESH,
        )
    pl.semaphore_wait(barrier, (nd - 1) + (nx - 1) + nx)

    mine = pl.ds(md * shard_rows, shard_rows)
    shard_src = (sg, sa.at[0], sm, sa.at[1])
    shard_dst = (
        wg.at[core, mine],
        wa.at[core, 0, :, mine],
        wm.at[core, :, mine],
        wa.at[core, 1, :, mine],
    )

    def share_weight(which):
        def push(step, carry):
            remote(
                shard_src[which],
                shard_dst[which],
                w_send.at[which],
                w_recv.at[which],
                dp=d_peer(step),
            ).start()
            return carry

        local(shard_src[which], shard_dst[which], w_own.at[which]).start()
        lax.fori_loop(1, nd, push, 0)

    all_but_one = pl.ds(0, (nd - 1) * shard_rows)
    whole = (wg, wa.at[:, 0], wm, wa.at[:, 1])

    def arrived_part(which):
        if which == 0:
            return wg.at[0, all_but_one]
        if which == 2:
            return wm.at[0, :, all_but_one]
        return wa.at[0, which // 2, :, all_but_one]

    def whole_part(which, section):
        if which == 0:
            return wg.at[section]
        if which == 2:
            return wm.at[section]
        return wa.at[section, which // 2]

    def weight_forward(which):
        wait_for(arrived_part(which), w_recv.at[which])
        local(shard_src[which], shard_dst[which], w_own.at[which]).wait()
        remote(
            whole_part(which, core),
            whole_part(which, core),
            wf_send.at[which],
            wf_recv.at[which],
            pipe=other,
        ).start()

    def weight_ready(which):
        wait_for(whole_part(which, 0), wf_recv.at[which])

    def misc_copies():
        return (
            remote(bnd.at[other], bx, m_send.at[0], m_recv.at[0], pipe=other),
            remote(rt_in.at[other], rt.at[core], m_send.at[1], m_recv.at[1], pipe=other),
        )

    def expert_copies():
        return (
            remote(ein, we.at[core, 0], m_send.at[2], m_recv.at[2], pipe=other),
            remote(eout, we.at[core, 1], m_send.at[3], m_recv.at[3], pipe=other),
        )

    def expert_own():
        return (
            local(ein, we.at[core, 0], m_own.at[0]),
            local(eout, we.at[core, 1], m_own.at[1]),
        )

    for copy in misc_copies():
        copy.start()
    share_weight(0)

    @pl.when(core == 0)
    def first_section():
        for which in range(1, 4):
            share_weight(which)

    rt[core] = rt_in[core]
    row_id = lax.broadcasted_iota(jnp.int32, (nd * 16, nd * extras), 0)
    col_id = lax.broadcasted_iota(jnp.int32, (nd * 16, nd * extras), 1)
    for q in range(quarters):
        hit = (
            ((row_id >> 4) == (col_id >> 2))
            & (((row_id >> 2) & 3) == q)
            & ((row_id & 3) == (col_id & 3))
        )
        sel[q] = jnp.where(hit, 1.0, 0.0).astype(BF16)
    dgn[...] = jnp.zeros_like(dgn)

    for copy in misc_copies():
        copy.wait()
    place = lax.broadcasted_iota(jnp.int32, (slots, tokens), 0)
    for s in range(2):
        table = rt[s]
        for k in range(2):
            hit = place == table[k : k + 1].astype(jnp.int32)
            pk[s, k] = jnp.where(hit, 1.0, 0.0).astype(BF16)
        gt[s] = jnp.transpose(jnp.concatenate([table] * (tokens // 8), axis=0))

    @pl.when(core == 0)
    def first_input():
        ags[0, 0, 0] = bnd[0].reshape(nx, rows, features)
        ags[1, 1, 3] = bx[...].reshape(nx, rows, features)

    @pl.when(core == 1)
    def second_input():
        ags[0, 0, 0] = bx[...].reshape(nx, rows, features)
        ags[1, 1, 3] = bnd[1].reshape(nx, rows, features)

    cur[...] = ags[0, 0, 0, mx].astype(F32)
    weight_forward(0)
    weight_ready(0)
    for s in range(2):
        turned = jnp.transpose(wg[s].astype(F32))
        gn[s] = turned[:8]

    lane = lax.broadcasted_iota(jnp.int32, (1, wide_features), 1)
    head_masks = [
        jnp.where((lane >= h * HEAD_DIM) & (lane < (h + 1) * HEAD_DIM), 1.0, 0.0).astype(BF16)
        for h in range(heads)
    ]

    def per_head(values):
        return [values * mask for mask in head_masks]

    def norm_parts(stream):
        center = stream - jnp.mean(stream, axis=-1, keepdims=True)
        scale = lax.rsqrt(jnp.mean(center * center, axis=-1, keepdims=True) + EPSILON)
        return center * scale, scale

    def norm_back(s, k, grad_normed):
        normal, scale = norm_parts(hs[s, k])
        dgn[s, k : k + 1, :] = jnp.sum(grad_normed * normal, axis=0, keepdims=True)
        pulled = grad_normed * gn[s][k : k + 1]
        return scale * (
            pulled
            - jnp.mean(pulled, axis=-1, keepdims=True)
            - normal * jnp.mean(pulled * normal, axis=-1, keepdims=True)
        )

    some = pl.ds(0, nx - 1)

    def all_rows(s, way, k, own_rows):
        ags[s, way, k, mx] = own_rows.astype(BF16)
        for step in range(1, nx):
            remote(
                ags.at[s, way, k, mx],
                ags.at[s, way, k, mx],
                ag_send.at[0],
                ag_recv.at[s, way, k],
                tensor=x_peer(step),
            ).start()
        wait_for(ags.at[s, way, k, some], ag_recv.at[s, way, k])
        wait_for(ags.at[s, way, k, some], ag_send.at[0])
        return ags[s, way, k].reshape(tokens, features)

    def sum_start(s, way, k, partial_rows):
        rs_out[...] = partial_rows.astype(BF16).reshape(nx, rows, features)
        for step in range(1, nx):
            peer = x_peer(step)
            remote(
                rs_out.at[peer],
                rs_in.at[s, way, k, mx],
                rs_send.at[0],
                rs_recv.at[s, way, k],
                tensor=peer,
            ).start()

    def sum_end(s, way, k):
        wait_for(rs_in.at[s, way, k, some], rs_recv.at[s, way, k])
        wait_for(rs_out.at[some], rs_send.at[0])
        total = rs_out[mx].astype(F32)
        for step in range(1, nx):
            total = total + rs_in[s, way, k, x_peer(step)].astype(F32)
        return total

    def slots_start(s, which, values):
        main = values[: nd * MAIN]
        extra = values[nd * MAIN :]
        folded = None
        for q in range(quarters):
            columns = slice(256 * q, 256 * (q + 1))
            a2_out[:, 16 * q : 16 * (q + 1), :] = main[:, columns].reshape(nd, 16, 256)
            term = nn(sel[q], extra[:, columns])
            folded = term if folded is None else folded + term
        a2_out[:, 16 * quarters :, :] = folded.astype(BF16).reshape(nd, 16, 256)

        def push(step, carry):
            peer = d_peer(step)
            remote(
                a2_out.at[peer],
                a2_in.at[s, which, md],
                a2_send.at[0],
                a2_recv.at[s, which],
                dp=peer,
            ).start()
            return carry

        lax.fori_loop(1, nd, push, 0)
        a2_in[s, which, md] = a2_out[md]

    def slots_end(s, which):
        wait_for(a2_in.at[s, which, pl.ds(0, nd - 1)], a2_recv.at[s, which])
        mains = []
        extra = []
        folded = a2_in[s, which, :, 16 * quarters :, :].reshape(nd * 16, 256)
        for q in range(quarters):
            block = a2_in[s, which, :, 16 * q : 16 * (q + 1), :]
            mains.append(block.reshape(nd * 16, 256))
            extra.append(tn(sel[q], folded).astype(BF16))
        return jnp.concatenate(
            [jnp.concatenate(mains, axis=1), jnp.concatenate(extra, axis=1)], axis=0
        )

    def slots_sent():
        wait_for(a2_out.at[pl.ds(0, nd - 1)], a2_send.at[0])

    def dback_start(s, grad_rows):
        wide = grad_rows.astype(F32)
        gates = gt[s]
        dback = nn(pk[s, 0], (wide * gates[:, 2:3]).astype(BF16)) + nn(
            pk[s, 1], (wide * gates[:, 3:4]).astype(BF16)
        )
        slots_start(s, 2, dback.astype(BF16))

    def attend(s, j, k):
        stream = cur[...]
        hs[s, k] = stream
        normal, unused = norm_parts(stream)
        if j == 0:

            @pl.when(s != 0)
            def fetch():
                all_rows(s, 0, k, normal * gn[s][k : k + 1])

            normed = ags[s, 0, k].reshape(tokens, features)
        else:
            normed = all_rows(s, 0, k, normal * gn[s][k : k + 1])

        @pl.when(core != s)
        def weights():
            weight_ready(1 + 2 * j)

        query, key, value = [nn(normed, wa[s, j, c]).astype(BF16) for c in range(3)]
        proj[s, j, 0] = query
        proj[s, j, 1] = key
        proj[s, j, 2] = value
        logits = nt(jnp.concatenate(per_head(query), axis=0), key) * (HEAD_DIM**-0.5)
        exponent = jnp.exp(logits - jnp.max(logits, axis=-1, keepdims=True))
        probs = exponent / jnp.sum(exponent, axis=-1, keepdims=True)
        prb[s, j] = probs
        low = probs.astype(BF16)
        mixed = None
        for h, part in enumerate(per_head(value)):
            term = nn(low[h * tokens : (h + 1) * tokens], part)
            mixed = term if mixed is None else mixed + term
        mixed = mixed.astype(BF16)
        mix[s, j] = mixed
        sum_start(s, 0, k, nt(mixed, wa[s, j, 3]))

        if j == 0:

            @pl.when((s == 0) & (core == 0))
            def onward():
                weight_forward(2)

        else:

            @pl.when((s == 0) & (core == 1))
            def share():
                share_weight(3)

            @pl.when(s == 1)
            def early_end():
                slots_sent()

        cur[...] = stream + sum_end(s, 0, k)

    def feed(s):
        stream = cur[...]
        hs[s, 1] = stream
        normal, unused = norm_parts(stream)
        normed = all_rows(s, 0, 1, normal * gn[s][1:2])

        @pl.when(core != s)
        def weights():
            weight_ready(2)

        active, slope = gelu_both(nn(normed, wm[s, 0]))
        active = active.astype(BF16)
        dgm[s] = slope
        act[s] = active
        sum_start(s, 0, 1, nt(active, wm[s, 1]))

        @pl.when((s == 0) & (core == 0))
        def onward():
            weight_forward(3)

        @pl.when((s == 0) & (core == 1))
        def share():
            share_weight(1)
            share_weight(2)

        @pl.when(s == 1)
        def early():
            dback_start(s, ags[1, 1, 3].reshape(tokens, features))

        cur[...] = stream + sum_end(s, 0, 1)

    def experts(s):
        stream = cur[...]
        hs[s, 3] = stream
        normal, unused = norm_parts(stream)
        normed = all_rows(s, 0, 3, normal * gn[s][3:4])
        slots_start(s, 0, nn(pk[s, 0] + pk[s, 1], normed).astype(BF16))

        @pl.when(s == 0)
        def weights():
            for copy in expert_copies() + expert_own():
                copy.wait()

        sent = slots_end(s, 0)
        slots_sent()
        arr[s] = sent
        active, slope = gelu_both(nn(sent, we[s, 0]))
        active = active.astype(BF16)
        ace[s] = active
        dge[s] = slope
        slots_start(s, 1, nn(active, we[s, 1]).astype(BF16))

    def experts_start(s):
        back = slots_end(s, 1)
        gates = gt[s]
        partial_rows = tn(pk[s, 0], back) * gates[:, 2:3] + tn(pk[s, 1], back) * gates[:, 3:4]
        sum_start(s, 0, 3, partial_rows)

    def experts_end(s):
        return hs[s, 3] + sum_end(s, 0, 3)

    def forward(s, carry):
        cur[...] = cur[...].astype(BF16).astype(F32)
        attend(s, 0, 0)
        feed(s)
        attend(s, 1, 2)
        experts(s)

        @pl.when(s == 0)
        def to_the_next():
            @pl.when(core == 1)
            def onward():
                for which in range(1, 4):
                    weight_forward(which)

            experts_start(s)
            slots_sent()
            cur[...] = experts_end(s)

        return carry

    def result_copies(buffer, target, start):
        slot = core * nx + mx

        @pl.when(core == target)
        def near():
            copy = local(buffer, res.at[slot], res_own.at[0])
            copy.start() if start else copy.wait()

        @pl.when(core != target)
        def far():
            copy = remote(
                buffer,
                res.at[slot],
                res_send.at[1],
                res_recv.at[0],
                pipe=target,
            )
            copy.start() if start else copy.wait_send()

        for step in range(1, nx):
            copy = remote(
                buffer,
                res.at[slot],
                res_send.at[1 + step],
                res_recv.at[0],
                pipe=target,
                tensor=x_peer(step),
            )
            copy.start() if start else copy.wait_send()

    @pl.when(core == 0)
    def first_weights():
        weight_forward(1)

    for copy in expert_copies() + expert_own():
        copy.start()
    given = ags[0, 0, 0].reshape(tokens, features).astype(F32)
    normal, unused = norm_parts(given)
    ags[0, 0, 0] = (normal * gn[0][0:1]).astype(BF16).reshape(nx, rows, features)
    lax.fori_loop(0, 2, forward, 0)

    staged = (ga.at[0], gm, ga.at[1])
    partner = (pa.at[0], pm, pa.at[1])
    landing = (ra.at[0], rm, ra.at[1])

    def chunk(which, owner):
        return staged[which].at[:, pl.ds(owner * shard_rows, shard_rows)]

    def staged_wait(which, section):
        @pl.when(core == section)
        def owned():
            wait_for(staged[which].at[:, all_but_one], ch_send.at[which])
            local(chunk(which, md), landing[which].at[md], ch_own.at[which]).wait()

        @pl.when(core != section)
        def lent():
            wait_for(staged[which], pg_send.at[which])

    def lend(which, section):
        @pl.when(core != section)
        def lent():
            remote(
                staged[which],
                partner[which],
                pg_send.at[which],
                pg_recv.at[which],
                pipe=other,
            ).start()

    def combine(which, section):
        @pl.when(core == section)
        def owned():
            wait_for(partner[which], pg_recv.at[which])
            for c in range(staged[which].shape[0]):
                staged[which][c] = (
                    staged[which][c].astype(F32) + partner[which][c].astype(F32)
                ).astype(BF16)

            def push(step, carry):
                peer = d_peer(step)
                remote(
                    chunk(which, peer),
                    landing[which].at[md],
                    ch_send.at[which],
                    ch_recv.at[which],
                    dp=peer,
                ).start()
                return carry

            lax.fori_loop(1, nd, push, 0)
            local(chunk(which, md), landing[which].at[md], ch_own.at[which]).start()

    def experts_back(s):
        grad = cur[...]

        @pl.when(s == 0)
        def later():
            dback_start(s, all_rows(s, 1, 3, grad))
            combine(0, 1)

        dback = slots_end(s, 2)
        dpre = (nt(dback, we[s, 1]) * dge[s]).astype(BF16)
        dsent = nt(dpre, we[s, 0]).astype(BF16)
        slots_sent()
        slots_start(s, 3, dsent)

        @pl.when(s == 1)
        def last_result_start():
            experts_start(s)

        eg[0] = tn(arr[s], dpre)
        eg[1] = tn(ace[s], dback)

        @pl.when(core == s)
        def keep():
            local(eg, eo, e_own.at[0]).start()

        @pl.when(core != s)
        def give():
            remote(eg, ep, e_send.at[0], e_recv.at[0], pipe=other).start()

        @pl.when(s == 1)
        def last_result_end():
            hout[...] = experts_end(s)
            result_copies(hout, 1, True)

        dsent = slots_end(s, 3)
        slots_sent()
        sum_start(s, 1, 3, tn(pk[s, 0] + pk[s, 1], dsent))
        cur[...] = grad + norm_back(s, 3, sum_end(s, 1, 3))

    def attend_back(s, j, k):
        grad = cur[...]
        dz = all_rows(s, 1, k, grad)
        dmixed = nn(dz, wa[s, j, 3]).astype(BF16)
        query, key, value = [proj[s, j, c] for c in range(3)]
        probs = prb[s, j]
        dmixed_heads = jnp.concatenate(per_head(dmixed), axis=0)
        dprobs = nt(dmixed_heads, value)
        dscores = probs * (dprobs - jnp.sum(probs * dprobs, axis=-1, keepdims=True))
        dscores = dscores.astype(BF16)
        dvalue = tn(probs.astype(BF16), dmixed_heads)
        dkey = tn(dscores, jnp.concatenate(per_head(query), axis=0)) * (HEAD_DIM**-0.5)
        dquery = None
        for h, part in enumerate(per_head(key)):
            term = nn(dscores[h * tokens : (h + 1) * tokens], part)
            dquery = term if dquery is None else dquery + term
        dquery = dquery * (HEAD_DIM**-0.5)
        dproj = [d.astype(BF16) for d in (dquery, dkey, dvalue)]
        partial_rows = None
        for c in range(3):
            term = nt(dproj[c], wa[s, j, c])
            partial_rows = term if partial_rows is None else partial_rows + term
        sum_start(s, 1, k, partial_rows)

        @pl.when(s == 0)
        def free():
            staged_wait(2 * j, 1)

        normed = ags[s, 0, k].reshape(tokens, features)
        for c in range(3):
            ga[j, c] = tn(normed, dproj[c]).astype(BF16)
        ga[j, 3] = tn(dz, mix[s, j]).astype(BF16)
        lend(2 * j, s)
        if j == 0:
            combine(1, s)
        cur[...] = grad + norm_back(s, k, sum_end(s, 1, k))

    def feed_back(s):
        grad = cur[...]
        dout = all_rows(s, 1, 1, grad)
        dpre = (nn(dout, wm[s, 1]) * dgm[s]).astype(BF16)
        sum_start(s, 1, 1, nt(dpre, wm[s, 0]))

        @pl.when(s == 0)
        def free():
            staged_wait(1, 1)

        normed = ags[s, 0, 1].reshape(tokens, features)
        gm[0] = tn(normed, dpre).astype(BF16)
        gm[1] = tn(dout, act[s]).astype(BF16)
        lend(1, s)
        combine(2, s)
        cur[...] = grad + norm_back(s, 1, sum_end(s, 1, 1))

    def expert_grads_wait(s):
        @pl.when(core == s)
        def keep():
            local(eg, eo, e_own.at[0]).wait()

        @pl.when(core != s)
        def give():
            wait_for(eg, e_send.at[0])

    def backward(turn, carry):
        s = 1 - turn
        cur[...] = cur[...].astype(BF16).astype(F32)
        experts_back(s)
        attend_back(s, 1, 2)
        feed_back(s)
        attend_back(s, 0, 0)
        expert_grads_wait(s)
        return carry

    cur[...] = ags[1, 1, 3, mx].astype(F32)
    lax.fori_loop(0, 2, backward, 0)
    gout[...] = cur[...]
    result_copies(hout, 1, False)
    result_copies(gout, 0, True)

    place_here = core * nx + mx
    for section in range(2):

        @pl.when(core == section)
        def near():
            gx[place_here] = dgn[section]

        @pl.when(core != section)
        def far():
            remote(
                dgn.at[section],
                gx.at[place_here],
                gx_send.at[section, 0],
                gx_recv.at[0],
                pipe=section,
            ).start()

        for step in range(1, nx):
            remote(
                dgn.at[section],
                gx.at[place_here],
                gx_send.at[section, step],
                gx_recv.at[0],
                pipe=section,
                tensor=x_peer(step),
            ).start()
    combine(0, 0)
    wait_for(gx.at[pl.ds(0, 2 * nx - 1)], gx_recv.at[0])
    gains_total = gx[0]
    for source in range(1, 2 * nx):
        gains_total = gains_total + gx[source]
    gs[...] = gains_total

    def push_gains(step, carry):
        remote(gs, rg.at[md], rg_send.at[0], rg_recv.at[0], dp=d_peer(step)).start()
        return carry

    lax.fori_loop(1, nd, push_gains, 0)
    local(gs, rg.at[md], rg_own.at[0]).start()

    for section in range(2):

        @pl.when(core != section)
        def far_end():
            wait_for(dgn.at[section], gx_send.at[section, 0])

        for step in range(1, nx):
            wait_for(dgn.at[section], gx_send.at[section, step])
    for which in range(4):
        wait_for(whole_part(which, 0), wf_send.at[which])
        wait_for(arrived_part(which), w_send.at[which])
    result_copies(gout, 0, False)
    wait_for(res.at[pl.ds(0, 2 * nx - 1)], res_recv.at[0])
    for which in range(3):
        staged_wait(which, 0)
        wait_for(landing[which].at[pl.ds(0, nd - 1)], ch_recv.at[which])
    wait_for(ep, e_recv.at[0])
    wait_for(rg.at[pl.ds(0, nd - 1)], rg_recv.at[0])
    wait_for(rg.at[pl.ds(0, nd - 1)], rg_send.at[0])
    local(gs, rg.at[md], rg_own.at[0]).wait()


def shards(
    nx,
    nd,
    boundary,
    norm_gains,
    attn_qkv,
    attn_out,
    mlp_in,
    mlp_out,
    expert_in,
    expert_out,
    expert_ids,
    expert_slots,
    gate_weights,
):
    tokens, features = boundary.shape[3:]
    rows = tokens // nx
    shard_rows = features // nd
    wide = attn_qkv.shape[4]
    units = mlp_in.shape[2]
    hidden = expert_in.shape[3]
    slots = nd * CAP
    quarters = features // 256
    slab = 16 * quarters + 16
    heads = wide // HEAD_DIM

    slot = expert_slots[0, :, 0]
    owner = expert_ids[0, :, 0]
    place = jnp.where(
        slot < MAIN,
        owner * MAIN + slot,
        nd * MAIN + owner * (CAP - MAIN) + slot - MAIN,
    )
    table = jnp.concatenate(
        [
            jnp.swapaxes(place, 1, 2).astype(F32),
            jnp.swapaxes(gate_weights[0, :, 0], 1, 2),
            jnp.zeros((MICRO, 4, tokens), F32),
        ],
        axis=1,
    )
    sa = jnp.concatenate([attn_qkv[0], jnp.swapaxes(attn_out[0], 1, 2)[:, None]], axis=1)
    sm = jnp.stack([mlp_in[0], mlp_out[0].T])
    sg = jnp.pad(norm_gains[0].T, ((0, 0), (0, 128 - norm_gains.shape[1])))

    vmem = pl.BlockSpec(memory_space=pltpu.VMEM)
    hbm = pl.BlockSpec(memory_space=pl.ANY)
    dma = pltpu.SemaphoreType.DMA
    scratch = [
        pltpu.VMEM((2, 2, 4, features, wide), BF16),
        pltpu.VMEM((2, 2, features, units), BF16),
        pltpu.VMEM((2, 2, features, hidden), BF16),
        pltpu.VMEM((2, features, 128), BF16),
        pltpu.VMEM((2, 8, features), F32),
        pltpu.VMEM((2, 8, tokens), F32),
        pltpu.VMEM((2, tokens, tokens), F32),
        pltpu.VMEM((tokens, features), BF16),
        pltpu.VMEM((quarters, nd * 16, nd * (CAP - MAIN)), BF16),
        pltpu.VMEM((2, 2, slots, tokens), BF16),
        pltpu.VMEM((2, 4, rows, features), F32),
        pltpu.VMEM((2, 2, 4, nx, rows, features), BF16),
        pltpu.VMEM((nx, rows, features), BF16),
        pltpu.VMEM((2, 2, 4, nx, rows, features), BF16),
        pltpu.VMEM((nd, slab, 256), BF16),
        pltpu.VMEM((2, 4, nd, slab, 256), BF16),
        pltpu.VMEM((2, 2, 3, tokens, wide), BF16),
        pltpu.VMEM((2, 2, tokens, wide), BF16),
        pltpu.VMEM((2, 2, heads * tokens, tokens), F32),
        pltpu.VMEM((2, tokens, units), F32),
        pltpu.VMEM((2, tokens, units), BF16),
        pltpu.VMEM((2, slots, features), BF16),
        pltpu.VMEM((2, slots, hidden), F32),
        pltpu.VMEM((2, slots, hidden), BF16),
        pltpu.VMEM((2, 4, features, wide), BF16),
        pltpu.VMEM((2, features, units), BF16),
        pltpu.VMEM((2, 4, features, wide), BF16),
        pltpu.VMEM((2, features, units), BF16),
        pltpu.VMEM((2, features, hidden), F32),
        pltpu.VMEM((2, 8, features), F32),
        pltpu.VMEM((2 * nx, 8, features), F32),
        pltpu.VMEM((8, features), F32),
        pltpu.VMEM((rows, features), F32),
        pltpu.VMEM((rows, features), F32),
        pltpu.VMEM((rows, features), F32),
        dma((1,)),
        dma((2, 2, 4)),
        dma((1,)),
        dma((2, 2, 4)),
        dma((1,)),
        dma((2, 4)),
        dma((4,)),
        dma((4,)),
        dma((4,)),
        dma((4,)),
        dma((4,)),
        dma((4,)),
        dma((4,)),
        dma((2,)),
        dma((3,)),
        dma((3,)),
        dma((3,)),
        dma((3,)),
        dma((3,)),
        dma((1,)),
        dma((1,)),
        dma((1,)),
        dma((1 + nx,)),
        dma((1,)),
        dma((1,)),
        dma((2, nx)),
        dma((1,)),
        dma((1,)),
        dma((1,)),
        dma((1,)),
    ]
    res, ra, rm, rg, eo, ep = pl.pallas_call(
        functools.partial(kernel, nx, nd),
        out_shape=(
            jax.ShapeDtypeStruct((2 * nx, rows, features), F32),
            jax.ShapeDtypeStruct((2, nd, 4, shard_rows, wide), BF16),
            jax.ShapeDtypeStruct((nd, 2, shard_rows, units), BF16),
            jax.ShapeDtypeStruct((nd, 8, features), F32),
            jax.ShapeDtypeStruct((2, features, hidden), F32),
            jax.ShapeDtypeStruct((2, features, hidden), F32),
        ),
        in_specs=[vmem, vmem, hbm, hbm, hbm, hbm, hbm],
        out_specs=(hbm,) * 6,
        scratch_shapes=scratch,
        compiler_params=pltpu.CompilerParams(
            collective_id=0, has_side_effects=True, vmem_limit_bytes=VMEM_LIMIT
        ),
    )(boundary[0, :, 0], table, sa, sm, sg, expert_in[0, 0], expert_out[0, 0])

    dense = jnp.sum(ra.astype(F32), axis=1)
    feed = jnp.sum(rm.astype(F32), axis=0)
    gains = jnp.sum(rg, axis=0)[: norm_gains.shape[1]]
    gains = lax.dynamic_slice_in_dim(gains, lax.axis_index("dp") * shard_rows, shard_rows, 1)
    expert = eo + ep
    return (
        res.reshape(1, MICRO, 1, tokens, features),
        gains[None],
        dense[None, :, :3],
        jnp.swapaxes(dense[:, 3], 1, 2)[None],
        feed[0][None],
        feed[1].T[None],
        expert[0][None, None],
        expert[1][None, None],
    )


VMEM_LIMIT = 62 * 1024 * 1024


def solution(mesh):
    in_specs = (
        P("pipe", None, "dp", None, None),
        P("pipe", None, "dp"),
        P("pipe", None, None, "dp", "tensor"),
        P("pipe", None, "tensor", "dp"),
        P("pipe", "dp", "tensor"),
        P("pipe", "tensor", "dp"),
        P("pipe", "dp", None, "tensor"),
        P("pipe", "dp", "tensor", None),
        P("pipe", None, "dp", None, None),
        P("pipe", None, "dp", None, None),
        P("pipe", None, "dp", None, None),
    )
    out_specs = (
        P("pipe", None, "dp", None, None),
        P("pipe", None, "dp"),
        P("pipe", None, None, "dp", "tensor"),
        P("pipe", None, "tensor", "dp"),
        P("pipe", "dp", "tensor"),
        P("pipe", "tensor", "dp"),
        P("pipe", "dp", None, "tensor"),
        P("pipe", "dp", "tensor", None),
    )
    return jax.shard_map(
        functools.partial(shards, mesh.shape["tensor"], mesh.shape["dp"]),
        mesh=mesh,
        in_specs=in_specs,
        out_specs=out_specs,
        check_vma=False,
    )
```

```python
import functools

import jax
import jax.numpy as jnp
from jax import lax
from jax.experimental import pallas as pl
from jax.experimental.pallas import tpu as pltpu
from jax.sharding import PartitionSpec as P

MESH = pl.DeviceIdType.MESH
BF16 = jnp.bfloat16
F32 = jnp.float32
HEAD_DIM = 64
EPSILON = 1e-06
CAP = 20
MAIN = 16
MICRO = 2


def dims(lhs, rhs, left_dim, right_dim):
    return lax.dot_general(
        lhs, rhs, (((left_dim,), (right_dim,)), ((), ())), preferred_element_type=F32
    )


def nn(lhs, rhs):
    return dims(lhs, rhs, 1, 0)


def nt(lhs, rhs):
    return dims(lhs, rhs, 1, 1)


def tn(lhs, rhs):
    return dims(lhs, rhs, 0, 0)


def gelu_both(pre):
    phi = 0.5 * (1.0 + lax.erf(pre * 0.7071067811865476))
    density = 0.3989422804014327 * jnp.exp(-0.5 * pre * pre)
    return pre * phi, phi + pre * density


def kernel(
    nx,
    nd,
    bnd,
    ids,
    seat,
    gate,
    sq,
    so,
    mi,
    mo,
    gains,
    ein,
    eout,
    res,
    dense_sum,
    feed_sum,
    gains_sum,
    ei_own,
    eo_own,
    ei_far,
    eo_far,
    ra,
    rm,
    rg,
    rt_in,
    sg,
    sa,
    sm,
    put,
    xh,
    wa,
    wm,
    we,
    wg,
    gn,
    rt,
    gt,
    bx,
    sel,
    pk,
    hs,
    ags,
    rs_out,
    rs_in,
    a2_out,
    a2_in,
    proj,
    mix,
    prb,
    dgm,
    act,
    arr,
    dge,
    ace,
    ga,
    gm,
    pa,
    pm,
    eg,
    dgn,
    gx,
    gs,
    cur,
    hout,
    gout,
    ag_send,
    ag_recv,
    rs_send,
    rs_recv,
    a2_send,
    a2_recv,
    w_send,
    w_recv,
    w_own,
    wf_send,
    wf_recv,
    m_send,
    m_recv,
    m_own,
    pg_send,
    pg_recv,
    ch_send,
    ch_recv,
    ch_own,
    e_send,
    e_recv,
    e_own,
    res_send,
    res_recv,
    res_own,
    gx_send,
    gx_recv,
    rg_send,
    rg_recv,
    rg_own,
):
    core = lax.axis_index("pipe")
    md = lax.axis_index("dp")
    mx = lax.axis_index("tensor")
    other = 1 - core
    rows, features = cur.shape
    tokens = nx * rows
    shard_rows = sa.shape[1]
    wide_features = sq.shape[3]
    heads = wide_features // HEAD_DIM
    quarters = features // 256
    slots = nd * CAP
    extras = CAP - MAIN

    def x_peer(step):
        return lax.rem(mx + step, nx)

    def d_peer(step):
        return lax.rem(md + step, nd)

    def far_first(step):
        turned = step + nd // 2 - 1
        return jnp.where(turned >= nd, turned - nd + 1, turned)

    def remote(src, dst, send, recv, **where):
        return pltpu.make_async_remote_copy(
            src_ref=src,
            dst_ref=dst,
            send_sem=send,
            recv_sem=recv,
            device_id=where,
            device_id_type=MESH,
        )

    def local(src, dst, sem):
        return pltpu.make_async_copy(src, dst, sem)

    def wait_for(ref, sem):
        pltpu.make_async_copy(ref, ref, sem).wait()

    mine = pl.ds(md * shard_rows, shard_rows)
    shard_src = (sg, sa.at[0], sm, sa.at[1])
    shard_dst = (
        wg.at[core, mine],
        wa.at[core, 0, mine],
        wm.at[core, :, mine],
        wa.at[core, 1, mine],
    )

    def share_weight(which):
        def push(step, carry):
            remote(
                shard_src[which],
                shard_dst[which],
                w_send.at[which],
                w_recv.at[which],
                dp=d_peer(step),
            ).start()
            return carry

        local(shard_src[which], shard_dst[which], w_own.at[which]).start()
        lax.fori_loop(1, nd, push, 0)

    all_but_one = pl.ds(0, (nd - 1) * shard_rows)

    def arrived_part(which):
        if which == 0:
            return wg.at[0, all_but_one]
        if which == 2:
            return wm.at[0, :, all_but_one]
        return wa.at[0, which // 2, all_but_one]

    def whole_part(which, section):
        if which == 0:
            return wg.at[section]
        if which == 2:
            return wm.at[section]
        return wa.at[section, which // 2]

    def weight_forward(which):
        wait_for(arrived_part(which), w_recv.at[which])
        local(shard_src[which], shard_dst[which], w_own.at[which]).wait()
        remote(
            whole_part(which, core),
            whole_part(which, core),
            wf_send.at[which],
            wf_recv.at[which],
            pipe=other,
        ).start()

    def weight_ready(which):
        wait_for(whole_part(which, 0), wf_recv.at[which])

    def misc_copies():
        return (
            remote(bnd.at[other], bx, m_send.at[0], m_recv.at[0], pipe=other),
            remote(rt_in.at[other], rt.at[core], m_send.at[1], m_recv.at[1], pipe=other),
        )

    def expert_copies():
        return (
            remote(ein, we.at[core, 0], m_send.at[2], m_recv.at[2], pipe=other),
            remote(eout, we.at[core, 1], m_send.at[3], m_recv.at[3], pipe=other),
        )

    def expert_own():
        return (
            local(ein, we.at[core, 0], m_own.at[0]),
            local(eout, we.at[core, 1], m_own.at[1]),
        )

    put_row = lax.broadcasted_iota(jnp.int32, put.shape[1:], 0)
    put_col = lax.broadcasted_iota(jnp.int32, put.shape[1:], 1)
    for c in range(4):
        put[c] = jnp.where(put_col == put_row + c * wide_features, 1.0, 0.0).astype(BF16)

    def attention_shard(j):
        total = nn(so[j], put[0])
        for c in range(3):
            total = total + nn(sq[j, c], put[1 + c])
        sa[j] = total.astype(BF16)

    attention_shard(0)
    count = gains.shape[0]
    pick_row = lax.broadcasted_iota(jnp.int32, (count, 128), 0)
    pick_col = lax.broadcasted_iota(jnp.int32, (count, 128), 1)
    sg[...] = tn(gains[...], jnp.where(pick_row == pick_col, 1.0, 0.0).astype(BF16)).astype(BF16)
    for m in range(MICRO):
        expert = ids[m]
        seats = seat[m]
        place = jnp.where(
            seats < MAIN,
            expert * MAIN + seats,
            nd * MAIN + expert * extras + seats - MAIN,
        )
        rt_in[m] = jnp.concatenate(
            [place.astype(F32), gate[m], jnp.zeros((4, tokens), F32)], axis=0
        )

    barrier = pltpu.get_barrier_semaphore()

    def greet(step, carry):
        pl.semaphore_signal(
            barrier, inc=1, device_id={"dp": d_peer(step)}, device_id_type=MESH
        )
        return carry

    lax.fori_loop(1, nd, greet, 0)
    for step in range(1, nx):
        pl.semaphore_signal(
            barrier, inc=1, device_id={"tensor": x_peer(step)}, device_id_type=MESH
        )
    for step in range(nx):
        pl.semaphore_signal(
            barrier,
            inc=1,
            device_id={"pipe": other, "tensor": x_peer(step)},
            device_id_type=MESH,
        )
    pl.semaphore_wait(barrier, (nd - 1) + (nx - 1) + nx)

    @pl.when(core == 0)
    def first_attention():
        share_weight(1)

    for copy in misc_copies():
        copy.start()
    share_weight(0)
    sm[0] = mi[...]
    sm[1] = mo[...]
    attention_shard(1)

    @pl.when(core == 0)
    def first_section():
        share_weight(2)
        share_weight(3)

    rt[core] = rt_in[core]
    row_id = lax.broadcasted_iota(jnp.int32, (nd * 16, nd * extras), 0)
    col_id = lax.broadcasted_iota(jnp.int32, (nd * 16, nd * extras), 1)
    for q in range(quarters):
        hit = (
            ((row_id >> 4) == (col_id >> 2))
            & (((row_id >> 2) & 3) == q)
            & ((row_id & 3) == (col_id & 3))
        )
        sel[q] = jnp.where(hit, 1.0, 0.0).astype(BF16)
    dgn[...] = jnp.zeros_like(dgn)

    for copy in misc_copies():
        copy.wait()
    place = lax.broadcasted_iota(jnp.int32, (slots, tokens), 0)
    for s in range(2):
        table = rt[s]
        for k in range(2):
            hit = place == table[k : k + 1].astype(jnp.int32)
            pk[s, k] = jnp.where(hit, 1.0, 0.0).astype(BF16)
        gt[s] = jnp.transpose(jnp.concatenate([table] * (tokens // 8), axis=0))

    @pl.when(core == 0)
    def first_input():
        ags[0, 0, 0] = bnd[0].reshape(nx, rows, features)
        ags[1, 1, 3] = bx[...].reshape(nx, rows, features)

    @pl.when(core == 1)
    def second_input():
        ags[0, 0, 0] = bx[...].reshape(nx, rows, features)
        ags[1, 1, 3] = bnd[1].reshape(nx, rows, features)

    cur[...] = ags[0, 0, 0, mx].astype(F32)
    weight_forward(0)
    weight_ready(0)
    for s in range(2):
        turned = jnp.transpose(wg[s].astype(F32))
        gn[s] = turned[:8]

    lane = lax.broadcasted_iota(jnp.int32, (1, wide_features), 1)
    head_masks = [
        jnp.where((lane >= h * HEAD_DIM) & (lane < (h + 1) * HEAD_DIM), 1.0, 0.0).astype(BF16)
        for h in range(heads)
    ]

    def per_head(values):
        return [values * mask for mask in head_masks]

    def norm_parts(stream):
        center = stream - jnp.mean(stream, axis=-1, keepdims=True)
        scale = lax.rsqrt(jnp.mean(center * center, axis=-1, keepdims=True) + EPSILON)
        return center * scale, scale

    def norm_back(s, k, grad_normed):
        normal, scale = norm_parts(hs[s, k])
        gain_rows = jnp.sum(grad_normed * normal, axis=0, keepdims=True)
        if k == 0:

            @pl.when(s == 1)
            def not_sent_yet():
                dgn[s, k : k + 1, :] = gain_rows

        else:
            dgn[s, k : k + 1, :] = gain_rows
        pulled = grad_normed * gn[s][k : k + 1]
        return scale * (
            pulled
            - jnp.mean(pulled, axis=-1, keepdims=True)
            - normal * jnp.mean(pulled * normal, axis=-1, keepdims=True)
        )

    some = pl.ds(0, nx - 1)

    def all_rows(s, way, k, own_rows, meanwhile=None):
        ags[s, way, k, mx] = own_rows.astype(BF16)
        for step in range(1, nx):
            remote(
                ags.at[s, way, k, mx],
                ags.at[s, way, k, mx],
                ag_send.at[s, way, k],
                ag_recv.at[s, way, k],
                tensor=x_peer(step),
            ).start()
        if meanwhile is not None:
            meanwhile()
        wait_for(ags.at[s, way, k, some], ag_recv.at[s, way, k])
        return ags[s, way, k].reshape(tokens, features)

    def sum_start(s, way, k, partial_rows):
        rs_out[s, way, k] = partial_rows.astype(BF16).reshape(nx, rows, features)
        for step in range(1, nx):
            peer = x_peer(step)
            remote(
                rs_out.at[s, way, k, peer],
                rs_in.at[s, way, k, mx],
                rs_send.at[s, way, k],
                rs_recv.at[s, way, k],
                tensor=peer,
            ).start()

    def sum_end(s, way, k):
        wait_for(rs_in.at[s, way, k, some], rs_recv.at[s, way, k])
        total = rs_out[s, way, k, mx].astype(F32)
        for step in range(1, nx):
            total = total + rs_in[s, way, k, x_peer(step)].astype(F32)
        return total

    def slots_start(s, which, values):
        main = values[: nd * MAIN]
        extra = values[nd * MAIN :]
        folded = None
        for q in range(quarters):
            columns = slice(256 * q, 256 * (q + 1))
            a2_out[:, 16 * q : 16 * (q + 1), :] = main[:, columns].reshape(nd, 16, 256)
            term = nn(sel[q], extra[:, columns])
            folded = term if folded is None else folded + term
        a2_out[:, 16 * quarters :, :] = folded.astype(BF16).reshape(nd, 16, 256)

        def push(step, carry):
            peer = d_peer(far_first(step))
            remote(
                a2_out.at[peer],
                a2_in.at[s, which, md],
                a2_send.at[0],
                a2_recv.at[s, which],
                dp=peer,
            ).start()
            return carry

        lax.fori_loop(1, nd, push, 0)
        a2_in[s, which, md] = a2_out[md]

    def slots_end(s, which):
        wait_for(a2_in.at[s, which, pl.ds(0, nd - 1)], a2_recv.at[s, which])
        mains = []
        extra = []
        folded = a2_in[s, which, :, 16 * quarters :, :].reshape(nd * 16, 256)
        for q in range(quarters):
            block = a2_in[s, which, :, 16 * q : 16 * (q + 1), :]
            mains.append(block.reshape(nd * 16, 256))
            extra.append(tn(sel[q], folded).astype(BF16))
        return jnp.concatenate(
            [jnp.concatenate(mains, axis=1), jnp.concatenate(extra, axis=1)], axis=0
        )

    def slots_sent():
        wait_for(a2_out.at[pl.ds(0, nd - 1)], a2_send.at[0])

    def dback_start(s, grad_rows):
        wide = grad_rows.astype(F32)
        gates = gt[s]
        dback = nn(pk[s, 0], (wide * gates[:, 2:3]).astype(BF16)) + nn(
            pk[s, 1], (wide * gates[:, 3:4]).astype(BF16)
        )
        slots_start(s, 2, dback.astype(BF16))

    def attend(s, j, k):
        stream = cur[...]
        hs[s, k] = stream
        normal, unused = norm_parts(stream)
        if j == 0:

            @pl.when(s != 0)
            def fetch():
                all_rows(s, 0, k, normal * gn[s][k : k + 1])

            normed = ags[s, 0, k].reshape(tokens, features)
        else:
            normed = all_rows(s, 0, k, normal * gn[s][k : k + 1])

        @pl.when(core != s)
        def weights():
            weight_ready(1 + 2 * j)

        projected = nn(normed, wa[s, j])
        query, key, value = [
            projected[:, c * wide_features : (c + 1) * wide_features].astype(BF16)
            for c in range(1, 4)
        ]
        proj[s, j, 0] = query
        proj[s, j, 1] = key
        proj[s, j, 2] = value
        logits = nt(jnp.concatenate(per_head(query), axis=0), key) * (HEAD_DIM**-0.5)
        exponent = jnp.exp(logits - jnp.max(logits, axis=-1, keepdims=True))
        probs = exponent / jnp.sum(exponent, axis=-1, keepdims=True)
        prb[s, j] = probs
        low = probs.astype(BF16)
        mixed = None
        for h, part in enumerate(per_head(value)):
            term = nn(low[h * tokens : (h + 1) * tokens], part)
            mixed = term if mixed is None else mixed + term
        mixed = mixed.astype(BF16)
        mix[s, j] = mixed
        sum_start(s, 0, k, nt(mixed, wa[s, j, :, :wide_features]))

        if j == 1:

            @pl.when((s == 0) & (core == 1))
            def share():
                share_weight(3)

            @pl.when(s == 1)
            def early_end():
                slots_sent()

        cur[...] = stream + sum_end(s, 0, k)

    def feed(s):
        stream = cur[...]
        hs[s, 1] = stream
        normal, unused = norm_parts(stream)

        def meanwhile():
            @pl.when((s == 0) & (core == 0))
            def onward():
                weight_forward(2)

        normed = all_rows(s, 0, 1, normal * gn[s][1:2], meanwhile)

        @pl.when(core != s)
        def weights():
            weight_ready(2)

        active, slope = gelu_both(nn(normed, wm[s, 0]))
        active = active.astype(BF16)
        dgm[s] = slope
        act[s] = active
        sum_start(s, 0, 1, nt(active, wm[s, 1]))

        @pl.when((s == 0) & (core == 0))
        def onward():
            weight_forward(3)

        @pl.when((s == 0) & (core == 1))
        def share():
            share_weight(1)
            share_weight(2)

        @pl.when(s == 1)
        def early():
            slots_sent()
            dback_start(s, ags[1, 1, 3].reshape(tokens, features))

        cur[...] = stream + sum_end(s, 0, 1)

    def experts(s):
        stream = cur[...]
        hs[s, 3] = stream
        normal, unused = norm_parts(stream)
        normed = all_rows(s, 0, 3, normal * gn[s][3:4])
        slots_start(s, 0, nn(pk[s, 0] + pk[s, 1], normed).astype(BF16))

        @pl.when(s == 0)
        def weights():
            for copy in expert_copies() + expert_own():
                copy.wait()

        sent = slots_end(s, 0)
        arr[s] = sent
        active, slope = gelu_both(nn(sent, we[s, 0]))
        active = active.astype(BF16)
        ace[s] = active
        dge[s] = slope
        partial_rows = nn(active, we[s, 1]).astype(BF16)
        slots_sent()
        slots_start(s, 1, partial_rows)

    def experts_start(s):
        back = slots_end(s, 1)
        gates = gt[s]
        partial_rows = tn(pk[s, 0], back) * gates[:, 2:3] + tn(pk[s, 1], back) * gates[:, 3:4]
        sum_start(s, 0, 3, partial_rows)

    def experts_end(s):
        return hs[s, 3] + sum_end(s, 0, 3)

    def forward(s, carry):
        cur[...] = cur[...].astype(BF16).astype(F32)
        attend(s, 0, 0)
        feed(s)
        attend(s, 1, 2)
        experts(s)

        @pl.when(s == 0)
        def to_the_next():
            @pl.when(core == 1)
            def onward():
                for which in range(1, 4):
                    weight_forward(which)

            experts_start(s)
            cur[...] = experts_end(s)

        return carry

    def result_copies(buffer, target, start):
        slot = core * nx + mx

        @pl.when(core == target)
        def near():
            copy = local(buffer, res.at[slot], res_own.at[0])
            copy.start() if start else copy.wait()

        @pl.when(core != target)
        def far():
            copy = remote(
                buffer,
                res.at[slot],
                res_send.at[1],
                res_recv.at[0],
                pipe=target,
            )
            copy.start() if start else copy.wait_send()

        for step in range(1, nx):
            copy = remote(
                buffer,
                res.at[slot],
                res_send.at[1 + step],
                res_recv.at[0],
                pipe=target,
                tensor=x_peer(step),
            )
            copy.start() if start else copy.wait_send()

    @pl.when(core == 0)
    def first_weights():
        weight_forward(1)

    for copy in expert_copies() + expert_own():
        copy.start()
    given = ags[0, 0, 0].reshape(tokens, features).astype(F32)
    normal, unused = norm_parts(given)
    xh[...] = normal
    ags[0, 0, 0] = (normal * gn[0][0:1]).astype(BF16).reshape(nx, rows, features)
    lax.fori_loop(0, 2, forward, 0)

    staged = (ga.at[0], gm, ga.at[1])
    partner = (pa.at[0], pm, pa.at[1])
    landing = (ra.at[0], rm, ra.at[1])

    def some_rows(which, part):
        return staged[which].at[:, part] if which == 1 else staged[which].at[part]

    def chunk(which, owner):
        return some_rows(which, pl.ds(owner * shard_rows, shard_rows))

    def staged_wait(which, section):
        @pl.when(core == section)
        def owned():
            wait_for(some_rows(which, all_but_one), ch_send.at[which])
            local(chunk(which, md), landing[which].at[md], ch_own.at[which]).wait()

        @pl.when(core != section)
        def lent():
            wait_for(staged[which], pg_send.at[which])

    def lend(which, section):
        @pl.when(core != section)
        def lent():
            remote(
                staged[which],
                partner[which],
                pg_send.at[which],
                pg_recv.at[which],
                pipe=other,
            ).start()

    def combine(which, section):
        @pl.when(core == section)
        def owned():
            wait_for(partner[which], pg_recv.at[which])
            staged[which][...] = (
                staged[which][...].astype(F32) + partner[which][...].astype(F32)
            ).astype(BF16)

            def push(step, carry):
                peer = d_peer(step)
                remote(
                    chunk(which, peer),
                    landing[which].at[md],
                    ch_send.at[which],
                    ch_recv.at[which],
                    dp=peer,
                ).start()
                return carry

            lax.fori_loop(1, nd, push, 0)
            local(chunk(which, md), landing[which].at[md], ch_own.at[which]).start()

    def gains_start():
        place_here = core * nx + mx
        for section in range(2):

            @pl.when(core == section)
            def near():
                gx[place_here] = dgn[section]

            @pl.when(core != section)
            def far():
                remote(
                    dgn.at[section],
                    gx.at[place_here],
                    gx_send.at[section, 0],
                    gx_recv.at[0],
                    pipe=section,
                ).start()

            for step in range(1, nx):
                remote(
                    dgn.at[section],
                    gx.at[place_here],
                    gx_send.at[section, step],
                    gx_recv.at[0],
                    pipe=section,
                    tensor=x_peer(step),
                ).start()

    def gains_push():
        wait_for(gx.at[pl.ds(0, 2 * nx - 1)], gx_recv.at[0])
        gains_total = gx[0]
        for source in range(1, 2 * nx):
            gains_total = gains_total + gx[source]
        gs[...] = gains_total

        def push_gains(step, carry):
            remote(gs, rg.at[md], rg_send.at[0], rg_recv.at[0], dp=d_peer(step)).start()
            return carry

        lax.fori_loop(1, nd, push_gains, 0)
        local(gs, rg.at[md], rg_own.at[0]).start()

    def experts_back(s):
        grad = cur[...]

        @pl.when(s == 0)
        def later():
            wide = all_rows(s, 1, 3, grad, slots_sent)
            dback_start(s, wide)
            combine(0, 1)

        dback = slots_end(s, 2)
        dpre = (nt(dback, we[s, 1]) * dge[s]).astype(BF16)
        dsent = nt(dpre, we[s, 0]).astype(BF16)
        slots_sent()
        slots_start(s, 3, dsent)

        @pl.when(s == 1)
        def last_result_start():
            experts_start(s)

        eg[0] = tn(arr[s], dpre).astype(BF16)
        eg[1] = tn(ace[s], dback).astype(BF16)

        @pl.when(core == s)
        def keep():
            local(eg.at[0], ei_own, e_own.at[0]).start()
            local(eg.at[1], eo_own, e_own.at[1]).start()

        @pl.when(core != s)
        def give():
            remote(eg.at[0], ei_far, e_send.at[0], e_recv.at[0], pipe=other).start()
            remote(eg.at[1], eo_far, e_send.at[1], e_recv.at[1], pipe=other).start()

        @pl.when(s == 1)
        def last_result_end():
            hout[...] = experts_end(s)
            result_copies(hout, 1, True)

        dsent = slots_end(s, 3)
        sum_start(s, 1, 3, tn(pk[s, 0] + pk[s, 1], dsent))
        cur[...] = grad + norm_back(s, 3, sum_end(s, 1, 3))

    def attend_back(s, j, k):
        grad = cur[...]
        dz = all_rows(s, 1, k, grad, (lambda: combine(1, s)) if j == 0 else None)
        dmixed = nn(dz, wa[s, j, :, :wide_features]).astype(BF16)
        query, key, value = [proj[s, j, c] for c in range(3)]
        probs = prb[s, j]
        dmixed_heads = jnp.concatenate(per_head(dmixed), axis=0)
        dprobs = nt(dmixed_heads, value)
        dscores = probs * (dprobs - jnp.sum(probs * dprobs, axis=-1, keepdims=True))
        dscores = dscores.astype(BF16)
        dvalue = tn(probs.astype(BF16), dmixed_heads)
        dkey = tn(dscores, jnp.concatenate(per_head(query), axis=0)) * (HEAD_DIM**-0.5)
        dquery = None
        for h, part in enumerate(per_head(key)):
            term = nn(dscores[h * tokens : (h + 1) * tokens], part)
            dquery = term if dquery is None else dquery + term
        dquery = dquery * (HEAD_DIM**-0.5)
        dproj = [d.astype(BF16) for d in (dquery, dkey, dvalue)]
        placed = None
        for c in range(3):
            term = nn(dproj[c], put[1 + c])
            placed = term if placed is None else placed + term
        placed = placed.astype(BF16)
        partial_rows = nt(placed, wa[s, j])
        sum_start(s, 1, k, partial_rows)
        if j == 0:

            @pl.when(s == 0)
            def last_gain():
                dgn[0, 0:1, :] = jnp.sum(partial_rows * xh[...], axis=0, keepdims=True)
                gains_start()

        @pl.when(s == 0)
        def free():
            staged_wait(2 * j, 1)

        normed = ags[s, 0, k].reshape(tokens, features)
        mixed = nn(mix[s, j], put[0]).astype(BF16)
        ga[j] = tn(
            jnp.concatenate([normed, dz], axis=0), jnp.concatenate([placed, mixed], axis=0)
        ).astype(BF16)
        lend(2 * j, s)
        if j == 0:

            @pl.when(s == 0)
            def gains_on():
                gains_push()

        cur[...] = grad + norm_back(s, k, sum_end(s, 1, k))

    def feed_back(s):
        grad = cur[...]
        dout = all_rows(s, 1, 1, grad, lambda: combine(2, s))
        dpre = (nn(dout, wm[s, 1]) * dgm[s]).astype(BF16)
        sum_start(s, 1, 1, nt(dpre, wm[s, 0]))

        @pl.when(s == 0)
        def free():
            staged_wait(1, 1)

        normed = ags[s, 0, 1].reshape(tokens, features)
        gm[0] = tn(normed, dpre).astype(BF16)
        gm[1] = tn(dout, act[s]).astype(BF16)
        lend(1, s)
        cur[...] = grad + norm_back(s, 1, sum_end(s, 1, 1))

    def expert_grads_wait(s):
        @pl.when(core == s)
        def keep():
            local(eg.at[0], ei_own, e_own.at[0]).wait()
            local(eg.at[1], eo_own, e_own.at[1]).wait()

        @pl.when(core != s)
        def give():
            wait_for(eg.at[0], e_send.at[0])
            wait_for(eg.at[1], e_send.at[1])

    def backward(turn, carry):
        s = 1 - turn
        cur[...] = cur[...].astype(BF16).astype(F32)
        experts_back(s)
        attend_back(s, 1, 2)
        feed_back(s)
        attend_back(s, 0, 0)
        expert_grads_wait(s)
        return carry

    cur[...] = ags[1, 1, 3, mx].astype(F32)
    lax.fori_loop(0, 2, backward, 0)
    gout[...] = cur[...]
    result_copies(hout, 1, False)
    result_copies(gout, 0, True)

    combine(0, 0)

    slots_sent()
    for s in range(2):
        for way in range(2):
            for k in range(4):
                wait_for(rs_out.at[s, way, k, some], rs_send.at[s, way, k])
                if (s, way, k) not in ((0, 0, 0), (1, 1, 3)):
                    wait_for(ags.at[s, way, k, some], ag_send.at[s, way, k])
    for section in range(2):

        @pl.when(core != section)
        def far_end():
            wait_for(dgn.at[section], gx_send.at[section, 0])

        for step in range(1, nx):
            wait_for(dgn.at[section], gx_send.at[section, step])
    for which in range(4):
        wait_for(whole_part(which, 0), wf_send.at[which])
        wait_for(arrived_part(which), w_send.at[which])
    result_copies(gout, 0, False)
    wait_for(res.at[pl.ds(0, 2 * nx - 1)], res_recv.at[0])
    for which in range(3):
        staged_wait(which, 0)
        wait_for(landing[which].at[pl.ds(0, nd - 1)], ch_recv.at[which])
    wait_for(ei_far, e_recv.at[0])
    wait_for(eo_far, e_recv.at[1])
    wait_for(rg.at[pl.ds(0, nd - 1)], rg_recv.at[0])
    wait_for(rg.at[pl.ds(0, nd - 1)], rg_send.at[0])
    local(gs, rg.at[md], rg_own.at[0]).wait()

    def over_sources(parts):
        total = parts[0].astype(F32)
        for source in range(1, nd):
            total = total + parts[source].astype(F32)
        return total

    for j in range(2):
        dense_sum[j] = over_sources(ra[j])
    for c in range(2):
        feed_sum[c] = over_sources([rm[source, c] for source in range(nd)])
    gains_sum[...] = over_sources(rg)


def shards(
    nx,
    nd,
    boundary,
    norm_gains,
    attn_qkv,
    attn_out,
    mlp_in,
    mlp_out,
    expert_in,
    expert_out,
    expert_ids,
    expert_slots,
    gate_weights,
):
    tokens, features = boundary.shape[3:]
    rows = tokens // nx
    shard_rows = features // nd
    wide = attn_qkv.shape[4]
    units = mlp_in.shape[2]
    hidden = expert_in.shape[3]
    slots = nd * CAP
    quarters = features // 256
    slab = 16 * quarters + 16
    heads = wide // HEAD_DIM

    vmem = pl.BlockSpec(memory_space=pltpu.VMEM)
    hbm = pl.BlockSpec(memory_space=pl.ANY)
    dma = pltpu.SemaphoreType.DMA
    scratch = [
        pltpu.VMEM((2, nd, shard_rows, 4 * wide), BF16),
        pltpu.VMEM((nd, 2, shard_rows, units), BF16),
        pltpu.VMEM((nd, 8, features), F32),
        pltpu.VMEM((MICRO, 8, tokens), F32),
        pltpu.VMEM((shard_rows, 128), BF16),
        pltpu.VMEM((2, shard_rows, 4 * wide), BF16),
        pltpu.VMEM((2, shard_rows, units), BF16),
        pltpu.VMEM((4, wide, 4 * wide), BF16),
        pltpu.VMEM((tokens, features), F32),
        pltpu.VMEM((2, 2, features, 4 * wide), BF16),
        pltpu.VMEM((2, 2, features, units), BF16),
        pltpu.VMEM((2, 2, features, hidden), BF16),
        pltpu.VMEM((2, features, 128), BF16),
        pltpu.VMEM((2, 8, features), F32),
        pltpu.VMEM((2, 8, tokens), F32),
        pltpu.VMEM((2, tokens, tokens), F32),
        pltpu.VMEM((tokens, features), BF16),
        pltpu.VMEM((quarters, nd * 16, nd * (CAP - MAIN)), BF16),
        pltpu.VMEM((2, 2, slots, tokens), BF16),
        pltpu.VMEM((2, 4, rows, features), F32),
        pltpu.VMEM((2, 2, 4, nx, rows, features), BF16),
        pltpu.VMEM((2, 2, 4, nx, rows, features), BF16),
        pltpu.VMEM((2, 2, 4, nx, rows, features), BF16),
        pltpu.VMEM((nd, slab, 256), BF16),
        pltpu.VMEM((2, 4, nd, slab, 256), BF16),
        pltpu.VMEM((2, 2, 3, tokens, wide), BF16),
        pltpu.VMEM((2, 2, tokens, wide), BF16),
        pltpu.VMEM((2, 2, heads * tokens, tokens), F32),
        pltpu.VMEM((2, tokens, units), F32),
        pltpu.VMEM((2, tokens, units), BF16),
        pltpu.VMEM((2, slots, features), BF16),
        pltpu.VMEM((2, slots, hidden), F32),
        pltpu.VMEM((2, slots, hidden), BF16),
        pltpu.VMEM((2, features, 4 * wide), BF16),
        pltpu.VMEM((2, features, units), BF16),
        pltpu.VMEM((2, features, 4 * wide), BF16),
        pltpu.VMEM((2, features, units), BF16),
        pltpu.VMEM((2, features, hidden), BF16),
        pltpu.VMEM((2, 8, features), F32),
        pltpu.VMEM((2 * nx, 8, features), F32),
        pltpu.VMEM((8, features), F32),
        pltpu.VMEM((rows, features), F32),
        pltpu.VMEM((rows, features), F32),
        pltpu.VMEM((rows, features), F32),
        dma((2, 2, 4)),
        dma((2, 2, 4)),
        dma((2, 2, 4)),
        dma((2, 2, 4)),
        dma((1,)),
        dma((2, 4)),
        dma((4,)),
        dma((4,)),
        dma((4,)),
        dma((4,)),
        dma((4,)),
        dma((4,)),
        dma((4,)),
        dma((2,)),
        dma((3,)),
        dma((3,)),
        dma((3,)),
        dma((3,)),
        dma((3,)),
        dma((2,)),
        dma((2,)),
        dma((2,)),
        dma((1 + nx,)),
        dma((1,)),
        dma((1,)),
        dma((2, nx)),
        dma((1,)),
        dma((1,)),
        dma((1,)),
        dma((1,)),
    ]
    res, dense, feed, gains, ei_own, eo_own, ei_far, eo_far = pl.pallas_call(
        functools.partial(kernel, nx, nd),
        out_shape=(
            jax.ShapeDtypeStruct((2 * nx, rows, features), F32),
            jax.ShapeDtypeStruct((2, shard_rows, 4 * wide), F32),
            jax.ShapeDtypeStruct((2, shard_rows, units), F32),
            jax.ShapeDtypeStruct((8, features), F32),
            jax.ShapeDtypeStruct((features, hidden), BF16),
            jax.ShapeDtypeStruct((hidden, features), BF16),
            jax.ShapeDtypeStruct((features, hidden), BF16),
            jax.ShapeDtypeStruct((hidden, features), BF16),
        ),
        in_specs=[vmem] * 9 + [hbm] * 2,
        out_specs=(hbm,) + (vmem,) * 3 + (hbm,) * 4,
        scratch_shapes=scratch,
        compiler_params=pltpu.CompilerParams(
            collective_id=0, has_side_effects=True, vmem_limit_bytes=VMEM_LIMIT
        ),
    )(
        boundary[0, :, 0],
        jnp.swapaxes(expert_ids[0, :, 0], 1, 2),
        jnp.swapaxes(expert_slots[0, :, 0], 1, 2),
        jnp.swapaxes(gate_weights[0, :, 0], 1, 2),
        attn_qkv[0],
        jnp.swapaxes(attn_out[0], 1, 2),
        mlp_in[0],
        mlp_out[0].T,
        norm_gains[0],
        expert_in[0, 0],
        expert_out[0, 0],
    )

    gains = gains[: norm_gains.shape[1]]
    gains = lax.dynamic_slice_in_dim(gains, lax.axis_index("dp") * shard_rows, shard_rows, 1)
    qkv = dense[:, :, wide:].reshape(2, shard_rows, 3, wide)
    return (
        res.reshape(1, MICRO, 1, tokens, features),
        gains[None],
        jnp.swapaxes(qkv, 1, 2)[None],
        jnp.swapaxes(dense[:, :, :wide], 1, 2)[None],
        feed[0][None],
        feed[1].T[None],
        (ei_own.astype(F32) + ei_far.astype(F32))[None, None],
        (eo_own.astype(F32) + eo_far.astype(F32))[None, None],
    )


VMEM_LIMIT = 62 * 1024 * 1024


def solution(mesh):
    in_specs = (
        P("pipe", None, "dp", None, None),
        P("pipe", None, "dp"),
        P("pipe", None, None, "dp", "tensor"),
        P("pipe", None, "tensor", "dp"),
        P("pipe", "dp", "tensor"),
        P("pipe", "tensor", "dp"),
        P("pipe", "dp", None, "tensor"),
        P("pipe", "dp", "tensor", None),
        P("pipe", None, "dp", None, None),
        P("pipe", None, "dp", None, None),
        P("pipe", None, "dp", None, None),
    )
    out_specs = (
        P("pipe", None, "dp", None, None),
        P("pipe", None, "dp"),
        P("pipe", None, None, "dp", "tensor"),
        P("pipe", None, "tensor", "dp"),
        P("pipe", "dp", "tensor"),
        P("pipe", "tensor", "dp"),
        P("pipe", "dp", None, "tensor"),
        P("pipe", "dp", "tensor", None),
    )
    return jax.shard_map(
        functools.partial(shards, mesh.shape["tensor"], mesh.shape["dp"]),
        mesh=mesh,
        in_specs=in_specs,
        out_specs=out_specs,
        check_vma=False,
    )
```

```python
import functools

import jax
import jax.numpy as jnp
from jax import lax
from jax.experimental import pallas as pl
from jax.experimental.pallas import tpu as pltpu
from jax.sharding import PartitionSpec as P

MESH = pl.DeviceIdType.MESH
BF16 = jnp.bfloat16
F32 = jnp.float32
HEAD_DIM = 64
EPSILON = 1e-06
CAP = 20
MAIN = 16
MICRO = 2


def dims(lhs, rhs, left_dim, right_dim):
    return lax.dot_general(
        lhs, rhs, (((left_dim,), (right_dim,)), ((), ())), preferred_element_type=F32
    )


def nn(lhs, rhs):
    return dims(lhs, rhs, 1, 0)


def nt(lhs, rhs):
    return dims(lhs, rhs, 1, 1)


def tn(lhs, rhs):
    return dims(lhs, rhs, 0, 0)


def normal_cdf(pre):
    return 0.5 * (1.0 + lax.erf(pre * 0.7071067811865476))


def gelu_slope(pre, phi):
    return phi + pre * (0.3989422804014327 * jnp.exp(-0.5 * pre * pre))


def kernel(
    nx,
    nd,
    bnd,
    ids,
    seat,
    gate,
    sq,
    so,
    mi,
    mo,
    gains,
    ein,
    eout,
    res,
    dense_sum,
    feed_sum,
    gains_sum,
    ei_own,
    eo_own,
    ei_far,
    eo_far,
    ra,
    rm,
    rg,
    rt_in,
    sg,
    sa,
    sm,
    put,
    xh,
    wa,
    wm,
    we,
    wg,
    gn,
    rt,
    gt,
    bx,
    sel,
    sel_back,
    pk,
    hs,
    ags,
    rs_out,
    rs_in,
    a2_out,
    a2_in,
    proj,
    mix,
    prb,
    dgm,
    act,
    arr,
    dge,
    ace,
    ga,
    gm,
    pa,
    pm,
    eg,
    dgn,
    gx,
    gs,
    cur,
    hout,
    gout,
    ag_send,
    ag_recv,
    rs_send,
    rs_recv,
    a2_send,
    a2_recv,
    w_send,
    w_recv,
    w_own,
    wf_send,
    wf_recv,
    m_send,
    m_recv,
    m_own,
    pg_send,
    pg_recv,
    ch_send,
    ch_recv,
    ch_own,
    e_send,
    e_recv,
    e_own,
    res_send,
    res_recv,
    res_own,
    gx_send,
    gx_recv,
    rg_send,
    rg_recv,
    rg_own,
):
    core = lax.axis_index("pipe")
    md = lax.axis_index("dp")
    mx = lax.axis_index("tensor")
    other = 1 - core
    rows, features = cur.shape
    tokens = nx * rows
    shard_rows = sa.shape[1]
    wide_features = sq.shape[3]
    heads = wide_features // HEAD_DIM
    quarters = features // 256
    slots = nd * CAP
    extras = CAP - MAIN

    def x_peer(step):
        peer = mx + step
        return peer - jnp.where(peer >= nx, nx, 0)

    x_steps = sorted(range(1, nx), key=lambda step: -min(step, nx - step))

    def d_peer(step):
        peer = md + step
        return peer - jnp.where(peer >= nd, nd, 0)

    unit = 5 if (nd - 1) % 5 == 0 else 1

    def each_step(push):
        def some_steps(turn, carry):
            for at in range(unit):
                push(1 + turn * unit + at)
            return carry

        lax.fori_loop(0, (nd - 1) // unit, some_steps, 0)

    def far_first(step):
        turned = step + nd // 2 - 1
        return jnp.where(turned >= nd, turned - nd + 1, turned)

    def remote(src, dst, send, recv, **where):
        return pltpu.make_async_remote_copy(
            src_ref=src,
            dst_ref=dst,
            send_sem=send,
            recv_sem=recv,
            device_id=where,
            device_id_type=MESH,
        )

    def local(src, dst, sem):
        return pltpu.make_async_copy(src, dst, sem)

    def wait_for(ref, sem):
        pltpu.make_async_copy(ref, ref, sem).wait()

    barrier = pltpu.get_barrier_semaphore()

    def greet(step, carry):
        pl.semaphore_signal(
            barrier, inc=1, device_id={"dp": d_peer(step)}, device_id_type=MESH
        )
        return carry

    lax.fori_loop(1, nd, greet, 0)
    for step in range(1, nx):
        pl.semaphore_signal(
            barrier, inc=1, device_id={"tensor": x_peer(step)}, device_id_type=MESH
        )
    for step in range(nx):
        pl.semaphore_signal(
            barrier,
            inc=1,
            device_id={"pipe": other, "tensor": x_peer(step)},
            device_id_type=MESH,
        )

    mine = pl.ds(md * shard_rows, shard_rows)
    shard_src = (sg, sa.at[0], sm, sa.at[1])
    shard_dst = (
        wg.at[core, mine],
        wa.at[core, 0, mine],
        wm.at[core, :, mine],
        wa.at[core, 1, mine],
    )

    def share_weight(which):
        def push(step):
            remote(
                shard_src[which],
                shard_dst[which],
                w_send.at[which],
                w_recv.at[which],
                dp=d_peer(step),
            ).start()

        local(shard_src[which], shard_dst[which], w_own.at[which]).start()
        each_step(push)

    all_but_one = pl.ds(0, (nd - 1) * shard_rows)

    def arrived_part(which):
        if which == 0:
            return wg.at[0, all_but_one]
        if which == 2:
            return wm.at[0, :, all_but_one]
        return wa.at[0, which // 2, all_but_one]

    def whole_part(which, section):
        if which == 0:
            return wg.at[section]
        if which == 2:
            return wm.at[section]
        return wa.at[section, which // 2]

    def weight_forward(which):
        wait_for(arrived_part(which), w_recv.at[which])
        local(shard_src[which], shard_dst[which], w_own.at[which]).wait()
        remote(
            whole_part(which, core),
            whole_part(which, core),
            wf_send.at[which],
            wf_recv.at[which],
            pipe=other,
        ).start()

    def weight_ready(which):
        wait_for(whole_part(which, 0), wf_recv.at[which])

    def misc_copies():
        return (
            remote(bnd.at[other], bx, m_send.at[0], m_recv.at[0], pipe=other),
            remote(rt_in.at[other], rt.at[core], m_send.at[1], m_recv.at[1], pipe=other),
        )

    def expert_copies():
        return (
            remote(ein, we.at[core, 0], m_send.at[2], m_recv.at[2], pipe=other),
            remote(eout, we.at[core, 1], m_send.at[3], m_recv.at[3], pipe=other),
        )

    def expert_own():
        return (
            local(ein, we.at[core, 0], m_own.at[0]),
            local(eout, we.at[core, 1], m_own.at[1]),
        )

    put_row = lax.broadcasted_iota(jnp.int32, put.shape[1:], 0)
    put_col = lax.broadcasted_iota(jnp.int32, put.shape[1:], 1)
    for c in range(4):
        put[c] = jnp.where(put_col == put_row + c * wide_features, 1.0, 0.0).astype(BF16)

    def attention_shard(j):
        total = nn(so[j], put[0])
        for c in range(3):
            total = total + nn(sq[j, c], put[1 + c])
        sa[j] = total.astype(BF16)

    attention_shard(0)
    count = gains.shape[0]
    pick_row = lax.broadcasted_iota(jnp.int32, (count, 128), 0)
    pick_col = lax.broadcasted_iota(jnp.int32, (count, 128), 1)
    sg[...] = tn(gains[...], jnp.where(pick_row == pick_col, 1.0, 0.0).astype(BF16)).astype(BF16)
    for m in range(MICRO):
        expert = ids[m]
        seats = seat[m]
        place = jnp.where(
            seats < MAIN,
            expert * MAIN + seats,
            nd * MAIN + expert * extras + seats - MAIN,
        )
        rt_in[m] = jnp.concatenate(
            [place.astype(F32), gate[m], jnp.zeros((4, tokens), F32)], axis=0
        )

    pl.semaphore_wait(barrier, (nd - 1) + (nx - 1) + nx)

    @pl.when(core == 0)
    def first_attention():
        share_weight(1)

    for copy in misc_copies():
        copy.start()
    share_weight(0)
    sm[0] = mi[...]
    sm[1] = mo[...]
    attention_shard(1)

    @pl.when(core == 0)
    def first_section():
        share_weight(2)
        share_weight(3)

    rt[core] = rt_in[core]
    row_id = lax.broadcasted_iota(jnp.int32, (nd * 16, nd * extras), 0)
    col_id = lax.broadcasted_iota(jnp.int32, (nd * 16, nd * extras), 1)
    back_row = lax.broadcasted_iota(jnp.int32, (nd * extras, nd * 16), 0)
    back_col = lax.broadcasted_iota(jnp.int32, (nd * extras, nd * 16), 1)
    for q in range(quarters):
        hit = (
            ((row_id >> 4) == (col_id >> 2))
            & (((row_id >> 2) & 3) == q)
            & ((row_id & 3) == (col_id & 3))
        )
        sel[q] = jnp.where(hit, 1.0, 0.0).astype(BF16)
        hit = (
            ((back_col >> 4) == (back_row >> 2))
            & (((back_col >> 2) & 3) == q)
            & ((back_col & 3) == (back_row & 3))
        )
        sel_back[q] = jnp.where(hit, 1.0, 0.0).astype(BF16)
    dgn[...] = jnp.zeros_like(dgn)

    for copy in misc_copies():
        copy.wait()
    place = lax.broadcasted_iota(jnp.int32, (slots, tokens), 0)
    for s in range(2):
        table = rt[s]
        for k in range(2):
            hit = place == table[k : k + 1].astype(jnp.int32)
            pk[s, k] = jnp.where(hit, 1.0, 0.0).astype(BF16)
        gt[s] = jnp.transpose(jnp.concatenate([table] * (tokens // 8), axis=0))

    @pl.when(core == 0)
    def first_input():
        ags[0, 0, 0] = bnd[0].reshape(nx, rows, features)
        ags[1, 1, 3] = bx[...].reshape(nx, rows, features)

    @pl.when(core == 1)
    def second_input():
        ags[0, 0, 0] = bx[...].reshape(nx, rows, features)
        ags[1, 1, 3] = bnd[1].reshape(nx, rows, features)

    cur[...] = ags[0, 0, 0, mx].astype(F32)
    weight_forward(0)
    weight_ready(0)
    for s in range(2):
        turned = jnp.transpose(wg[s].astype(F32))
        gn[s] = turned[:8]

    lane = lax.broadcasted_iota(jnp.int32, (1, wide_features), 1)
    head_masks = [
        jnp.where((lane >= h * HEAD_DIM) & (lane < (h + 1) * HEAD_DIM), 1.0, 0.0).astype(BF16)
        for h in range(heads)
    ]

    def per_head(values):
        return [values * mask for mask in head_masks]

    def norm_parts(stream):
        center = stream - jnp.mean(stream, axis=-1, keepdims=True)
        scale = lax.rsqrt(jnp.mean(center * center, axis=-1, keepdims=True) + EPSILON)
        return center * scale, scale

    def norm_back(s, k, parts, grad_normed):
        normal, scale = parts
        gain_rows = jnp.sum(grad_normed * normal, axis=0, keepdims=True)
        if k == 0:

            @pl.when(s == 1)
            def not_sent_yet():
                dgn[s, k : k + 1, :] = gain_rows

        else:
            dgn[s, k : k + 1, :] = gain_rows
        pulled = grad_normed * gn[s][k : k + 1]
        return scale * (
            pulled
            - jnp.mean(pulled, axis=-1, keepdims=True)
            - normal * jnp.mean(pulled * normal, axis=-1, keepdims=True)
        )

    some = pl.ds(0, nx - 1)

    def all_rows(s, way, k, own_rows, meanwhile=None):
        ags[s, way, k, mx] = own_rows.astype(BF16)
        for step in x_steps:
            remote(
                ags.at[s, way, k, mx],
                ags.at[s, way, k, mx],
                ag_send.at[s, way, k],
                ag_recv.at[s, way, k],
                tensor=x_peer(step),
            ).start()
        if meanwhile is not None:
            meanwhile()
        wait_for(ags.at[s, way, k, some], ag_recv.at[s, way, k])
        return ags[s, way, k].reshape(tokens, features)

    def sum_start(s, way, k, partial_rows):
        rs_out[s, way, k] = partial_rows.astype(BF16).reshape(nx, rows, features)
        for step in x_steps:
            peer = x_peer(step)
            remote(
                rs_out.at[s, way, k, peer],
                rs_in.at[s, way, k, mx],
                rs_send.at[s, way, k],
                rs_recv.at[s, way, k],
                tensor=peer,
            ).start()

    def sum_end(s, way, k):
        wait_for(rs_in.at[s, way, k, some], rs_recv.at[s, way, k])
        total = rs_out[s, way, k, mx].astype(F32)
        for step in range(1, nx):
            total = total + rs_in[s, way, k, x_peer(step)].astype(F32)
        return total

    def slots_start(s, which, values):
        main = values[: nd * MAIN]
        extra = values[nd * MAIN :]
        folded = None
        for q in range(quarters):
            columns = slice(256 * q, 256 * (q + 1))
            a2_out[:, 16 * q : 16 * (q + 1), :] = main[:, columns].reshape(nd, 16, 256)
            term = nn(sel[q], extra[:, columns])
            folded = term if folded is None else folded + term
        a2_out[:, 16 * quarters :, :] = folded.astype(BF16).reshape(nd, 16, 256)

        def push(step):
            peer = d_peer(far_first(step))
            remote(
                a2_out.at[peer],
                a2_in.at[s, which, md],
                a2_send.at[0],
                a2_recv.at[s, which],
                dp=peer,
            ).start()

        each_step(push)
        a2_in[s, which, md] = a2_out[md]

    def slots_end(s, which):
        wait_for(a2_in.at[s, which, pl.ds(0, nd - 1)], a2_recv.at[s, which])
        mains = []
        extra = []
        folded = a2_in[s, which, :, 16 * quarters :, :].reshape(nd * 16, 256)
        for q in range(quarters):
            block = a2_in[s, which, :, 16 * q : 16 * (q + 1), :]
            mains.append(block.reshape(nd * 16, 256))
            extra.append(nn(sel_back[q], folded).astype(BF16))
        return jnp.concatenate(
            [jnp.concatenate(mains, axis=1), jnp.concatenate(extra, axis=1)], axis=0
        )

    def slots_sent():
        wait_for(a2_out.at[pl.ds(0, nd - 1)], a2_send.at[0])

    def dback_start(s, grad_rows):
        wide = grad_rows.astype(F32)
        gates = gt[s]
        dback = nn(pk[s, 0], (wide * gates[:, 2:3]).astype(BF16)) + nn(
            pk[s, 1], (wide * gates[:, 3:4]).astype(BF16)
        )
        slots_start(s, 2, dback.astype(BF16))

    def attend(s, j, k):
        stream = cur[...]
        hs[s, k] = stream
        normal, unused = norm_parts(stream)
        if j == 0:

            @pl.when(s != 0)
            def fetch():
                all_rows(s, 0, k, normal * gn[s][k : k + 1])

            normed = ags[s, 0, k].reshape(tokens, features)
        else:
            normed = all_rows(s, 0, k, normal * gn[s][k : k + 1])

        @pl.when(core != s)
        def weights():
            weight_ready(1 + 2 * j)

        projected = nn(normed, wa[s, j])
        query, key, value = [
            projected[:, c * wide_features : (c + 1) * wide_features].astype(BF16)
            for c in range(1, 4)
        ]
        proj[s, j, 0] = query
        proj[s, j, 1] = key
        proj[s, j, 2] = value
        logits = nt(jnp.concatenate(per_head(query), axis=0), key) * (HEAD_DIM**-0.5)
        exponent = jnp.exp(logits - jnp.max(logits, axis=-1, keepdims=True))
        probs = exponent / jnp.sum(exponent, axis=-1, keepdims=True)
        prb[s, j] = probs
        low = probs.astype(BF16)
        mixed = None
        for h, part in enumerate(per_head(value)):
            term = nn(low[h * tokens : (h + 1) * tokens], part)
            mixed = term if mixed is None else mixed + term
        mixed = mixed.astype(BF16)
        mix[s, j] = mixed
        sum_start(s, 0, k, nt(mixed, wa[s, j, :, :wide_features]))

        if j == 1:

            @pl.when((s == 0) & (core == 1))
            def share():
                share_weight(3)

            @pl.when(s == 1)
            def early_end():
                slots_sent()

        cur[...] = stream + sum_end(s, 0, k)

    def feed(s):
        stream = cur[...]
        hs[s, 1] = stream
        normal, unused = norm_parts(stream)

        def meanwhile():
            @pl.when((s == 0) & (core == 0))
            def onward():
                weight_forward(2)

        normed = all_rows(s, 0, 1, normal * gn[s][1:2], meanwhile)

        @pl.when(core != s)
        def weights():
            weight_ready(2)

        pre = nn(normed, wm[s, 0])
        phi = normal_cdf(pre)
        active = (pre * phi).astype(BF16)
        sum_start(s, 0, 1, nt(active, wm[s, 1]))
        act[s] = active
        dgm[s] = gelu_slope(pre, phi)

        @pl.when((s == 0) & (core == 0))
        def onward():
            weight_forward(3)

        @pl.when((s == 0) & (core == 1))
        def share():
            share_weight(1)
            share_weight(2)

        @pl.when(s == 1)
        def early():
            slots_sent()
            dback_start(s, ags[1, 1, 3].reshape(tokens, features))

        cur[...] = stream + sum_end(s, 0, 1)

    def experts(s):
        stream = cur[...]
        hs[s, 3] = stream
        normal, unused = norm_parts(stream)
        normed = all_rows(s, 0, 3, normal * gn[s][3:4])
        slots_start(s, 0, nn(pk[s, 0] + pk[s, 1], normed).astype(BF16))

        @pl.when(s == 0)
        def weights():
            for copy in expert_copies() + expert_own():
                copy.wait()

        sent = slots_end(s, 0)
        pre = nn(sent, we[s, 0])
        phi = normal_cdf(pre)
        active = (pre * phi).astype(BF16)
        partial_rows = nn(active, we[s, 1]).astype(BF16)
        slots_sent()
        slots_start(s, 1, partial_rows)
        arr[s] = sent
        ace[s] = active
        dge[s] = gelu_slope(pre, phi)

    def experts_start(s):
        back = slots_end(s, 1)
        gates = gt[s]
        partial_rows = tn(pk[s, 0], back) * gates[:, 2:3] + tn(pk[s, 1], back) * gates[:, 3:4]
        sum_start(s, 0, 3, partial_rows)

    def experts_end(s):
        return hs[s, 3] + sum_end(s, 0, 3)

    def forward(s, carry):
        cur[...] = cur[...].astype(BF16).astype(F32)
        attend(s, 0, 0)
        feed(s)
        attend(s, 1, 2)
        experts(s)

        @pl.when(s == 0)
        def to_the_next():
            @pl.when(core == 1)
            def onward():
                for which in range(1, 4):
                    weight_forward(which)

            experts_start(s)
            cur[...] = experts_end(s)

        return carry

    def result_copies(buffer, target, start):
        slot = core * nx + mx

        @pl.when(core == target)
        def near():
            copy = local(buffer, res.at[slot], res_own.at[0])
            copy.start() if start else copy.wait()

        @pl.when(core != target)
        def far():
            copy = remote(
                buffer,
                res.at[slot],
                res_send.at[1],
                res_recv.at[0],
                pipe=target,
            )
            copy.start() if start else copy.wait_send()

        for step in range(1, nx):
            copy = remote(
                buffer,
                res.at[slot],
                res_send.at[1 + step],
                res_recv.at[0],
                pipe=target,
                tensor=x_peer(step),
            )
            copy.start() if start else copy.wait_send()

    @pl.when(core == 0)
    def first_weights():
        weight_forward(1)

    for copy in expert_copies() + expert_own():
        copy.start()
    given = ags[0, 0, 0].reshape(tokens, features).astype(F32)
    normal, unused = norm_parts(given)
    xh[...] = normal
    ags[0, 0, 0] = (normal * gn[0][0:1]).astype(BF16).reshape(nx, rows, features)
    lax.fori_loop(0, 2, forward, 0)

    staged = (ga.at[0], gm, ga.at[1])
    partner = (pa.at[0], pm, pa.at[1])
    landing = (ra.at[0], rm, ra.at[1])

    def some_rows(which, part):
        return staged[which].at[:, part] if which == 1 else staged[which].at[part]

    def chunk(which, owner):
        return some_rows(which, pl.ds(owner * shard_rows, shard_rows))

    def staged_wait(which, section):
        @pl.when(core == section)
        def owned():
            wait_for(some_rows(which, all_but_one), ch_send.at[which])
            local(chunk(which, md), landing[which].at[md], ch_own.at[which]).wait()

        @pl.when(core != section)
        def lent():
            wait_for(staged[which], pg_send.at[which])

    def lend(which, section):
        @pl.when(core != section)
        def lent():
            remote(
                staged[which],
                partner[which],
                pg_send.at[which],
                pg_recv.at[which],
                pipe=other,
            ).start()

    def combine(which, section):
        @pl.when(core == section)
        def owned():
            wait_for(partner[which], pg_recv.at[which])
            staged[which][...] = (
                staged[which][...].astype(F32) + partner[which][...].astype(F32)
            ).astype(BF16)

            def push(step):
                peer = d_peer(step)
                remote(
                    chunk(which, peer),
                    landing[which].at[md],
                    ch_send.at[which],
                    ch_recv.at[which],
                    dp=peer,
                ).start()

            each_step(push)
            local(chunk(which, md), landing[which].at[md], ch_own.at[which]).start()

    def gains_start():
        place_here = core * nx + mx
        for section in range(2):

            @pl.when(core == section)
            def near():
                gx[place_here] = dgn[section]

            @pl.when(core != section)
            def far():
                remote(
                    dgn.at[section],
                    gx.at[place_here],
                    gx_send.at[section, 0],
                    gx_recv.at[0],
                    pipe=section,
                ).start()

            for step in range(1, nx):
                remote(
                    dgn.at[section],
                    gx.at[place_here],
                    gx_send.at[section, step],
                    gx_recv.at[0],
                    pipe=section,
                    tensor=x_peer(step),
                ).start()

    def gains_push():
        wait_for(gx.at[pl.ds(0, 2 * nx - 1)], gx_recv.at[0])
        gains_total = gx[0]
        for source in range(1, 2 * nx):
            gains_total = gains_total + gx[source]
        gs[...] = gains_total

        def push_gains(step):
            remote(gs, rg.at[md], rg_send.at[0], rg_recv.at[0], dp=d_peer(step)).start()

        each_step(push_gains)
        local(gs, rg.at[md], rg_own.at[0]).start()

    def experts_back(s):
        grad = cur[...]

        @pl.when(s == 0)
        def later():
            wide = all_rows(s, 1, 3, grad, slots_sent)
            dback_start(s, wide)
            combine(0, 1)

        dback = slots_end(s, 2)
        dpre = (nt(dback, we[s, 1]) * dge[s]).astype(BF16)
        dsent = nt(dpre, we[s, 0]).astype(BF16)
        slots_sent()
        slots_start(s, 3, dsent)

        @pl.when(s == 1)
        def last_result_start():
            experts_start(s)

        eg[0] = tn(arr[s], dpre).astype(BF16)
        eg[1] = tn(ace[s], dback).astype(BF16)

        @pl.when(core == s)
        def keep():
            local(eg.at[0], ei_own, e_own.at[0]).start()
            local(eg.at[1], eo_own, e_own.at[1]).start()

        @pl.when(core != s)
        def give():
            remote(eg.at[0], ei_far, e_send.at[0], e_recv.at[0], pipe=other).start()
            remote(eg.at[1], eo_far, e_send.at[1], e_recv.at[1], pipe=other).start()

        @pl.when(s == 1)
        def last_result_end():
            hout[...] = experts_end(s)
            result_copies(hout, 1, True)

        parts = norm_parts(hs[s, 3])
        dsent = slots_end(s, 3)
        sum_start(s, 1, 3, tn(pk[s, 0] + pk[s, 1], dsent))
        cur[...] = grad + norm_back(s, 3, parts, sum_end(s, 1, 3))

    def attend_back(s, j, k):
        grad = cur[...]
        dz = all_rows(s, 1, k, grad, (lambda: combine(1, s)) if j == 0 else None)
        dmixed = nn(dz, wa[s, j, :, :wide_features]).astype(BF16)
        query, key, value = [proj[s, j, c] for c in range(3)]
        probs = prb[s, j]
        dmixed_heads = jnp.concatenate(per_head(dmixed), axis=0)
        dprobs = nt(dmixed_heads, value)
        dscores = probs * (dprobs - jnp.sum(probs * dprobs, axis=-1, keepdims=True))
        dscores = dscores.astype(BF16)
        dvalue = tn(probs.astype(BF16), dmixed_heads)
        dkey = tn(dscores, jnp.concatenate(per_head(query), axis=0)) * (HEAD_DIM**-0.5)
        dquery = None
        for h, part in enumerate(per_head(key)):
            term = nn(dscores[h * tokens : (h + 1) * tokens], part)
            dquery = term if dquery is None else dquery + term
        dquery = dquery * (HEAD_DIM**-0.5)
        dproj = [d.astype(BF16) for d in (dquery, dkey, dvalue)]
        placed = None
        for c in range(3):
            term = nn(dproj[c], put[1 + c])
            placed = term if placed is None else placed + term
        placed = placed.astype(BF16)
        partial_rows = nt(placed, wa[s, j])

        def weight_grads():
            normed = ags[s, 0, k].reshape(tokens, features)
            mixed = nn(mix[s, j], put[0]).astype(BF16)
            ga[j] = tn(
                jnp.concatenate([normed, dz], axis=0), jnp.concatenate([placed, mixed], axis=0)
            ).astype(BF16)
            lend(2 * j, s)

        if j == 0:

            @pl.when(s == 0)
            def last_of_all():
                dgn[0, 0:1, :] = jnp.sum(partial_rows * xh[...], axis=0, keepdims=True)
                gains_start()
                staged_wait(0, 1)
                weight_grads()

            sum_start(s, 1, k, partial_rows)

            @pl.when(s == 1)
            def not_last():
                weight_grads()

            @pl.when(s == 0)
            def last_onward():
                gains_push()
                combine(0, 0)

        else:
            sum_start(s, 1, k, partial_rows)

            @pl.when(s == 0)
            def free():
                staged_wait(2, 1)

            weight_grads()

        parts = norm_parts(hs[s, k])
        cur[...] = grad + norm_back(s, k, parts, sum_end(s, 1, k))

    def feed_back(s):
        grad = cur[...]
        dout = all_rows(s, 1, 1, grad, lambda: combine(2, s))
        dpre = (nn(dout, wm[s, 1]) * dgm[s]).astype(BF16)
        sum_start(s, 1, 1, nt(dpre, wm[s, 0]))

        @pl.when(s == 0)
        def free():
            staged_wait(1, 1)

        normed = ags[s, 0, 1].reshape(tokens, features)
        gm[0] = tn(normed, dpre).astype(BF16)
        gm[1] = tn(dout, act[s]).astype(BF16)
        lend(1, s)
        parts = norm_parts(hs[s, 1])
        cur[...] = grad + norm_back(s, 1, parts, sum_end(s, 1, 1))

    def expert_grads_wait(s):
        @pl.when(core == s)
        def keep():
            local(eg.at[0], ei_own, e_own.at[0]).wait()
            local(eg.at[1], eo_own, e_own.at[1]).wait()

        @pl.when(core != s)
        def give():
            wait_for(eg.at[0], e_send.at[0])
            wait_for(eg.at[1], e_send.at[1])

    def backward(turn, carry):
        s = 1 - turn
        cur[...] = cur[...].astype(BF16).astype(F32)
        experts_back(s)
        attend_back(s, 1, 2)
        feed_back(s)
        attend_back(s, 0, 0)
        expert_grads_wait(s)
        return carry

    cur[...] = ags[1, 1, 3, mx].astype(F32)
    lax.fori_loop(0, 2, backward, 0)
    gout[...] = cur[...]
    result_copies(hout, 1, False)
    result_copies(gout, 0, True)

    slots_sent()
    for s in range(2):
        for way in range(2):
            for k in range(4):
                wait_for(rs_out.at[s, way, k, some], rs_send.at[s, way, k])
                if (s, way, k) not in ((0, 0, 0), (1, 1, 3)):
                    wait_for(ags.at[s, way, k, some], ag_send.at[s, way, k])
    for section in range(2):

        @pl.when(core != section)
        def far_end():
            wait_for(dgn.at[section], gx_send.at[section, 0])

        for step in range(1, nx):
            wait_for(dgn.at[section], gx_send.at[section, step])
    for which in range(4):
        wait_for(whole_part(which, 0), wf_send.at[which])
        wait_for(arrived_part(which), w_send.at[which])
    result_copies(gout, 0, False)
    wait_for(res.at[pl.ds(0, 2 * nx - 1)], res_recv.at[0])
    def over_sources(parts):
        total = parts[0].astype(F32)
        for source in range(1, nd):
            total = total + parts[source].astype(F32)
        return total

    def landed(which):
        staged_wait(which, 0)
        wait_for(landing[which].at[pl.ds(0, nd - 1)], ch_recv.at[which])

    landed(2)
    dense_sum[1] = over_sources(ra[1])
    landed(1)
    for c in range(2):
        feed_sum[c] = over_sources([rm[source, c] for source in range(nd)])
    wait_for(ei_far, e_recv.at[0])
    wait_for(eo_far, e_recv.at[1])
    wait_for(rg.at[pl.ds(0, nd - 1)], rg_recv.at[0])
    wait_for(rg.at[pl.ds(0, nd - 1)], rg_send.at[0])
    local(gs, rg.at[md], rg_own.at[0]).wait()
    gains_sum[...] = over_sources(rg)
    landed(0)
    dense_sum[0] = over_sources(ra[0])


def shards(
    nx,
    nd,
    boundary,
    norm_gains,
    attn_qkv,
    attn_out,
    mlp_in,
    mlp_out,
    expert_in,
    expert_out,
    expert_ids,
    expert_slots,
    gate_weights,
):
    tokens, features = boundary.shape[3:]
    rows = tokens // nx
    shard_rows = features // nd
    wide = attn_qkv.shape[4]
    units = mlp_in.shape[2]
    hidden = expert_in.shape[3]
    slots = nd * CAP
    quarters = features // 256
    slab = 16 * quarters + 16
    heads = wide // HEAD_DIM

    vmem = pl.BlockSpec(memory_space=pltpu.VMEM)
    hbm = pl.BlockSpec(memory_space=pl.ANY)
    dma = pltpu.SemaphoreType.DMA
    scratch = [
        pltpu.VMEM((2, nd, shard_rows, 4 * wide), BF16),
        pltpu.VMEM((nd, 2, shard_rows, units), BF16),
        pltpu.VMEM((nd, 8, features), F32),
        pltpu.VMEM((MICRO, 8, tokens), F32),
        pltpu.VMEM((shard_rows, 128), BF16),
        pltpu.VMEM((2, shard_rows, 4 * wide), BF16),
        pltpu.VMEM((2, shard_rows, units), BF16),
        pltpu.VMEM((4, wide, 4 * wide), BF16),
        pltpu.VMEM((tokens, features), F32),
        pltpu.VMEM((2, 2, features, 4 * wide), BF16),
        pltpu.VMEM((2, 2, features, units), BF16),
        pltpu.VMEM((2, 2, features, hidden), BF16),
        pltpu.VMEM((2, features, 128), BF16),
        pltpu.VMEM((2, 8, features), F32),
        pltpu.VMEM((2, 8, tokens), F32),
        pltpu.VMEM((2, tokens, tokens), F32),
        pltpu.VMEM((tokens, features), BF16),
        pltpu.VMEM((quarters, nd * 16, nd * (CAP - MAIN)), BF16),
        pltpu.VMEM((quarters, nd * (CAP - MAIN), nd * 16), BF16),
        pltpu.VMEM((2, 2, slots, tokens), BF16),
        pltpu.VMEM((2, 4, rows, features), F32),
        pltpu.VMEM((2, 2, 4, nx, rows, features), BF16),
        pltpu.VMEM((2, 2, 4, nx, rows, features), BF16),
        pltpu.VMEM((2, 2, 4, nx, rows, features), BF16),
        pltpu.VMEM((nd, slab, 256), BF16),
        pltpu.VMEM((2, 4, nd, slab, 256), BF16),
        pltpu.VMEM((2, 2, 3, tokens, wide), BF16),
        pltpu.VMEM((2, 2, tokens, wide), BF16),
        pltpu.VMEM((2, 2, heads * tokens, tokens), F32),
        pltpu.VMEM((2, tokens, units), F32),
        pltpu.VMEM((2, tokens, units), BF16),
        pltpu.VMEM((2, slots, features), BF16),
        pltpu.VMEM((2, slots, hidden), F32),
        pltpu.VMEM((2, slots, hidden), BF16),
        pltpu.VMEM((2, features, 4 * wide), BF16),
        pltpu.VMEM((2, features, units), BF16),
        pltpu.VMEM((2, features, 4 * wide), BF16),
        pltpu.VMEM((2, features, units), BF16),
        pltpu.VMEM((2, features, hidden), BF16),
        pltpu.VMEM((2, 8, features), F32),
        pltpu.VMEM((2 * nx, 8, features), F32),
        pltpu.VMEM((8, features), F32),
        pltpu.VMEM((rows, features), F32),
        pltpu.VMEM((rows, features), F32),
        pltpu.VMEM((rows, features), F32),
        dma((2, 2, 4)),
        dma((2, 2, 4)),
        dma((2, 2, 4)),
        dma((2, 2, 4)),
        dma((1,)),
        dma((2, 4)),
        dma((4,)),
        dma((4,)),
        dma((4,)),
        dma((4,)),
        dma((4,)),
        dma((4,)),
        dma((4,)),
        dma((2,)),
        dma((3,)),
        dma((3,)),
        dma((3,)),
        dma((3,)),
        dma((3,)),
        dma((2,)),
        dma((2,)),
        dma((2,)),
        dma((1 + nx,)),
        dma((1,)),
        dma((1,)),
        dma((2, nx)),
        dma((1,)),
        dma((1,)),
        dma((1,)),
        dma((1,)),
    ]
    res, dense, feed, gains, ei_own, eo_own, ei_far, eo_far = pl.pallas_call(
        functools.partial(kernel, nx, nd),
        out_shape=(
            jax.ShapeDtypeStruct((2 * nx, rows, features), F32),
            jax.ShapeDtypeStruct((2, shard_rows, 4 * wide), F32),
            jax.ShapeDtypeStruct((2, shard_rows, units), F32),
            jax.ShapeDtypeStruct((8, features), F32),
            jax.ShapeDtypeStruct((features, hidden), BF16),
            jax.ShapeDtypeStruct((hidden, features), BF16),
            jax.ShapeDtypeStruct((features, hidden), BF16),
            jax.ShapeDtypeStruct((hidden, features), BF16),
        ),
        in_specs=[vmem] * 9 + [hbm] * 2,
        out_specs=(hbm,) + (vmem,) * 3 + (hbm,) * 4,
        scratch_shapes=scratch,
        compiler_params=pltpu.CompilerParams(
            collective_id=0, has_side_effects=True, vmem_limit_bytes=VMEM_LIMIT
        ),
    )(
        boundary[0, :, 0],
        jnp.swapaxes(expert_ids[0, :, 0], 1, 2),
        jnp.swapaxes(expert_slots[0, :, 0], 1, 2),
        jnp.swapaxes(gate_weights[0, :, 0], 1, 2),
        attn_qkv[0],
        jnp.swapaxes(attn_out[0], 1, 2),
        mlp_in[0],
        mlp_out[0].T,
        norm_gains[0],
        expert_in[0, 0],
        expert_out[0, 0],
    )

    gains = gains[: norm_gains.shape[1]]
    gains = lax.dynamic_slice_in_dim(gains, lax.axis_index("dp") * shard_rows, shard_rows, 1)
    qkv = dense[:, :, wide:].reshape(2, shard_rows, 3, wide)
    return (
        res.reshape(1, MICRO, 1, tokens, features),
        gains[None],
        jnp.swapaxes(qkv, 1, 2)[None],
        jnp.swapaxes(dense[:, :, :wide], 1, 2)[None],
        feed[0][None],
        feed[1].T[None],
        (ei_own.astype(F32) + ei_far.astype(F32))[None, None],
        (eo_own.astype(F32) + eo_far.astype(F32))[None, None],
    )


VMEM_LIMIT = 62 * 1024 * 1024


def solution(mesh):
    in_specs = (
        P("pipe", None, "dp", None, None),
        P("pipe", None, "dp"),
        P("pipe", None, None, "dp", "tensor"),
        P("pipe", None, "tensor", "dp"),
        P("pipe", "dp", "tensor"),
        P("pipe", "tensor", "dp"),
        P("pipe", "dp", None, "tensor"),
        P("pipe", "dp", "tensor", None),
        P("pipe", None, "dp", None, None),
        P("pipe", None, "dp", None, None),
        P("pipe", None, "dp", None, None),
    )
    out_specs = (
        P("pipe", None, "dp", None, None),
        P("pipe", None, "dp"),
        P("pipe", None, None, "dp", "tensor"),
        P("pipe", None, "tensor", "dp"),
        P("pipe", "dp", "tensor"),
        P("pipe", "tensor", "dp"),
        P("pipe", "dp", None, "tensor"),
        P("pipe", "dp", "tensor", None),
    )
    return jax.shard_map(
        functools.partial(shards, mesh.shape["tensor"], mesh.shape["dp"]),
        mesh=mesh,
        in_specs=in_specs,
        out_specs=out_specs,
        check_vma=False,
    )
```

```python
import functools

import jax
import jax.numpy as jnp
from jax import lax
from jax.experimental import pallas as pl
from jax.experimental.pallas import tpu as pltpu
from jax.sharding import PartitionSpec as P

MESH = pl.DeviceIdType.MESH
BF16 = jnp.bfloat16
F32 = jnp.float32
HEAD_DIM = 64
EPSILON = 1e-06
CAP = 20
MAIN = 16
MICRO = 2


def dims(lhs, rhs, left_dim, right_dim):
    return lax.dot_general(
        lhs, rhs, (((left_dim,), (right_dim,)), ((), ())), preferred_element_type=F32
    )


def nn(lhs, rhs):
    return dims(lhs, rhs, 1, 0)


def nt(lhs, rhs):
    return dims(lhs, rhs, 1, 1)


def tn(lhs, rhs):
    return dims(lhs, rhs, 0, 0)


def normal_cdf(pre):
    return 0.5 * (1.0 + lax.erf(pre * 0.7071067811865476))


def gelu_slope(pre, phi):
    return phi + pre * (0.3989422804014327 * jnp.exp(-0.5 * pre * pre))


def kernel(
    nx,
    nd,
    bnd,
    ids,
    seat,
    gate,
    sq,
    so,
    mi,
    mo,
    gains,
    ein,
    eout,
    res,
    dense_sum,
    feed_sum,
    gains_sum,
    ei_own,
    eo_own,
    ei_far,
    eo_far,
    ra,
    rm,
    rg,
    rt_in,
    sg,
    sa,
    sm,
    put,
    xh,
    wa,
    wm,
    we,
    wg,
    gn,
    rt,
    gt,
    bx,
    sel,
    sel_back,
    pk,
    hs,
    ags,
    rs_out,
    rs_in,
    a2_out,
    a2_in,
    proj,
    mix,
    prb,
    dgm,
    act,
    arr,
    dge,
    ace,
    ga,
    gm,
    pa,
    pm,
    eg,
    dgn,
    gx,
    gs,
    cur,
    hout,
    gout,
    ag_send,
    ag_recv,
    rs_send,
    rs_recv,
    a2_send,
    a2_recv,
    w_send,
    w_recv,
    w_own,
    wf_send,
    wf_recv,
    m_send,
    m_recv,
    m_own,
    pg_send,
    pg_recv,
    ch_send,
    ch_recv,
    ch_own,
    e_send,
    e_recv,
    e_own,
    res_send,
    res_recv,
    res_own,
    gx_send,
    gx_recv,
    rg_send,
    rg_recv,
    rg_own,
):
    core = lax.axis_index("pipe")
    md = lax.axis_index("dp")
    mx = lax.axis_index("tensor")
    other = 1 - core
    rows, features = cur.shape
    tokens = nx * rows
    shard_rows = sa.shape[1]
    wide_features = sq.shape[3]
    heads = wide_features // HEAD_DIM
    quarters = features // 256
    slots = nd * CAP
    extras = CAP - MAIN

    def x_peer(step):
        peer = mx + step
        return peer - jnp.where(peer >= nx, nx, 0)

    x_steps = sorted(range(1, nx), key=lambda step: -min(step, nx - step))

    def d_peer(step):
        peer = md + step
        return peer - jnp.where(peer >= nd, nd, 0)

    unit = 5 if (nd - 1) % 5 == 0 else 1

    def each_step(push):
        def some_steps(turn, carry):
            for at in range(unit):
                push(1 + turn * unit + at)
            return carry

        lax.fori_loop(0, (nd - 1) // unit, some_steps, 0)

    def remote(src, dst, send, recv, **where):
        return pltpu.make_async_remote_copy(
            src_ref=src,
            dst_ref=dst,
            send_sem=send,
            recv_sem=recv,
            device_id=where,
            device_id_type=MESH,
        )

    def local(src, dst, sem):
        return pltpu.make_async_copy(src, dst, sem)

    def wait_for(ref, sem):
        pltpu.make_async_copy(ref, ref, sem).wait()

    barrier = pltpu.get_barrier_semaphore()

    def greet(step, carry):
        pl.semaphore_signal(
            barrier, inc=1, device_id={"dp": d_peer(step)}, device_id_type=MESH
        )
        return carry

    lax.fori_loop(1, nd, greet, 0)
    for step in range(1, nx):
        pl.semaphore_signal(
            barrier, inc=1, device_id={"tensor": x_peer(step)}, device_id_type=MESH
        )
    for step in range(nx):
        pl.semaphore_signal(
            barrier,
            inc=1,
            device_id={"pipe": other, "tensor": x_peer(step)},
            device_id_type=MESH,
        )

    mine = pl.ds(md * shard_rows, shard_rows)
    shard_src = (sg, sa.at[0], sm, sa.at[1])
    shard_dst = (
        wg.at[core, mine],
        wa.at[core, 0, mine],
        wm.at[core, :, mine],
        wa.at[core, 1, mine],
    )

    def share_weight(which):
        def push(step):
            remote(
                shard_src[which],
                shard_dst[which],
                w_send.at[which],
                w_recv.at[which],
                dp=d_peer(step),
            ).start()

        local(shard_src[which], shard_dst[which], w_own.at[which]).start()
        each_step(push)

    all_but_one = pl.ds(0, (nd - 1) * shard_rows)

    def arrived_part(which):
        if which == 0:
            return wg.at[0, all_but_one]
        if which == 2:
            return wm.at[0, :, all_but_one]
        return wa.at[0, which // 2, all_but_one]

    def whole_part(which, section):
        if which == 0:
            return wg.at[section]
        if which == 2:
            return wm.at[section]
        return wa.at[section, which // 2]

    def weight_forward(which):
        wait_for(arrived_part(which), w_recv.at[which])
        local(shard_src[which], shard_dst[which], w_own.at[which]).wait()
        remote(
            whole_part(which, core),
            whole_part(which, core),
            wf_send.at[which],
            wf_recv.at[which],
            pipe=other,
        ).start()

    def weight_ready(which):
        wait_for(whole_part(which, 0), wf_recv.at[which])

    def misc_copies():
        return (
            remote(bnd.at[other], bx, m_send.at[0], m_recv.at[0], pipe=other),
            remote(rt_in.at[other], rt.at[core], m_send.at[1], m_recv.at[1], pipe=other),
        )

    def expert_copies():
        return (
            remote(ein, we.at[core, 0], m_send.at[2], m_recv.at[2], pipe=other),
            remote(eout, we.at[core, 1], m_send.at[3], m_recv.at[3], pipe=other),
        )

    def expert_own():
        return (
            local(ein, we.at[core, 0], m_own.at[0]),
            local(eout, we.at[core, 1], m_own.at[1]),
        )

    put_row = lax.broadcasted_iota(jnp.int32, put.shape[1:], 0)
    put_col = lax.broadcasted_iota(jnp.int32, put.shape[1:], 1)
    for c in range(4):
        put[c] = jnp.where(put_col == put_row + c * wide_features, 1.0, 0.0).astype(BF16)

    def attention_shard(j):
        total = nn(so[j], put[0])
        for c in range(3):
            total = total + nn(sq[j, c], put[1 + c])
        sa[j] = total.astype(BF16)

    attention_shard(0)
    count = gains.shape[0]
    pick_row = lax.broadcasted_iota(jnp.int32, (count, 128), 0)
    pick_col = lax.broadcasted_iota(jnp.int32, (count, 128), 1)
    sg[...] = tn(gains[...], jnp.where(pick_row == pick_col, 1.0, 0.0).astype(BF16)).astype(BF16)
    for m in range(MICRO):
        expert = ids[m]
        seats = seat[m]
        place = jnp.where(
            seats < MAIN,
            expert * MAIN + seats,
            nd * MAIN + expert * extras + seats - MAIN,
        )
        rt_in[m] = jnp.concatenate(
            [place.astype(F32), gate[m], jnp.zeros((4, tokens), F32)], axis=0
        )

    pl.semaphore_wait(barrier, (nd - 1) + (nx - 1) + nx)

    @pl.when(core == 0)
    def first_attention():
        share_weight(1)

    for copy in misc_copies():
        copy.start()
    share_weight(0)
    sm[0] = mi[...]
    sm[1] = mo[...]
    attention_shard(1)

    @pl.when(core == 0)
    def first_section():
        share_weight(2)
        share_weight(3)

    rt[core] = rt_in[core]
    row_id = lax.broadcasted_iota(jnp.int32, (nd * 16, nd * extras), 0)
    col_id = lax.broadcasted_iota(jnp.int32, (nd * 16, nd * extras), 1)
    back_row = lax.broadcasted_iota(jnp.int32, (nd * extras, nd * 16), 0)
    back_col = lax.broadcasted_iota(jnp.int32, (nd * extras, nd * 16), 1)
    for q in range(quarters):
        hit = (
            ((row_id >> 4) == (col_id >> 2))
            & (((row_id >> 2) & 3) == q)
            & ((row_id & 3) == (col_id & 3))
        )
        sel[q] = jnp.where(hit, 1.0, 0.0).astype(BF16)
        hit = (
            ((back_col >> 4) == (back_row >> 2))
            & (((back_col >> 2) & 3) == q)
            & ((back_col & 3) == (back_row & 3))
        )
        sel_back[q] = jnp.where(hit, 1.0, 0.0).astype(BF16)
    dgn[...] = jnp.zeros_like(dgn)

    for copy in misc_copies():
        copy.wait()
    place = lax.broadcasted_iota(jnp.int32, (slots, tokens), 0)
    for s in range(2):
        table = rt[s]
        for k in range(2):
            hit = place == table[k : k + 1].astype(jnp.int32)
            pk[s, k] = jnp.where(hit, 1.0, 0.0).astype(BF16)
        gt[s] = jnp.transpose(jnp.concatenate([table] * (tokens // 8), axis=0))

    @pl.when(core == 0)
    def first_input():
        ags[0, 0, 0] = bnd[0].reshape(nx, rows, features)
        ags[1, 1, 3] = bx[...].reshape(nx, rows, features)

    @pl.when(core == 1)
    def second_input():
        ags[0, 0, 0] = bx[...].reshape(nx, rows, features)
        ags[1, 1, 3] = bnd[1].reshape(nx, rows, features)

    cur[...] = ags[0, 0, 0, mx].astype(F32)
    weight_forward(0)
    weight_ready(0)
    for s in range(2):
        turned = jnp.transpose(wg[s].astype(F32))
        gn[s] = turned[:8]

    lane = lax.broadcasted_iota(jnp.int32, (1, wide_features), 1)
    head_masks = [
        jnp.where((lane >= h * HEAD_DIM) & (lane < (h + 1) * HEAD_DIM), 1.0, 0.0).astype(BF16)
        for h in range(heads)
    ]

    def per_head(values):
        return [values * mask for mask in head_masks]

    def norm_parts(stream):
        center = stream - jnp.mean(stream, axis=-1, keepdims=True)
        scale = lax.rsqrt(jnp.mean(center * center, axis=-1, keepdims=True) + EPSILON)
        return center * scale, scale

    def norm_back(s, k, parts, grad_normed):
        normal, scale = parts
        gain_rows = jnp.sum(grad_normed * normal, axis=0, keepdims=True)
        if k == 0:

            @pl.when(s == 1)
            def not_sent_yet():
                dgn[s, k : k + 1, :] = gain_rows

        else:
            dgn[s, k : k + 1, :] = gain_rows
        pulled = grad_normed * gn[s][k : k + 1]
        return scale * (
            pulled
            - jnp.mean(pulled, axis=-1, keepdims=True)
            - normal * jnp.mean(pulled * normal, axis=-1, keepdims=True)
        )

    some = pl.ds(0, nx - 1)

    def all_rows(s, way, k, own_rows, meanwhile=None):
        ags[s, way, k, mx] = own_rows.astype(BF16)
        for step in x_steps:
            remote(
                ags.at[s, way, k, mx],
                ags.at[s, way, k, mx],
                ag_send.at[s, way, k],
                ag_recv.at[s, way, k],
                tensor=x_peer(step),
            ).start()
        if meanwhile is not None:
            meanwhile()
        wait_for(ags.at[s, way, k, some], ag_recv.at[s, way, k])
        return ags[s, way, k].reshape(tokens, features)

    def sum_start(s, way, k, partial_rows):
        rs_out[s, way, k] = partial_rows.astype(BF16).reshape(nx, rows, features)
        for step in x_steps:
            peer = x_peer(step)
            remote(
                rs_out.at[s, way, k, peer],
                rs_in.at[s, way, k, mx],
                rs_send.at[s, way, k],
                rs_recv.at[s, way, k],
                tensor=peer,
            ).start()

    def sum_end(s, way, k):
        wait_for(rs_in.at[s, way, k, some], rs_recv.at[s, way, k])
        total = rs_out[s, way, k, mx].astype(F32)
        for step in range(1, nx):
            total = total + rs_in[s, way, k, x_peer(step)].astype(F32)
        return total

    def slots_start(s, which, values):
        main = values[: nd * MAIN]
        extra = values[nd * MAIN :]
        folded = None
        for q in range(quarters):
            columns = slice(256 * q, 256 * (q + 1))
            a2_out[:, 16 * q : 16 * (q + 1), :] = main[:, columns].reshape(nd, 16, 256)
            term = nn(sel[q], extra[:, columns])
            folded = term if folded is None else folded + term
        a2_out[:, 16 * quarters :, :] = folded.astype(BF16).reshape(nd, 16, 256)

        def push(step):
            peer = d_peer(step)
            remote(
                a2_out.at[peer],
                a2_in.at[s, which, md],
                a2_send.at[0],
                a2_recv.at[s, which],
                dp=peer,
            ).start()

        each_step(push)
        a2_in[s, which, md] = a2_out[md]

    def slots_end(s, which):
        wait_for(a2_in.at[s, which, pl.ds(0, nd - 1)], a2_recv.at[s, which])
        mains = []
        extra = []
        folded = a2_in[s, which, :, 16 * quarters :, :].reshape(nd * 16, 256)
        for q in range(quarters):
            block = a2_in[s, which, :, 16 * q : 16 * (q + 1), :]
            mains.append(block.reshape(nd * 16, 256))
            extra.append(nn(sel_back[q], folded).astype(BF16))
        return jnp.concatenate(
            [jnp.concatenate(mains, axis=1), jnp.concatenate(extra, axis=1)], axis=0
        )

    def slots_sent():
        wait_for(a2_out.at[pl.ds(0, nd - 1)], a2_send.at[0])

    def dback_start(s, grad_rows):
        wide = grad_rows.astype(F32)
        gates = gt[s]
        dback = nn(pk[s, 0], (wide * gates[:, 2:3]).astype(BF16)) + nn(
            pk[s, 1], (wide * gates[:, 3:4]).astype(BF16)
        )
        slots_start(s, 2, dback.astype(BF16))

    def attend(s, j, k):
        stream = cur[...]
        hs[s, k] = stream
        normal, unused = norm_parts(stream)
        if j == 0:

            @pl.when(s != 0)
            def fetch():
                all_rows(s, 0, k, normal * gn[s][k : k + 1])

            normed = ags[s, 0, k].reshape(tokens, features)
        else:
            normed = all_rows(s, 0, k, normal * gn[s][k : k + 1])

        @pl.when(core != s)
        def weights():
            weight_ready(1 + 2 * j)

        projected = nn(normed, wa[s, j])
        query, key, value = [
            projected[:, c * wide_features : (c + 1) * wide_features].astype(BF16)
            for c in range(1, 4)
        ]
        proj[s, j, 0] = query
        proj[s, j, 1] = key
        proj[s, j, 2] = value
        logits = nt(jnp.concatenate(per_head(query), axis=0), key) * (HEAD_DIM**-0.5)
        exponent = jnp.exp(logits - jnp.max(logits, axis=-1, keepdims=True))
        probs = exponent / jnp.sum(exponent, axis=-1, keepdims=True)
        prb[s, j] = probs
        low = probs.astype(BF16)
        mixed = None
        for h, part in enumerate(per_head(value)):
            term = nn(low[h * tokens : (h + 1) * tokens], part)
            mixed = term if mixed is None else mixed + term
        mixed = mixed.astype(BF16)
        mix[s, j] = mixed
        sum_start(s, 0, k, nt(mixed, wa[s, j, :, :wide_features]))

        if j == 1:

            @pl.when((s == 0) & (core == 1))
            def share():
                share_weight(3)

            @pl.when(s == 1)
            def early_end():
                slots_sent()

        cur[...] = stream + sum_end(s, 0, k)

    def feed(s):
        stream = cur[...]
        hs[s, 1] = stream
        normal, unused = norm_parts(stream)

        def meanwhile():
            @pl.when((s == 0) & (core == 0))
            def onward():
                weight_forward(2)

        normed = all_rows(s, 0, 1, normal * gn[s][1:2], meanwhile)

        @pl.when(core != s)
        def weights():
            weight_ready(2)

        pre = nn(normed, wm[s, 0])
        phi = normal_cdf(pre)
        active = (pre * phi).astype(BF16)
        sum_start(s, 0, 1, nt(active, wm[s, 1]))
        act[s] = active
        dgm[s] = gelu_slope(pre, phi)

        @pl.when((s == 0) & (core == 0))
        def onward():
            weight_forward(3)

        @pl.when((s == 0) & (core == 1))
        def share():
            share_weight(1)
            share_weight(2)

        @pl.when(s == 1)
        def early():
            slots_sent()
            dback_start(s, ags[1, 1, 3].reshape(tokens, features))

        cur[...] = stream + sum_end(s, 0, 1)

    def experts(s):
        stream = cur[...]
        hs[s, 3] = stream
        normal, unused = norm_parts(stream)
        normed = all_rows(s, 0, 3, normal * gn[s][3:4])
        slots_start(s, 0, nn(pk[s, 0] + pk[s, 1], normed).astype(BF16))

        @pl.when(s == 0)
        def weights():
            for copy in expert_copies() + expert_own():
                copy.wait()

        sent = slots_end(s, 0)
        pre = nn(sent, we[s, 0])
        phi = normal_cdf(pre)
        active = (pre * phi).astype(BF16)
        partial_rows = nn(active, we[s, 1]).astype(BF16)
        slots_sent()
        slots_start(s, 1, partial_rows)
        arr[s] = sent
        ace[s] = active
        dge[s] = gelu_slope(pre, phi)

    def experts_start(s):
        back = slots_end(s, 1)
        gates = gt[s]
        partial_rows = tn(pk[s, 0], back) * gates[:, 2:3] + tn(pk[s, 1], back) * gates[:, 3:4]
        sum_start(s, 0, 3, partial_rows)

    def experts_end(s):
        return hs[s, 3] + sum_end(s, 0, 3)

    def forward(s, carry):
        cur[...] = cur[...].astype(BF16).astype(F32)
        attend(s, 0, 0)
        feed(s)
        attend(s, 1, 2)
        experts(s)

        @pl.when(s == 0)
        def to_the_next():
            @pl.when(core == 1)
            def onward():
                for which in range(1, 4):
                    weight_forward(which)

            experts_start(s)
            cur[...] = experts_end(s)

        return carry

    def result_copies(buffer, target, start):
        slot = core * nx + mx

        @pl.when(core == target)
        def near():
            copy = local(buffer, res.at[slot], res_own.at[0])
            copy.start() if start else copy.wait()

        @pl.when(core != target)
        def far():
            copy = remote(
                buffer,
                res.at[slot],
                res_send.at[1],
                res_recv.at[0],
                pipe=target,
            )
            copy.start() if start else copy.wait_send()

        for step in range(1, nx):
            copy = remote(
                buffer,
                res.at[slot],
                res_send.at[1 + step],
                res_recv.at[0],
                pipe=target,
                tensor=x_peer(step),
            )
            copy.start() if start else copy.wait_send()

    @pl.when(core == 0)
    def first_weights():
        weight_forward(1)

    for copy in expert_copies() + expert_own():
        copy.start()
    given = ags[0, 0, 0].reshape(tokens, features).astype(F32)
    normal, unused = norm_parts(given)
    xh[...] = normal
    ags[0, 0, 0] = (normal * gn[0][0:1]).astype(BF16).reshape(nx, rows, features)
    lax.fori_loop(0, 2, forward, 0)

    staged = (ga.at[0], gm, ga.at[1])
    partner = (pa.at[0], pm, pa.at[1])
    landing = (ra.at[0], rm, ra.at[1])

    def some_rows(which, part):
        return staged[which].at[:, part] if which == 1 else staged[which].at[part]

    def chunk(which, owner):
        return some_rows(which, pl.ds(owner * shard_rows, shard_rows))

    def staged_wait(which, section):
        @pl.when(core == section)
        def owned():
            wait_for(some_rows(which, all_but_one), ch_send.at[which])
            local(chunk(which, md), landing[which].at[md], ch_own.at[which]).wait()

        @pl.when(core != section)
        def lent():
            wait_for(staged[which], pg_send.at[which])

    def lend(which, section):
        @pl.when(core != section)
        def lent():
            remote(
                staged[which],
                partner[which],
                pg_send.at[which],
                pg_recv.at[which],
                pipe=other,
            ).start()

    def combine(which, section):
        @pl.when(core == section)
        def owned():
            wait_for(partner[which], pg_recv.at[which])
            staged[which][...] = (
                staged[which][...].astype(F32) + partner[which][...].astype(F32)
            ).astype(BF16)

            def push(step):
                peer = d_peer(step)
                remote(
                    chunk(which, peer),
                    landing[which].at[md],
                    ch_send.at[which],
                    ch_recv.at[which],
                    dp=peer,
                ).start()

            each_step(push)
            local(chunk(which, md), landing[which].at[md], ch_own.at[which]).start()

    def gains_start():
        place_here = core * nx + mx
        for section in range(2):

            @pl.when(core == section)
            def near():
                gx[place_here] = dgn[section]

            @pl.when(core != section)
            def far():
                remote(
                    dgn.at[section],
                    gx.at[place_here],
                    gx_send.at[section, 0],
                    gx_recv.at[0],
                    pipe=section,
                ).start()

            for step in range(1, nx):
                remote(
                    dgn.at[section],
                    gx.at[place_here],
                    gx_send.at[section, step],
                    gx_recv.at[0],
                    pipe=section,
                    tensor=x_peer(step),
                ).start()

    def gains_push():
        wait_for(gx.at[pl.ds(0, 2 * nx - 1)], gx_recv.at[0])
        gains_total = gx[0]
        for source in range(1, 2 * nx):
            gains_total = gains_total + gx[source]
        gs[...] = gains_total

        def push_gains(step):
            remote(gs, rg.at[md], rg_send.at[0], rg_recv.at[0], dp=d_peer(step)).start()

        each_step(push_gains)
        local(gs, rg.at[md], rg_own.at[0]).start()

    def experts_back(s):
        grad = cur[...]

        @pl.when(s == 0)
        def later():
            wide = all_rows(s, 1, 3, grad, slots_sent)
            dback_start(s, wide)
            combine(0, 1)

        dback = slots_end(s, 2)
        dpre = (nt(dback, we[s, 1]) * dge[s]).astype(BF16)
        dsent = nt(dpre, we[s, 0]).astype(BF16)
        slots_sent()
        slots_start(s, 3, dsent)

        @pl.when(s == 1)
        def last_result_start():
            experts_start(s)

        eg[0] = tn(arr[s], dpre).astype(BF16)
        eg[1] = tn(ace[s], dback).astype(BF16)

        @pl.when(core == s)
        def keep():
            local(eg.at[0], ei_own, e_own.at[0]).start()
            local(eg.at[1], eo_own, e_own.at[1]).start()

        @pl.when(core != s)
        def give():
            remote(eg.at[0], ei_far, e_send.at[0], e_recv.at[0], pipe=other).start()
            remote(eg.at[1], eo_far, e_send.at[1], e_recv.at[1], pipe=other).start()

        @pl.when(s == 1)
        def last_result_end():
            hout[...] = experts_end(s)
            result_copies(hout, 1, True)

        parts = norm_parts(hs[s, 3])
        dsent = slots_end(s, 3)
        sum_start(s, 1, 3, tn(pk[s, 0] + pk[s, 1], dsent))
        cur[...] = grad + norm_back(s, 3, parts, sum_end(s, 1, 3))

    def attend_back(s, j, k):
        grad = cur[...]
        dz = all_rows(s, 1, k, grad, (lambda: combine(1, s)) if j == 0 else None)
        dmixed = nn(dz, wa[s, j, :, :wide_features]).astype(BF16)
        query, key, value = [proj[s, j, c] for c in range(3)]
        probs = prb[s, j]
        dmixed_heads = jnp.concatenate(per_head(dmixed), axis=0)
        dprobs = nt(dmixed_heads, value)
        dscores = probs * (dprobs - jnp.sum(probs * dprobs, axis=-1, keepdims=True))
        dscores = dscores.astype(BF16)
        dvalue = tn(probs.astype(BF16), dmixed_heads)
        dkey = tn(dscores, jnp.concatenate(per_head(query), axis=0)) * (HEAD_DIM**-0.5)
        dquery = None
        for h, part in enumerate(per_head(key)):
            term = nn(dscores[h * tokens : (h + 1) * tokens], part)
            dquery = term if dquery is None else dquery + term
        dquery = dquery * (HEAD_DIM**-0.5)
        dproj = [d.astype(BF16) for d in (dquery, dkey, dvalue)]
        placed = None
        for c in range(3):
            term = nn(dproj[c], put[1 + c])
            placed = term if placed is None else placed + term
        placed = placed.astype(BF16)
        partial_rows = nt(placed, wa[s, j])

        def weight_grads():
            normed = ags[s, 0, k].reshape(tokens, features)
            mixed = nn(mix[s, j], put[0]).astype(BF16)
            ga[j] = tn(
                jnp.concatenate([normed, dz], axis=0), jnp.concatenate([placed, mixed], axis=0)
            ).astype(BF16)
            lend(2 * j, s)

        if j == 0:

            @pl.when(s == 0)
            def last_of_all():
                dgn[0, 0:1, :] = jnp.sum(partial_rows * xh[...], axis=0, keepdims=True)
                gains_start()
                staged_wait(0, 1)
                weight_grads()

            sum_start(s, 1, k, partial_rows)

            @pl.when(s == 1)
            def not_last():
                weight_grads()

            @pl.when(s == 0)
            def last_onward():
                gains_push()
                combine(0, 0)

        else:
            sum_start(s, 1, k, partial_rows)

            @pl.when(s == 0)
            def free():
                staged_wait(2, 1)

            weight_grads()

        parts = norm_parts(hs[s, k])
        cur[...] = grad + norm_back(s, k, parts, sum_end(s, 1, k))

    def feed_back(s):
        grad = cur[...]
        dout = all_rows(s, 1, 1, grad, lambda: combine(2, s))
        dpre = (nn(dout, wm[s, 1]) * dgm[s]).astype(BF16)
        sum_start(s, 1, 1, nt(dpre, wm[s, 0]))

        @pl.when(s == 0)
        def free():
            staged_wait(1, 1)

        normed = ags[s, 0, 1].reshape(tokens, features)
        gm[0] = tn(normed, dpre).astype(BF16)
        gm[1] = tn(dout, act[s]).astype(BF16)
        lend(1, s)
        parts = norm_parts(hs[s, 1])
        cur[...] = grad + norm_back(s, 1, parts, sum_end(s, 1, 1))

    def expert_grads_wait(s):
        @pl.when(core == s)
        def keep():
            local(eg.at[0], ei_own, e_own.at[0]).wait()
            local(eg.at[1], eo_own, e_own.at[1]).wait()

        @pl.when(core != s)
        def give():
            wait_for(eg.at[0], e_send.at[0])
            wait_for(eg.at[1], e_send.at[1])

    def backward(turn, carry):
        s = 1 - turn
        cur[...] = cur[...].astype(BF16).astype(F32)
        experts_back(s)
        attend_back(s, 1, 2)
        feed_back(s)
        attend_back(s, 0, 0)
        expert_grads_wait(s)
        return carry

    cur[...] = ags[1, 1, 3, mx].astype(F32)
    lax.fori_loop(0, 2, backward, 0)
    gout[...] = cur[...]
    result_copies(hout, 1, False)
    result_copies(gout, 0, True)

    slots_sent()
    for s in range(2):
        for way in range(2):
            for k in range(4):
                wait_for(rs_out.at[s, way, k, some], rs_send.at[s, way, k])
                if (s, way, k) not in ((0, 0, 0), (1, 1, 3)):
                    wait_for(ags.at[s, way, k, some], ag_send.at[s, way, k])
    for section in range(2):

        @pl.when(core != section)
        def far_end():
            wait_for(dgn.at[section], gx_send.at[section, 0])

        for step in range(1, nx):
            wait_for(dgn.at[section], gx_send.at[section, step])
    for which in range(4):
        wait_for(whole_part(which, 0), wf_send.at[which])
        wait_for(arrived_part(which), w_send.at[which])
    result_copies(gout, 0, False)
    wait_for(res.at[pl.ds(0, 2 * nx - 1)], res_recv.at[0])
    def over_sources(parts):
        total = parts[0].astype(F32)
        for source in range(1, nd):
            total = total + parts[source].astype(F32)
        return total

    def landed(which):
        staged_wait(which, 0)
        wait_for(landing[which].at[pl.ds(0, nd - 1)], ch_recv.at[which])

    landed(2)
    dense_sum[1] = over_sources(ra[1])
    landed(1)
    for c in range(2):
        feed_sum[c] = over_sources([rm[source, c] for source in range(nd)])
    wait_for(ei_far, e_recv.at[0])
    wait_for(eo_far, e_recv.at[1])
    wait_for(rg.at[pl.ds(0, nd - 1)], rg_recv.at[0])
    wait_for(rg.at[pl.ds(0, nd - 1)], rg_send.at[0])
    local(gs, rg.at[md], rg_own.at[0]).wait()
    gains_sum[...] = over_sources(rg)
    landed(0)
    dense_sum[0] = over_sources(ra[0])


def shards(
    nx,
    nd,
    boundary,
    norm_gains,
    attn_qkv,
    attn_out,
    mlp_in,
    mlp_out,
    expert_in,
    expert_out,
    expert_ids,
    expert_slots,
    gate_weights,
):
    tokens, features = boundary.shape[3:]
    rows = tokens // nx
    shard_rows = features // nd
    wide = attn_qkv.shape[4]
    units = mlp_in.shape[2]
    hidden = expert_in.shape[3]
    slots = nd * CAP
    quarters = features // 256
    slab = 16 * quarters + 16
    heads = wide // HEAD_DIM

    vmem = pl.BlockSpec(memory_space=pltpu.VMEM)
    hbm = pl.BlockSpec(memory_space=pl.ANY)
    dma = pltpu.SemaphoreType.DMA
    scratch = [
        pltpu.VMEM((2, nd, shard_rows, 4 * wide), BF16),
        pltpu.VMEM((nd, 2, shard_rows, units), BF16),
        pltpu.VMEM((nd, 8, features), F32),
        pltpu.VMEM((MICRO, 8, tokens), F32),
        pltpu.VMEM((shard_rows, 128), BF16),
        pltpu.VMEM((2, shard_rows, 4 * wide), BF16),
        pltpu.VMEM((2, shard_rows, units), BF16),
        pltpu.VMEM((4, wide, 4 * wide), BF16),
        pltpu.VMEM((tokens, features), F32),
        pltpu.VMEM((2, 2, features, 4 * wide), BF16),
        pltpu.VMEM((2, 2, features, units), BF16),
        pltpu.VMEM((2, 2, features, hidden), BF16),
        pltpu.VMEM((2, features, 128), BF16),
        pltpu.VMEM((2, 8, features), F32),
        pltpu.VMEM((2, 8, tokens), F32),
        pltpu.VMEM((2, tokens, tokens), F32),
        pltpu.VMEM((tokens, features), BF16),
        pltpu.VMEM((quarters, nd * 16, nd * (CAP - MAIN)), BF16),
        pltpu.VMEM((quarters, nd * (CAP - MAIN), nd * 16), BF16),
        pltpu.VMEM((2, 2, slots, tokens), BF16),
        pltpu.VMEM((2, 4, rows, features), F32),
        pltpu.VMEM((2, 2, 4, nx, rows, features), BF16),
        pltpu.VMEM((2, 2, 4, nx, rows, features), BF16),
        pltpu.VMEM((2, 2, 4, nx, rows, features), BF16),
        pltpu.VMEM((nd, slab, 256), BF16),
        pltpu.VMEM((2, 4, nd, slab, 256), BF16),
        pltpu.VMEM((2, 2, 3, tokens, wide), BF16),
        pltpu.VMEM((2, 2, tokens, wide), BF16),
        pltpu.VMEM((2, 2, heads * tokens, tokens), F32),
        pltpu.VMEM((2, tokens, units), F32),
        pltpu.VMEM((2, tokens, units), BF16),
        pltpu.VMEM((2, slots, features), BF16),
        pltpu.VMEM((2, slots, hidden), F32),
        pltpu.VMEM((2, slots, hidden), BF16),
        pltpu.VMEM((2, features, 4 * wide), BF16),
        pltpu.VMEM((2, features, units), BF16),
        pltpu.VMEM((2, features, 4 * wide), BF16),
        pltpu.VMEM((2, features, units), BF16),
        pltpu.VMEM((2, features, hidden), BF16),
        pltpu.VMEM((2, 8, features), F32),
        pltpu.VMEM((2 * nx, 8, features), F32),
        pltpu.VMEM((8, features), F32),
        pltpu.VMEM((rows, features), F32),
        pltpu.VMEM((rows, features), F32),
        pltpu.VMEM((rows, features), F32),
        dma((2, 2, 4)),
        dma((2, 2, 4)),
        dma((2, 2, 4)),
        dma((2, 2, 4)),
        dma((1,)),
        dma((2, 4)),
        dma((4,)),
        dma((4,)),
        dma((4,)),
        dma((4,)),
        dma((4,)),
        dma((4,)),
        dma((4,)),
        dma((2,)),
        dma((3,)),
        dma((3,)),
        dma((3,)),
        dma((3,)),
        dma((3,)),
        dma((2,)),
        dma((2,)),
        dma((2,)),
        dma((1 + nx,)),
        dma((1,)),
        dma((1,)),
        dma((2, nx)),
        dma((1,)),
        dma((1,)),
        dma((1,)),
        dma((1,)),
    ]
    res, dense, feed, gains, ei_own, eo_own, ei_far, eo_far = pl.pallas_call(
        functools.partial(kernel, nx, nd),
        out_shape=(
            jax.ShapeDtypeStruct((2 * nx, rows, features), F32),
            jax.ShapeDtypeStruct((2, shard_rows, 4 * wide), F32),
            jax.ShapeDtypeStruct((2, shard_rows, units), F32),
            jax.ShapeDtypeStruct((8, features), F32),
            jax.ShapeDtypeStruct((features, hidden), BF16),
            jax.ShapeDtypeStruct((hidden, features), BF16),
            jax.ShapeDtypeStruct((features, hidden), BF16),
            jax.ShapeDtypeStruct((hidden, features), BF16),
        ),
        in_specs=[vmem] * 9 + [hbm] * 2,
        out_specs=(hbm,) + (vmem,) * 3 + (hbm,) * 4,
        scratch_shapes=scratch,
        compiler_params=pltpu.CompilerParams(
            collective_id=0, has_side_effects=True, vmem_limit_bytes=VMEM_LIMIT
        ),
    )(
        boundary[0, :, 0],
        jnp.swapaxes(expert_ids[0, :, 0], 1, 2),
        jnp.swapaxes(expert_slots[0, :, 0], 1, 2),
        jnp.swapaxes(gate_weights[0, :, 0], 1, 2),
        attn_qkv[0],
        jnp.swapaxes(attn_out[0], 1, 2),
        mlp_in[0],
        mlp_out[0].T,
        norm_gains[0],
        expert_in[0, 0],
        expert_out[0, 0],
    )

    gains = gains[: norm_gains.shape[1]]
    gains = lax.dynamic_slice_in_dim(gains, lax.axis_index("dp") * shard_rows, shard_rows, 1)
    qkv = dense[:, :, wide:].reshape(2, shard_rows, 3, wide)
    return (
        res.reshape(1, MICRO, 1, tokens, features),
        gains[None],
        jnp.swapaxes(qkv, 1, 2)[None],
        jnp.swapaxes(dense[:, :, :wide], 1, 2)[None],
        feed[0][None],
        feed[1].T[None],
        (ei_own.astype(F32) + ei_far.astype(F32))[None, None],
        (eo_own.astype(F32) + eo_far.astype(F32))[None, None],
    )


VMEM_LIMIT = 62 * 1024 * 1024


def solution(mesh):
    in_specs = (
        P("pipe", None, "dp", None, None),
        P("pipe", None, "dp"),
        P("pipe", None, None, "dp", "tensor"),
        P("pipe", None, "tensor", "dp"),
        P("pipe", "dp", "tensor"),
        P("pipe", "tensor", "dp"),
        P("pipe", "dp", None, "tensor"),
        P("pipe", "dp", "tensor", None),
        P("pipe", None, "dp", None, None),
        P("pipe", None, "dp", None, None),
        P("pipe", None, "dp", None, None),
    )
    out_specs = (
        P("pipe", None, "dp", None, None),
        P("pipe", None, "dp"),
        P("pipe", None, None, "dp", "tensor"),
        P("pipe", None, "tensor", "dp"),
        P("pipe", "dp", "tensor"),
        P("pipe", "tensor", "dp"),
        P("pipe", "dp", None, "tensor"),
        P("pipe", "dp", "tensor", None),
    )
    return jax.shard_map(
        functools.partial(shards, mesh.shape["tensor"], mesh.shape["dp"]),
        mesh=mesh,
        in_specs=in_specs,
        out_specs=out_specs,
        check_vma=False,
    )
```

```python
import functools

import jax
import jax.numpy as jnp
from jax import lax
from jax.experimental import pallas as pl
from jax.experimental.pallas import tpu as pltpu
from jax.sharding import PartitionSpec as P

MESH = pl.DeviceIdType.MESH
BF16 = jnp.bfloat16
F32 = jnp.float32
HEAD_DIM = 64
EPSILON = 1e-06
CAP = 20
MAIN = 16
MICRO = 2


def dims(lhs, rhs, left_dim, right_dim):
    return lax.dot_general(
        lhs, rhs, (((left_dim,), (right_dim,)), ((), ())), preferred_element_type=F32
    )


def nn(lhs, rhs):
    return dims(lhs, rhs, 1, 0)


def nt(lhs, rhs):
    return dims(lhs, rhs, 1, 1)


def tn(lhs, rhs):
    return dims(lhs, rhs, 0, 0)


def normal_cdf(pre):
    return 0.5 * (1.0 + lax.erf(pre * 0.7071067811865476))


def gelu_slope(pre, phi):
    return phi + pre * (0.3989422804014327 * jnp.exp(-0.5 * pre * pre))


def kernel(
    nx,
    nd,
    bnd,
    ids,
    seat,
    gate,
    sq,
    so,
    mi,
    mo,
    gains,
    ein,
    eout,
    res,
    dense_sum,
    feed_sum,
    gains_sum,
    ei_own,
    eo_own,
    ei_far,
    eo_far,
    ra,
    rm,
    rg,
    rt_in,
    sg,
    sa,
    sm,
    put,
    xh,
    wa,
    wm,
    we,
    wg,
    gn,
    rt,
    gt,
    bx,
    sel,
    sel_back,
    pk,
    hs,
    ags,
    rs_out,
    rs_in,
    a2_out,
    a2_in,
    proj,
    mix,
    prb,
    dgm,
    act,
    arr,
    dge,
    ace,
    ga,
    gm,
    pa,
    pm,
    eg,
    dgn,
    gx,
    gs,
    cur,
    hout,
    gout,
    ag_send,
    ag_recv,
    rs_send,
    rs_recv,
    a2_send,
    a2_recv,
    w_send,
    w_recv,
    w_own,
    wf_send,
    wf_recv,
    m_send,
    m_recv,
    m_own,
    pg_send,
    pg_recv,
    ch_send,
    ch_recv,
    ch_own,
    e_send,
    e_recv,
    e_own,
    res_send,
    res_recv,
    res_own,
    gx_send,
    gx_recv,
    rg_send,
    rg_recv,
    rg_own,
):
    core = lax.axis_index("pipe")
    md = lax.axis_index("dp")
    mx = lax.axis_index("tensor")
    other = 1 - core
    rows, features = cur.shape
    tokens = nx * rows
    shard_rows = sa.shape[1]
    wide_features = sq.shape[3]
    heads = wide_features // HEAD_DIM
    quarters = features // 256
    slots = nd * CAP
    extras = CAP - MAIN

    def x_peer(step):
        peer = mx + step
        return peer - jnp.where(peer >= nx, nx, 0)

    x_steps = sorted(range(1, nx), key=lambda step: -min(step, nx - step))

    def d_peer(step):
        peer = md + step
        return peer - jnp.where(peer >= nd, nd, 0)

    unit = 5 if (nd - 1) % 5 == 0 else 1

    def each_step(push):
        def some_steps(turn, carry):
            for at in range(unit):
                push(1 + turn * unit + at)
            return carry

        lax.fori_loop(0, (nd - 1) // unit, some_steps, 0)

    def remote(src, dst, send, recv, **where):
        return pltpu.make_async_remote_copy(
            src_ref=src,
            dst_ref=dst,
            send_sem=send,
            recv_sem=recv,
            device_id=where,
            device_id_type=MESH,
        )

    def local(src, dst, sem):
        return pltpu.make_async_copy(src, dst, sem)

    def wait_for(ref, sem):
        pltpu.make_async_copy(ref, ref, sem).wait()

    barrier = pltpu.get_barrier_semaphore()

    def greet(step):
        pl.semaphore_signal(
            barrier, inc=1, device_id={"dp": d_peer(step)}, device_id_type=MESH
        )

    each_step(greet)
    for step in range(1, nx):
        pl.semaphore_signal(
            barrier, inc=1, device_id={"tensor": x_peer(step)}, device_id_type=MESH
        )
    for step in range(nx):
        pl.semaphore_signal(
            barrier,
            inc=1,
            device_id={"pipe": other, "tensor": x_peer(step)},
            device_id_type=MESH,
        )

    mine = pl.ds(md * shard_rows, shard_rows)
    shard_src = (sg, sa.at[0], sm, sa.at[1])
    shard_dst = (
        wg.at[core, mine],
        wa.at[core, 0, mine],
        wm.at[core, :, mine],
        wa.at[core, 1, mine],
    )

    def share_weight(which):
        def push(step):
            remote(
                shard_src[which],
                shard_dst[which],
                w_send.at[which],
                w_recv.at[which],
                dp=d_peer(step),
            ).start()

        local(shard_src[which], shard_dst[which], w_own.at[which]).start()
        each_step(push)

    all_but_one = pl.ds(0, (nd - 1) * shard_rows)

    def arrived_part(which):
        if which == 0:
            return wg.at[0, all_but_one]
        if which == 2:
            return wm.at[0, :, all_but_one]
        return wa.at[0, which // 2, all_but_one]

    def whole_part(which, section):
        if which == 0:
            return wg.at[section]
        if which == 2:
            return wm.at[section]
        return wa.at[section, which // 2]

    def weight_forward(which):
        wait_for(arrived_part(which), w_recv.at[which])
        local(shard_src[which], shard_dst[which], w_own.at[which]).wait()
        remote(
            whole_part(which, core),
            whole_part(which, core),
            wf_send.at[which],
            wf_recv.at[which],
            pipe=other,
        ).start()

    def weight_ready(which):
        wait_for(whole_part(which, 0), wf_recv.at[which])

    def misc_copies():
        return (
            remote(bnd.at[other], bx, m_send.at[0], m_recv.at[0], pipe=other),
            remote(rt_in.at[other], rt.at[core], m_send.at[1], m_recv.at[1], pipe=other),
        )

    def expert_copies():
        return (
            remote(ein, we.at[core, 0], m_send.at[2], m_recv.at[2], pipe=other),
            remote(eout, we.at[core, 1], m_send.at[3], m_recv.at[3], pipe=other),
        )

    def expert_own():
        return (
            local(ein, we.at[core, 0], m_own.at[0]),
            local(eout, we.at[core, 1], m_own.at[1]),
        )

    put_row = lax.broadcasted_iota(jnp.int32, put.shape[1:], 0)
    put_col = lax.broadcasted_iota(jnp.int32, put.shape[1:], 1)
    for c in range(4):
        put[c] = jnp.where(put_col == put_row + c * wide_features, 1.0, 0.0).astype(BF16)

    def attention_shard(j):
        total = nn(so[j], put[0])
        for c in range(3):
            total = total + nn(sq[j, c], put[1 + c])
        sa[j] = total.astype(BF16)

    attention_shard(0)
    count = gains.shape[0]
    pick_row = lax.broadcasted_iota(jnp.int32, (count, 128), 0)
    pick_col = lax.broadcasted_iota(jnp.int32, (count, 128), 1)
    sg[...] = tn(gains[...], jnp.where(pick_row == pick_col, 1.0, 0.0).astype(BF16)).astype(BF16)
    for m in range(MICRO):
        expert = ids[m]
        seats = seat[m]
        place = jnp.where(
            seats < MAIN,
            expert * MAIN + seats,
            nd * MAIN + expert * extras + seats - MAIN,
        )
        rt_in[m] = jnp.concatenate(
            [place.astype(F32), gate[m], jnp.zeros((4, tokens), F32)], axis=0
        )

    pl.semaphore_wait(barrier, (nd - 1) + (nx - 1) + nx)

    @pl.when(core == 0)
    def first_attention():
        share_weight(1)

    for copy in misc_copies():
        copy.start()
    share_weight(0)
    sm[0] = mi[...]
    sm[1] = mo[...]
    attention_shard(1)

    @pl.when(core == 0)
    def first_section():
        share_weight(2)
        share_weight(3)

    rt[core] = rt_in[core]
    row_id = lax.broadcasted_iota(jnp.int32, (nd * 16, nd * extras), 0)
    col_id = lax.broadcasted_iota(jnp.int32, (nd * 16, nd * extras), 1)
    back_row = lax.broadcasted_iota(jnp.int32, (nd * extras, nd * 16), 0)
    back_col = lax.broadcasted_iota(jnp.int32, (nd * extras, nd * 16), 1)
    for q in range(quarters):
        hit = (
            ((row_id >> 4) == (col_id >> 2))
            & (((row_id >> 2) & 3) == q)
            & ((row_id & 3) == (col_id & 3))
        )
        sel[q] = jnp.where(hit, 1.0, 0.0).astype(BF16)
        hit = (
            ((back_col >> 4) == (back_row >> 2))
            & (((back_col >> 2) & 3) == q)
            & ((back_col & 3) == (back_row & 3))
        )
        sel_back[q] = jnp.where(hit, 1.0, 0.0).astype(BF16)
    dgn[...] = jnp.zeros_like(dgn)

    for copy in misc_copies():
        copy.wait()
    place = lax.broadcasted_iota(jnp.int32, (slots, tokens), 0)
    for s in range(2):
        table = rt[s]
        for k in range(2):
            hit = place == table[k : k + 1].astype(jnp.int32)
            pk[s, k] = jnp.where(hit, 1.0, 0.0).astype(BF16)
        gt[s] = jnp.transpose(jnp.concatenate([table] * (tokens // 8), axis=0))

    @pl.when(core == 0)
    def first_input():
        ags[0, 0, 0] = bnd[0].reshape(nx, rows, features)
        ags[1, 1, 3] = bx[...].reshape(nx, rows, features)

    @pl.when(core == 1)
    def second_input():
        ags[0, 0, 0] = bx[...].reshape(nx, rows, features)
        ags[1, 1, 3] = bnd[1].reshape(nx, rows, features)

    cur[...] = ags[0, 0, 0, mx].astype(F32)
    weight_forward(0)
    weight_ready(0)
    for s in range(2):
        turned = jnp.transpose(wg[s].astype(F32))
        gn[s] = turned[:8]

    lane = lax.broadcasted_iota(jnp.int32, (1, wide_features), 1)
    head_masks = [
        jnp.where((lane >= h * HEAD_DIM) & (lane < (h + 1) * HEAD_DIM), 1.0, 0.0).astype(BF16)
        for h in range(heads)
    ]

    def per_head(values):
        return [values * mask for mask in head_masks]

    def norm_parts(stream):
        center = stream - jnp.mean(stream, axis=-1, keepdims=True)
        scale = lax.rsqrt(jnp.mean(center * center, axis=-1, keepdims=True) + EPSILON)
        return center * scale, scale

    def norm_back(s, k, parts, grad_normed):
        normal, scale = parts
        gain_rows = jnp.sum(grad_normed * normal, axis=0, keepdims=True)
        if k == 0:

            @pl.when(s == 1)
            def not_sent_yet():
                dgn[s, k : k + 1, :] = gain_rows

        else:
            dgn[s, k : k + 1, :] = gain_rows
        pulled = grad_normed * gn[s][k : k + 1]
        return scale * (
            pulled
            - jnp.mean(pulled, axis=-1, keepdims=True)
            - normal * jnp.mean(pulled * normal, axis=-1, keepdims=True)
        )

    some = pl.ds(0, nx - 1)

    def all_rows(s, way, k, own_rows, meanwhile=None):
        ags[s, way, k, mx] = own_rows.astype(BF16)
        for step in x_steps:
            remote(
                ags.at[s, way, k, mx],
                ags.at[s, way, k, mx],
                ag_send.at[s, way, k],
                ag_recv.at[s, way, k],
                tensor=x_peer(step),
            ).start()
        if meanwhile is not None:
            meanwhile()
        wait_for(ags.at[s, way, k, some], ag_recv.at[s, way, k])
        return ags[s, way, k].reshape(tokens, features)

    def sum_start(s, way, k, partial_rows):
        rs_out[s, way, k] = partial_rows.astype(BF16).reshape(nx, rows, features)
        for step in x_steps:
            peer = x_peer(step)
            remote(
                rs_out.at[s, way, k, peer],
                rs_in.at[s, way, k, mx],
                rs_send.at[s, way, k],
                rs_recv.at[s, way, k],
                tensor=peer,
            ).start()

    def sum_end(s, way, k):
        wait_for(rs_in.at[s, way, k, some], rs_recv.at[s, way, k])
        total = rs_out[s, way, k, mx].astype(F32)
        for step in range(1, nx):
            total = total + rs_in[s, way, k, x_peer(step)].astype(F32)
        return total

    def slots_start(s, which, values):
        main = values[: nd * MAIN]
        extra = values[nd * MAIN :]
        folded = None
        for q in range(quarters):
            columns = slice(256 * q, 256 * (q + 1))
            a2_out[:, 16 * q : 16 * (q + 1), :] = main[:, columns].reshape(nd, 16, 256)
            term = nn(sel[q], extra[:, columns])
            folded = term if folded is None else folded + term
        a2_out[:, 16 * quarters :, :] = folded.astype(BF16).reshape(nd, 16, 256)

        def push(step):
            peer = d_peer(step)
            remote(
                a2_out.at[peer],
                a2_in.at[s, which, md],
                a2_send.at[0],
                a2_recv.at[s, which],
                dp=peer,
            ).start()

        each_step(push)
        a2_in[s, which, md] = a2_out[md]

    def slots_end(s, which):
        wait_for(a2_in.at[s, which, pl.ds(0, nd - 1)], a2_recv.at[s, which])
        mains = []
        extra = []
        folded = a2_in[s, which, :, 16 * quarters :, :].reshape(nd * 16, 256)
        for q in range(quarters):
            block = a2_in[s, which, :, 16 * q : 16 * (q + 1), :]
            mains.append(block.reshape(nd * 16, 256))
            extra.append(nn(sel_back[q], folded).astype(BF16))
        return jnp.concatenate(
            [jnp.concatenate(mains, axis=1), jnp.concatenate(extra, axis=1)], axis=0
        )

    def slots_sent():
        wait_for(a2_out.at[pl.ds(0, nd - 1)], a2_send.at[0])

    def dback_start(s, grad_rows):
        wide = grad_rows.astype(F32)
        gates = gt[s]
        weighted = [(wide * gates[:, c : c + 1]).astype(BF16) for c in (2, 3)]
        dback = nn(
            jnp.concatenate([pk[s, 0], pk[s, 1]], axis=1), jnp.concatenate(weighted, axis=0)
        )
        slots_start(s, 2, dback.astype(BF16))

    def attend(s, j, k):
        stream = cur[...]
        hs[s, k] = stream
        normal, unused = norm_parts(stream)
        if j == 0:

            @pl.when(s != 0)
            def fetch():
                all_rows(s, 0, k, normal * gn[s][k : k + 1])

            normed = ags[s, 0, k].reshape(tokens, features)
        else:
            normed = all_rows(s, 0, k, normal * gn[s][k : k + 1])

        @pl.when(core != s)
        def weights():
            weight_ready(1 + 2 * j)

        projected = nn(normed, wa[s, j])
        query, key, value = [
            projected[:, c * wide_features : (c + 1) * wide_features].astype(BF16)
            for c in range(1, 4)
        ]
        proj[s, j, 0] = query
        proj[s, j, 1] = key
        proj[s, j, 2] = value
        logits = nt(jnp.concatenate(per_head(query), axis=0), key) * (HEAD_DIM**-0.5)
        exponent = jnp.exp(logits - jnp.max(logits, axis=-1, keepdims=True))
        probs = exponent / jnp.sum(exponent, axis=-1, keepdims=True)
        prb[s, j] = probs
        low = probs.astype(BF16)
        mixed = None
        for h, part in enumerate(per_head(value)):
            term = nn(low[h * tokens : (h + 1) * tokens], part)
            mixed = term if mixed is None else mixed + term
        mixed = mixed.astype(BF16)
        mix[s, j] = mixed
        sum_start(s, 0, k, nt(mixed, wa[s, j, :, :wide_features]))

        if j == 1:

            @pl.when((s == 0) & (core == 1))
            def share():
                share_weight(3)

            @pl.when(s == 1)
            def early_end():
                slots_sent()

        cur[...] = stream + sum_end(s, 0, k)

    def feed(s):
        stream = cur[...]
        hs[s, 1] = stream
        normal, unused = norm_parts(stream)

        def meanwhile():
            @pl.when((s == 0) & (core == 0))
            def onward():
                weight_forward(2)

        normed = all_rows(s, 0, 1, normal * gn[s][1:2], meanwhile)

        @pl.when(core != s)
        def weights():
            weight_ready(2)

        pre = nn(normed, wm[s, 0])
        phi = normal_cdf(pre)
        active = (pre * phi).astype(BF16)
        sum_start(s, 0, 1, nt(active, wm[s, 1]))
        act[s] = active
        dgm[s] = gelu_slope(pre, phi)

        @pl.when((s == 0) & (core == 0))
        def onward():
            weight_forward(3)

        @pl.when((s == 0) & (core == 1))
        def share():
            share_weight(1)
            share_weight(2)

        @pl.when(s == 1)
        def early():
            slots_sent()
            dback_start(s, ags[1, 1, 3].reshape(tokens, features))

        cur[...] = stream + sum_end(s, 0, 1)

    def experts(s):
        stream = cur[...]
        hs[s, 3] = stream
        normal, unused = norm_parts(stream)
        normed = all_rows(s, 0, 3, normal * gn[s][3:4])
        slots_start(s, 0, nn(pk[s, 0] + pk[s, 1], normed).astype(BF16))

        @pl.when(s == 0)
        def weights():
            for copy in expert_copies() + expert_own():
                copy.wait()

        sent = slots_end(s, 0)
        pre = nn(sent, we[s, 0])
        phi = normal_cdf(pre)
        active = (pre * phi).astype(BF16)
        partial_rows = nn(active, we[s, 1]).astype(BF16)
        slots_sent()
        slots_start(s, 1, partial_rows)
        arr[s] = sent
        ace[s] = active
        dge[s] = gelu_slope(pre, phi)

    def experts_start(s):
        back = slots_end(s, 1)
        gates = gt[s]
        partial_rows = tn(pk[s, 0], back) * gates[:, 2:3] + tn(pk[s, 1], back) * gates[:, 3:4]
        sum_start(s, 0, 3, partial_rows)

    def experts_end(s):
        return hs[s, 3] + sum_end(s, 0, 3)

    def forward(s, carry):
        cur[...] = cur[...].astype(BF16).astype(F32)
        attend(s, 0, 0)
        feed(s)
        attend(s, 1, 2)
        experts(s)

        @pl.when(s == 0)
        def to_the_next():
            @pl.when(core == 1)
            def onward():
                for which in range(1, 4):
                    weight_forward(which)

            experts_start(s)
            cur[...] = experts_end(s)

        return carry

    def result_copies(buffer, target, start):
        slot = core * nx + mx

        @pl.when(core == target)
        def near():
            copy = local(buffer, res.at[slot], res_own.at[0])
            copy.start() if start else copy.wait()

        @pl.when(core != target)
        def far():
            copy = remote(
                buffer,
                res.at[slot],
                res_send.at[1],
                res_recv.at[0],
                pipe=target,
            )
            copy.start() if start else copy.wait_send()

        for step in range(1, nx):
            copy = remote(
                buffer,
                res.at[slot],
                res_send.at[1 + step],
                res_recv.at[0],
                pipe=target,
                tensor=x_peer(step),
            )
            copy.start() if start else copy.wait_send()

    @pl.when(core == 0)
    def first_weights():
        weight_forward(1)

    for copy in expert_copies() + expert_own():
        copy.start()
    given = ags[0, 0, 0].reshape(tokens, features).astype(F32)
    normal, unused = norm_parts(given)
    xh[...] = normal
    ags[0, 0, 0] = (normal * gn[0][0:1]).astype(BF16).reshape(nx, rows, features)
    lax.fori_loop(0, 2, forward, 0)

    staged = (ga.at[0], gm, ga.at[1])
    partner = (pa.at[0], pm, pa.at[1])
    landing = (ra.at[0], rm, ra.at[1])

    def some_rows(which, part):
        return staged[which].at[:, part] if which == 1 else staged[which].at[part]

    def chunk(which, owner):
        return some_rows(which, pl.ds(owner * shard_rows, shard_rows))

    def staged_wait(which, section):
        @pl.when(core == section)
        def owned():
            wait_for(some_rows(which, all_but_one), ch_send.at[which])
            local(chunk(which, md), landing[which].at[md], ch_own.at[which]).wait()

        @pl.when(core != section)
        def lent():
            wait_for(staged[which], pg_send.at[which])

    def lend(which, section):
        @pl.when(core != section)
        def lent():
            remote(
                staged[which],
                partner[which],
                pg_send.at[which],
                pg_recv.at[which],
                pipe=other,
            ).start()

    def combine(which, section):
        @pl.when(core == section)
        def owned():
            wait_for(partner[which], pg_recv.at[which])
            staged[which][...] = (
                staged[which][...].astype(F32) + partner[which][...].astype(F32)
            ).astype(BF16)

            def push(step):
                peer = d_peer(step)
                remote(
                    chunk(which, peer),
                    landing[which].at[md],
                    ch_send.at[which],
                    ch_recv.at[which],
                    dp=peer,
                ).start()

            each_step(push)
            local(chunk(which, md), landing[which].at[md], ch_own.at[which]).start()

    def gains_start():
        place_here = core * nx + mx
        for section in range(2):

            @pl.when(core == section)
            def near():
                gx[place_here] = dgn[section]

            @pl.when(core != section)
            def far():
                remote(
                    dgn.at[section],
                    gx.at[place_here],
                    gx_send.at[section, 0],
                    gx_recv.at[0],
                    pipe=section,
                ).start()

            for step in range(1, nx):
                remote(
                    dgn.at[section],
                    gx.at[place_here],
                    gx_send.at[section, step],
                    gx_recv.at[0],
                    pipe=section,
                    tensor=x_peer(step),
                ).start()

    def gains_push():
        wait_for(gx.at[pl.ds(0, 2 * nx - 1)], gx_recv.at[0])
        gains_total = gx[0]
        for source in range(1, 2 * nx):
            gains_total = gains_total + gx[source]
        gs[...] = gains_total

        def push_gains(step):
            remote(gs, rg.at[md], rg_send.at[0], rg_recv.at[0], dp=d_peer(step)).start()

        each_step(push_gains)
        local(gs, rg.at[md], rg_own.at[0]).start()

    def experts_back(s):
        grad = cur[...]

        @pl.when(s == 0)
        def later():
            wide = all_rows(s, 1, 3, grad, slots_sent)
            dback_start(s, wide)
            combine(0, 1)

        dback = slots_end(s, 2)
        dpre = (nt(dback, we[s, 1]) * dge[s]).astype(BF16)
        dsent = nt(dpre, we[s, 0]).astype(BF16)
        slots_sent()
        slots_start(s, 3, dsent)

        @pl.when(s == 1)
        def last_result_start():
            experts_start(s)

        eg[0] = tn(arr[s], dpre).astype(BF16)
        eg[1] = tn(ace[s], dback).astype(BF16)

        @pl.when(core == s)
        def keep():
            local(eg.at[0], ei_own, e_own.at[0]).start()
            local(eg.at[1], eo_own, e_own.at[1]).start()

        @pl.when(core != s)
        def give():
            remote(eg.at[0], ei_far, e_send.at[0], e_recv.at[0], pipe=other).start()
            remote(eg.at[1], eo_far, e_send.at[1], e_recv.at[1], pipe=other).start()

        @pl.when(s == 1)
        def last_result_end():
            hout[...] = experts_end(s)
            result_copies(hout, 1, True)

        parts = norm_parts(hs[s, 3])
        dsent = slots_end(s, 3)
        sum_start(s, 1, 3, tn(pk[s, 0] + pk[s, 1], dsent))
        cur[...] = grad + norm_back(s, 3, parts, sum_end(s, 1, 3))

    def attend_back(s, j, k):
        grad = cur[...]
        dz = all_rows(s, 1, k, grad, (lambda: combine(1, s)) if j == 0 else None)
        dmixed = nn(dz, wa[s, j, :, :wide_features]).astype(BF16)
        query, key, value = [proj[s, j, c] for c in range(3)]
        probs = prb[s, j]
        dmixed_heads = jnp.concatenate(per_head(dmixed), axis=0)
        dprobs = nt(dmixed_heads, value)
        dscores = probs * (dprobs - jnp.sum(probs * dprobs, axis=-1, keepdims=True))
        dscores = dscores.astype(BF16)
        dvalue = tn(probs.astype(BF16), dmixed_heads)
        dkey = tn(dscores, jnp.concatenate(per_head(query), axis=0)) * (HEAD_DIM**-0.5)
        dquery = None
        for h, part in enumerate(per_head(key)):
            term = nn(dscores[h * tokens : (h + 1) * tokens], part)
            dquery = term if dquery is None else dquery + term
        dquery = dquery * (HEAD_DIM**-0.5)
        dproj = [d.astype(BF16) for d in (dquery, dkey, dvalue)]
        placed = None
        for c in range(3):
            term = nn(dproj[c], put[1 + c])
            placed = term if placed is None else placed + term
        placed = placed.astype(BF16)
        partial_rows = nt(placed, wa[s, j])

        def weight_grads():
            normed = ags[s, 0, k].reshape(tokens, features)
            mixed = nn(mix[s, j], put[0]).astype(BF16)
            ga[j] = tn(
                jnp.concatenate([normed, dz], axis=0), jnp.concatenate([placed, mixed], axis=0)
            ).astype(BF16)
            lend(2 * j, s)

        if j == 0:

            @pl.when(s == 0)
            def last_of_all():
                dgn[0, 0:1, :] = jnp.sum(partial_rows * xh[...], axis=0, keepdims=True)
                gains_start()
                staged_wait(0, 1)
                weight_grads()

            sum_start(s, 1, k, partial_rows)

            @pl.when(s == 1)
            def not_last():
                weight_grads()

            @pl.when(s == 0)
            def last_onward():
                combine(0, 0)
                gains_push()

        else:
            sum_start(s, 1, k, partial_rows)

            @pl.when(s == 0)
            def free():
                staged_wait(2, 1)

            weight_grads()

        parts = norm_parts(hs[s, k])
        cur[...] = grad + norm_back(s, k, parts, sum_end(s, 1, k))

    def feed_back(s):
        grad = cur[...]
        dout = all_rows(s, 1, 1, grad, lambda: combine(2, s))
        dpre = (nn(dout, wm[s, 1]) * dgm[s]).astype(BF16)
        sum_start(s, 1, 1, nt(dpre, wm[s, 0]))

        @pl.when(s == 0)
        def free():
            staged_wait(1, 1)

        normed = ags[s, 0, 1].reshape(tokens, features)
        gm[0] = tn(normed, dpre).astype(BF16)
        gm[1] = tn(dout, act[s]).astype(BF16)
        lend(1, s)
        parts = norm_parts(hs[s, 1])
        cur[...] = grad + norm_back(s, 1, parts, sum_end(s, 1, 1))

    def expert_grads_wait(s):
        @pl.when(core == s)
        def keep():
            local(eg.at[0], ei_own, e_own.at[0]).wait()
            local(eg.at[1], eo_own, e_own.at[1]).wait()

        @pl.when(core != s)
        def give():
            wait_for(eg.at[0], e_send.at[0])
            wait_for(eg.at[1], e_send.at[1])

    def backward(turn, carry):
        s = 1 - turn
        cur[...] = cur[...].astype(BF16).astype(F32)
        experts_back(s)
        attend_back(s, 1, 2)
        feed_back(s)
        attend_back(s, 0, 0)
        expert_grads_wait(s)
        return carry

    cur[...] = ags[1, 1, 3, mx].astype(F32)
    lax.fori_loop(0, 2, backward, 0)
    gout[...] = cur[...]
    result_copies(hout, 1, False)
    result_copies(gout, 0, True)

    slots_sent()
    for s in range(2):
        for way in range(2):
            for k in range(4):
                wait_for(rs_out.at[s, way, k, some], rs_send.at[s, way, k])
                if (s, way, k) not in ((0, 0, 0), (1, 1, 3)):
                    wait_for(ags.at[s, way, k, some], ag_send.at[s, way, k])
    for section in range(2):

        @pl.when(core != section)
        def far_end():
            wait_for(dgn.at[section], gx_send.at[section, 0])

        for step in range(1, nx):
            wait_for(dgn.at[section], gx_send.at[section, step])
    for which in range(4):
        wait_for(whole_part(which, 0), wf_send.at[which])
        wait_for(arrived_part(which), w_send.at[which])
    result_copies(gout, 0, False)
    wait_for(res.at[pl.ds(0, 2 * nx - 1)], res_recv.at[0])
    def over_sources(parts):
        total = parts[0].astype(F32)
        for source in range(1, nd):
            total = total + parts[source].astype(F32)
        return total

    def landed(which):
        staged_wait(which, 0)
        wait_for(landing[which].at[pl.ds(0, nd - 1)], ch_recv.at[which])

    landed(2)
    dense_sum[1] = over_sources(ra[1])
    landed(1)
    for c in range(2):
        feed_sum[c] = over_sources([rm[source, c] for source in range(nd)])
    wait_for(ei_far, e_recv.at[0])
    wait_for(eo_far, e_recv.at[1])
    wait_for(rg.at[pl.ds(0, nd - 1)], rg_recv.at[0])
    wait_for(rg.at[pl.ds(0, nd - 1)], rg_send.at[0])
    local(gs, rg.at[md], rg_own.at[0]).wait()
    gains_sum[...] = over_sources(rg)
    landed(0)
    dense_sum[0] = over_sources(ra[0])


def shards(
    nx,
    nd,
    boundary,
    norm_gains,
    attn_qkv,
    attn_out,
    mlp_in,
    mlp_out,
    expert_in,
    expert_out,
    expert_ids,
    expert_slots,
    gate_weights,
):
    tokens, features = boundary.shape[3:]
    rows = tokens // nx
    shard_rows = features // nd
    wide = attn_qkv.shape[4]
    units = mlp_in.shape[2]
    hidden = expert_in.shape[3]
    slots = nd * CAP
    quarters = features // 256
    slab = 16 * quarters + 16
    heads = wide // HEAD_DIM

    vmem = pl.BlockSpec(memory_space=pltpu.VMEM)
    hbm = pl.BlockSpec(memory_space=pl.ANY)
    dma = pltpu.SemaphoreType.DMA
    scratch = [
        pltpu.VMEM((2, nd, shard_rows, 4 * wide), BF16),
        pltpu.VMEM((nd, 2, shard_rows, units), BF16),
        pltpu.VMEM((nd, 8, features), F32),
        pltpu.VMEM((MICRO, 8, tokens), F32),
        pltpu.VMEM((shard_rows, 128), BF16),
        pltpu.VMEM((2, shard_rows, 4 * wide), BF16),
        pltpu.VMEM((2, shard_rows, units), BF16),
        pltpu.VMEM((4, wide, 4 * wide), BF16),
        pltpu.VMEM((tokens, features), F32),
        pltpu.VMEM((2, 2, features, 4 * wide), BF16),
        pltpu.VMEM((2, 2, features, units), BF16),
        pltpu.VMEM((2, 2, features, hidden), BF16),
        pltpu.VMEM((2, features, 128), BF16),
        pltpu.VMEM((2, 8, features), F32),
        pltpu.VMEM((2, 8, tokens), F32),
        pltpu.VMEM((2, tokens, tokens), F32),
        pltpu.VMEM((tokens, features), BF16),
        pltpu.VMEM((quarters, nd * 16, nd * (CAP - MAIN)), BF16),
        pltpu.VMEM((quarters, nd * (CAP - MAIN), nd * 16), BF16),
        pltpu.VMEM((2, 2, slots, tokens), BF16),
        pltpu.VMEM((2, 4, rows, features), F32),
        pltpu.VMEM((2, 2, 4, nx, rows, features), BF16),
        pltpu.VMEM((2, 2, 4, nx, rows, features), BF16),
        pltpu.VMEM((2, 2, 4, nx, rows, features), BF16),
        pltpu.VMEM((nd, slab, 256), BF16),
        pltpu.VMEM((2, 4, nd, slab, 256), BF16),
        pltpu.VMEM((2, 2, 3, tokens, wide), BF16),
        pltpu.VMEM((2, 2, tokens, wide), BF16),
        pltpu.VMEM((2, 2, heads * tokens, tokens), F32),
        pltpu.VMEM((2, tokens, units), F32),
        pltpu.VMEM((2, tokens, units), BF16),
        pltpu.VMEM((2, slots, features), BF16),
        pltpu.VMEM((2, slots, hidden), F32),
        pltpu.VMEM((2, slots, hidden), BF16),
        pltpu.VMEM((2, features, 4 * wide), BF16),
        pltpu.VMEM((2, features, units), BF16),
        pltpu.VMEM((2, features, 4 * wide), BF16),
        pltpu.VMEM((2, features, units), BF16),
        pltpu.VMEM((2, features, hidden), BF16),
        pltpu.VMEM((2, 8, features), F32),
        pltpu.VMEM((2 * nx, 8, features), F32),
        pltpu.VMEM((8, features), F32),
        pltpu.VMEM((rows, features), F32),
        pltpu.VMEM((rows, features), F32),
        pltpu.VMEM((rows, features), F32),
        dma((2, 2, 4)),
        dma((2, 2, 4)),
        dma((2, 2, 4)),
        dma((2, 2, 4)),
        dma((1,)),
        dma((2, 4)),
        dma((4,)),
        dma((4,)),
        dma((4,)),
        dma((4,)),
        dma((4,)),
        dma((4,)),
        dma((4,)),
        dma((2,)),
        dma((3,)),
        dma((3,)),
        dma((3,)),
        dma((3,)),
        dma((3,)),
        dma((2,)),
        dma((2,)),
        dma((2,)),
        dma((1 + nx,)),
        dma((1,)),
        dma((1,)),
        dma((2, nx)),
        dma((1,)),
        dma((1,)),
        dma((1,)),
        dma((1,)),
    ]
    res, dense, feed, gains, ei_own, eo_own, ei_far, eo_far = pl.pallas_call(
        functools.partial(kernel, nx, nd),
        out_shape=(
            jax.ShapeDtypeStruct((2 * nx, rows, features), F32),
            jax.ShapeDtypeStruct((2, shard_rows, 4 * wide), F32),
            jax.ShapeDtypeStruct((2, shard_rows, units), F32),
            jax.ShapeDtypeStruct((8, features), F32),
            jax.ShapeDtypeStruct((features, hidden), BF16),
            jax.ShapeDtypeStruct((hidden, features), BF16),
            jax.ShapeDtypeStruct((features, hidden), BF16),
            jax.ShapeDtypeStruct((hidden, features), BF16),
        ),
        in_specs=[vmem] * 9 + [hbm] * 2,
        out_specs=(hbm,) + (vmem,) * 3 + (hbm,) * 4,
        scratch_shapes=scratch,
        compiler_params=pltpu.CompilerParams(
            collective_id=0, has_side_effects=True, vmem_limit_bytes=VMEM_LIMIT
        ),
    )(
        boundary[0, :, 0],
        jnp.swapaxes(expert_ids[0, :, 0], 1, 2),
        jnp.swapaxes(expert_slots[0, :, 0], 1, 2),
        jnp.swapaxes(gate_weights[0, :, 0], 1, 2),
        attn_qkv[0],
        jnp.swapaxes(attn_out[0], 1, 2),
        mlp_in[0],
        mlp_out[0].T,
        norm_gains[0],
        expert_in[0, 0],
        expert_out[0, 0],
    )

    gains = gains[: norm_gains.shape[1]]
    gains = lax.dynamic_slice_in_dim(gains, lax.axis_index("dp") * shard_rows, shard_rows, 1)
    qkv = dense[:, :, wide:].reshape(2, shard_rows, 3, wide)
    return (
        res.reshape(1, MICRO, 1, tokens, features),
        gains[None],
        jnp.swapaxes(qkv, 1, 2)[None],
        jnp.swapaxes(dense[:, :, :wide], 1, 2)[None],
        feed[0][None],
        feed[1].T[None],
        (ei_own.astype(F32) + ei_far.astype(F32))[None, None],
        (eo_own.astype(F32) + eo_far.astype(F32))[None, None],
    )


VMEM_LIMIT = 62 * 1024 * 1024


def solution(mesh):
    in_specs = (
        P("pipe", None, "dp", None, None),
        P("pipe", None, "dp"),
        P("pipe", None, None, "dp", "tensor"),
        P("pipe", None, "tensor", "dp"),
        P("pipe", "dp", "tensor"),
        P("pipe", "tensor", "dp"),
        P("pipe", "dp", None, "tensor"),
        P("pipe", "dp", "tensor", None),
        P("pipe", None, "dp", None, None),
        P("pipe", None, "dp", None, None),
        P("pipe", None, "dp", None, None),
    )
    out_specs = (
        P("pipe", None, "dp", None, None),
        P("pipe", None, "dp"),
        P("pipe", None, None, "dp", "tensor"),
        P("pipe", None, "tensor", "dp"),
        P("pipe", "dp", "tensor"),
        P("pipe", "tensor", "dp"),
        P("pipe", "dp", None, "tensor"),
        P("pipe", "dp", "tensor", None),
    )
    return jax.shard_map(
        functools.partial(shards, mesh.shape["tensor"], mesh.shape["dp"]),
        mesh=mesh,
        in_specs=in_specs,
        out_specs=out_specs,
        check_vma=False,
    )
```
